32 devices in a mesh: runs: 2 (over y), mode: 8 (over z, x), mer: 2 (over core).
Axes of the slice: x: 2, y: 2, z: 4, core: 2. Of those that a mesh axis runs over, the one named last changes fastest.
Arguments:
- velocity: float32 [6, 2, 16, 4096], P('runs', None, 'mode', 'mer'), parts along dimension 0, may hold values from -6 to 6
- vorticity: float32 [6, 2, 16, 4096], P('runs', None, 'mode', 'mer'), parts along dimension 0, may hold values from -6 to 6
- magnetic: float32 [6, 2, 16, 4096], P('runs', None, 'mode', 'mer'), parts along dimension 0, may hold values from -6 to 6
- current: float32 [6, 2, 16, 4096], P('runs', None, 'mode', 'mer'), parts along dimension 0, may hold values from -6 to 6
- elem_nodes: int32 [6, 2048], P(None, 'mer'), may hold values from 0 to 2047, as said below
- mass_coef: float32 [2048], P('mer'), may hold values from 0.5 to 2
- stiff_coef: float32 [2048], P('mer'), may hold values from 0.05 to 0.5
- radial_coef: float32 [2048], P('mer'), may hold values from 0.5 to 4
- iface: int32 [2, 128], P('mer'), may hold values from 0 to 2047, as said below
Outputs:
- velocity_new: float32 [6, 2, 16, 4096], P('runs', None, 'mode', 'mer'), parts along dimension 0
- magnetic_new: float32 [6, 2, 16, 4096], P('runs', None, 'mode', 'mer'), parts along dimension 0
The draws below stay inside these ranges and needn't reach their ends.
There are 2 independent parts, one for each index of `runs`. The reference program is written for one: setup_inputs(seed, part) draws one part's arguments, and reference() takes and returns one part's arrays. A program takes and returns all parts, laid end to end along the dimension named above; an argument that names none is the same for every part. Nothing has to cross between parts.
Inputs may be any that keep to these rules, and one draw needn't show every extreme that they name: `elem_nodes`: every node of a partition is named by some triangle of that partition. `iface`: entries of one row are distinct.
All inputs are finite; a program needn't handle non-finite values.
Results may differ from the reference program's by a relative error of at most 0.0003.
Values sent between devices are 32-bit elements; how exact they have to be, the bound alone decides.
No kernel may reach another device: no remote copies, remote signals or barrier semaphores. Data moves between devices by JAX's collectives and lax.ppermute only.
A program may use at most 64 MiB of HBM per device.

```python
import math
import jax
import jax.numpy as jnp
from jax import lax

MODES = 16
NODES_DEV = 2048
ELEM_DEV = 1024
IFACE = 128
NODES = 4096
ELEMS = 2048
N_MER = 2


def draw_elem_nodes(key, part):

    def single(sub):
        first, second, third = jax.random.split(sub, 3)
        cover = jax.random.permutation(first, NODES_DEV).astype(jnp.int32)
        extra = jax.random.randint(second, (6 * ELEM_DEV - NODES_DEV,), 0, NODES_DEV).astype(jnp.int32)
        flat = jax.random.permutation(third, jnp.concatenate([cover, extra]))
        return flat.reshape(6, ELEM_DEV)
    keys = jax.random.split(jax.random.fold_in(key, 11), N_MER)
    stacked = jax.vmap(single)(keys)
    return jnp.transpose(stacked, (1, 0, 2)).reshape(6, N_MER * ELEM_DEV)


def draw_iface(key, part):

    def single(sub):
        first, second = jax.random.split(sub)
        inner_ids = jax.random.permutation(first, NODES_DEV - 2)[:IFACE - 2].astype(jnp.int32) + 1
        ends = jnp.array([0, NODES_DEV - 1], dtype=jnp.int32)
        return jax.random.permutation(second, jnp.concatenate([inner_ids, ends]))
    keys = jax.random.split(jax.random.fold_in(key, 23), N_MER)
    return jax.vmap(single)(keys)


def steps_of(own_key, shape, shards, smallest, top_value):
    level, own = 1.0, jax.random.fold_in(own_key, 6)
    for dim, shards_of in shards:
        draws = jnp.exp(jax.random.uniform(jax.random.fold_in(own, dim), (shards_of,), jnp.float32, smallest / len(shards), top_value / len(shards)))
        level = level * jnp.repeat(draws, shape[dim] // shards_of).reshape([-1 if axis == dim else 1 for axis in range(len(shape))])
    return level


def gaussian(own_key, dims, deviation, bound, shards=(), kind=jnp.bfloat16):
    values = deviation * jax.random.normal(own_key, dims, jnp.float32)
    if shards:
        values = values * steps_of(own_key, dims, shards, -0.22, 0.18)
    return jnp.clip(values, -bound, bound).astype(kind)


def setup_inputs(seed: int = 0, part: int = 0) -> dict:
    seeds = jax.random.split(jax.random.key(seed), 10)
    part_splits = jax.random.split(jax.random.fold_in(seeds[9], part), 10)
    return {
        "velocity": gaussian(part_splits[0], (3, 2, MODES, NODES), 1.0, 6.0, ((2, 8), (3, 2)), jnp.float32),
        "vorticity": gaussian(part_splits[1], (3, 2, MODES, NODES), 1.0, 6.0, ((2, 8), (3, 2)), jnp.float32),
        "magnetic": gaussian(part_splits[2], (3, 2, MODES, NODES), 1.0, 6.0, ((2, 8), (3, 2)), jnp.float32),
        "current": gaussian(part_splits[3], (3, 2, MODES, NODES), 1.0, 6.0, ((2, 8), (3, 2)), jnp.float32),
        "elem_nodes": draw_elem_nodes(jax.random.fold_in(seeds[9], 71), part),
        "mass_coef": jnp.clip(jnp.exp(math.log(2.0) - 1.3862944 * jax.random.uniform(seeds[5], (ELEMS,), jnp.float32) ** steps_of(seeds[5], (ELEMS,), ((0, 2),), -0.2, 0.2)), 0.5, 2.0),
        "stiff_coef": jnp.clip(jnp.exp(math.log(0.5) - 2.3025851 * jax.random.uniform(seeds[6], (ELEMS,), jnp.float32) ** steps_of(seeds[6], (ELEMS,), ((0, 2),), -0.2, 0.2)), 0.05, 0.5),
        "radial_coef": jnp.clip(jnp.exp(math.log(4.0) - 2.0794415 * jax.random.uniform(seeds[7], (ELEMS,), jnp.float32) ** steps_of(seeds[7], (ELEMS,), ((0, 2),), -0.2, 0.2)), 0.5, 4.0),
        "iface": draw_iface(jax.random.fold_in(seeds[9], 71), part),
    }


step_size = 0.05
diffusion_ratio = 2.0


def fourier_tables(modes):
    angles = 2 * modes
    order = jnp.arange(modes, dtype=jnp.int32)
    points = jnp.arange(angles, dtype=jnp.int32)
    phase = ((points[:, None] * order[None, :]) % angles).astype(jnp.float32) * (2.0 * math.pi / angles)
    cosine = jnp.cos(phase)
    sine = jnp.sin(phase)
    synthesis = jnp.concatenate([cosine, sine], axis=1)
    factor = jnp.where(order == 0, 1.0, 2.0).astype(jnp.float32) / angles
    analysis = jnp.concatenate([cosine.T * factor[:, None], sine.T * factor[:, None]], axis=0)
    return synthesis, analysis


def to_physical(coef, synthesis):
    flat = coef.reshape(coef.shape[0], coef.shape[1] * coef.shape[2], coef.shape[3])
    return jnp.einsum("ak,ckn->can", synthesis, flat, precision=lax.Precision.HIGHEST)


def to_coefs(values, analysis, modes):
    out_coef = jnp.einsum("ka,can->ckn", analysis, values, precision=lax.Precision.HIGHEST)
    return out_coef.reshape(values.shape[0], 2, modes, values.shape[2])


def cross(left, right):
    return jnp.stack([left[1] * right[2] - left[2] * right[1],
                      left[2] * right[0] - left[0] * right[2],
                      left[0] * right[1] - left[1] * right[0]])


def element_apply(vector, nodes_of, c_mass, c_stiff):
    local = vector[:, nodes_of]
    total = jnp.sum(local, axis=1, keepdims=True)
    terms = c_mass[:, None, :] * (local + total) / 12.0
    if c_stiff is not None:
        terms = terms + c_stiff[:, None, :] * (6.0 * local - total)
    return jnp.zeros_like(vector).at[:, nodes_of].add(terms)


def reference(velocity, vorticity, magnetic, current, elem_nodes, mass_coef, stiff_coef, radial_coef, iface):
    modes = velocity.shape[2]
    synthesis, analysis = fourier_tables(modes)
    block = min(1024, NODES)
    starts = jnp.arange(NODES // block, dtype=jnp.int32) * block

    def nonlinear(start):
        def take(field):
            return to_physical(lax.dynamic_slice_in_dim(field, start, block, 3), synthesis)
        vel_p = take(velocity)
        vort_p = take(vorticity)
        mag_p = take(magnetic)
        cur_p = take(current)
        first = to_coefs(cross(vel_p, vort_p) + cross(cur_p, mag_p), analysis, modes)
        second = to_coefs(cross(vel_p, mag_p), analysis, modes)
        return first, second

    vel_blocks, mag_blocks = lax.map(nonlinear, starts)
    vel_nl = jnp.moveaxis(vel_blocks, 0, 3).reshape(3, 2, modes, NODES)
    mag_nl = jnp.moveaxis(mag_blocks, 0, 3).reshape(3, 2, modes, NODES)
    forcing = jnp.concatenate([velocity + step_size * vel_nl, magnetic + step_size * mag_nl], axis=0)
    by_mode = jnp.transpose(forcing, (2, 0, 1, 3)).reshape(modes, 12, NODES)

    conns = [elem_nodes[:, p * ELEM_DEV:(p + 1) * ELEM_DEV] for p in range(N_MER)]
    masses = [mass_coef[p * ELEM_DEV:(p + 1) * ELEM_DEV] for p in range(N_MER)]
    stiffs = [stiff_coef[p * ELEM_DEV:(p + 1) * ELEM_DEV] for p in range(N_MER)]
    radials = [radial_coef[p * ELEM_DEV:(p + 1) * ELEM_DEV] for p in range(N_MER)]
    weights = [jnp.ones((NODES_DEV,), jnp.float32).at[iface[p]].set(0.5) for p in range(N_MER)]
    scaling = jnp.where(jnp.arange(12) < 6, 1.0, diffusion_ratio).astype(jnp.float32)

    def shared(pieces):
        return [pieces[p].at[:, iface[p]].add(pieces[1 - p][:, iface[1 - p]]) for p in range(N_MER)]

    def inner(left, right):
        return sum(jnp.sum(left[p] * right[p] * weights[p][None, :], axis=1) for p in range(N_MER))

    def solve(args_in):
        order, rows = args_in
        shift = (order.astype(jnp.float32) / modes) ** 2
        pieces = [rows[:, p * NODES_DEV:(p + 1) * NODES_DEV] for p in range(N_MER)]

        def operator(vector):
            return shared([element_apply(vector[p], conns[p], (masses[p] + shift * radials[p])[None, :],
                                         scaling[:, None] * stiffs[p][None, :]) for p in range(N_MER)])

        rhs = shared([element_apply(pieces[p], conns[p], masses[p][None, :], None) for p in range(N_MER)])
        resid = rhs
        direction = rhs
        norm_now = inner(resid, resid)
        image = operator(direction)
        alpha = norm_now / inner(direction, image)
        answer = [alpha[:, None] * direction[p] for p in range(N_MER)]
        resid = [resid[p] - alpha[:, None] * image[p] for p in range(N_MER)]
        norm_next = inner(resid, resid)
        beta = norm_next / norm_now
        direction = [resid[p] + beta[:, None] * direction[p] for p in range(N_MER)]
        image = operator(direction)
        alpha = norm_next / inner(direction, image)
        answer = [answer[p] + alpha[:, None] * direction[p] for p in range(N_MER)]
        return jnp.concatenate(answer, axis=1)

    solved = lax.map(solve, (jnp.arange(modes, dtype=jnp.int32), by_mode))
    result = jnp.transpose(solved.reshape(modes, 6, 2, NODES), (1, 2, 0, 3))
    return result[:3], result[3:]
```

```python
import functools
import math

import jax
import jax.numpy as jnp
import numpy as np
from jax import lax
from jax.experimental import pallas as pl
from jax.experimental.pallas import tpu as pltpu
from jax.sharding import PartitionSpec as P

step_size = 0.05
diffusion_ratio = 2.0
f32 = jnp.float32
bf16 = jnp.bfloat16
vmem_limit = 16 * 2**20


def params():
    return pltpu.CompilerParams(vmem_limit_bytes=vmem_limit)


def halves(table):
    high = table.astype(np.float32).astype(jnp.bfloat16)
    low = (table - high.astype(np.float64)).astype(np.float32).astype(jnp.bfloat16)
    return high, low


def trig_tables(modes, per_dev):
    angles = 2 * modes
    order = np.arange(modes)
    points = np.arange(angles)
    phase = (points[:, None] * order[None, :] % angles) * (2.0 * math.pi / angles)
    both = np.stack([np.cos(phase), np.sin(phase)])
    both = both.reshape(2, angles, modes // per_dev, per_dev)
    factor = np.where(order == 0, 1.0, 2.0).reshape(modes // per_dev, per_dev) / angles
    same = np.eye(2)
    synthesis = np.einsum("pq,sajk->pajqsk", same, both).reshape(2 * angles, -1)
    analysis = np.einsum("pq,sajk,jk->jqskpa", same, both, factor * step_size).reshape(-1, 2 * angles)
    out = []
    for table in (synthesis, analysis):
        high, low = halves(table)
        out.append(jnp.asarray(np.concatenate([high, high, low], axis=1)))
    return out


def pieces(array, count):
    parts = []
    rest = array
    for i in range(count):
        part = rest.astype(bf16).astype(f32)
        parts.append(part)
        rest = rest - part
    return jnp.concatenate(parts, axis=0).astype(bf16)


def product(array, exact, contract, count=2):
    rows = array.shape[0]
    out = lax.dot_general(
        pieces(array, count), exact, (((1,), (contract,)), ((), ())), preferred_element_type=f32
    )
    total = out[:rows]
    for i in range(1, count):
        total = total + out[i * rows : (i + 1) * rows]
    return total


def table_product(table, values):
    high = values.astype(bf16)
    low = (values - high.astype(f32)).astype(bf16)
    return jnp.dot(table, jnp.concatenate([high, low, high], axis=0), preferred_element_type=f32)


def pack_kernel(vel, mag, vort, cur, out):
    blocks, _, block = out.shape
    row = 0
    for field in (vel, mag, vort, cur):
        comps, _, per_dev, _ = field.shape
        for c in range(comps):
            for s in range(2):
                piece = field[c, s]
                for b in range(blocks):
                    out[b, row : row + per_dev, :] = piece[:, b * block : (b + 1) * block]
                row += per_dev


def nonlinear_kernel(fields, synthesis, analysis, out):
    owners, rows, block = fields.shape
    pair = rows // 6
    angles = synthesis.shape[0] // 2
    phys = []
    for t in range(6):
        coef = jnp.concatenate([fields[j, t * pair : (t + 1) * pair, :] for j in range(owners)], axis=0)
        values = table_product(synthesis[...], coef)
        phys += [values[:angles], values[angles:]]
    vel, mag, vort, cur = phys[0:3], phys[3:6], phys[6:9], phys[9:12]

    def cross(a, b, i):
        j, k = (i + 1) % 3, (i + 2) % 3
        return a[j] * b[k] - a[k] * b[j]

    terms = [cross(vel, vort, i) + cross(cur, mag, i) for i in range(3)]
    terms += [cross(vel, mag, i) for i in range(3)]
    for t in range(3):
        coef = table_product(analysis[...], jnp.concatenate([terms[2 * t], terms[2 * t + 1]], axis=0))
        for j in range(owners):
            span = slice(t * pair, (t + 1) * pair)
            out[j, span, :] = fields[j, span, :] + coef[j * pair : (j + 1) * pair]


def mesh_kernel(elem_nodes, mass, radial, stiff, iface, touch, at_iface, diag):
    nodes, elems = touch.shape
    shared = iface.shape[1]
    fields = 8
    words = nodes // fields
    width = math.gcd(elems, 256)

    def chunk(c, carry):
        span = pl.ds(pl.multiple_of(c * width, width), width)
        word = lax.broadcasted_iota(jnp.int32, (words, width), 0)
        total = jnp.zeros((words, width), jnp.int32)
        for i in range(elem_nodes.shape[0]):
            ids = elem_nodes[i : i + 1, span]
            field = ids // words
            value = jnp.left_shift(1, field * 4)
            total = total + jnp.where(ids - field * words == word, value, 0)
        for q in range(fields):
            count = jnp.right_shift(total, 4 * q) & 15
            touch[q * words : (q + 1) * words, span] = count.astype(f32).astype(bf16)
        return carry

    lax.fori_loop(0, elems // width, chunk, 0)
    node = lax.broadcasted_iota(jnp.int32, (nodes, shared), 0)
    at_iface[...] = jnp.where(iface[...] == node, 1.0, 0.0).astype(bf16)
    zero = jnp.zeros((5, elems), f32)
    coefs = jnp.concatenate([mass[...] / 12.0, radial[...] / 12.0, 6.0 * stiff[...], zero], axis=0)
    sums = product(coefs, touch[...], 1, 3)
    ones = jnp.ones((16, shared), bf16)
    hits = lax.dot_general(ones, at_iface[...], (((1,), (1,)), ((), ())), preferred_element_type=f32)
    row = lax.broadcasted_iota(jnp.int32, (8, nodes), 0)
    diag[...] = jnp.where(row == 3, 1.0 - 0.5 * hits[:8], sums)


def row_factors(place, rows, per_dev, modes):
    row = lax.broadcasted_iota(jnp.int32, (rows, 1), 0)
    order = (place * per_dev + row % per_dev).astype(f32)
    shift = (order / modes) ** 2
    scale = jnp.where(row < rows // 2, 1.0, diffusion_ratio).astype(f32)
    return shift, scale


def operator_parts(place, rows, per_dev, modes, mass, radial, stiff, diag):
    shift, scale = row_factors(place[0], rows, per_dev, modes)
    per_elem = (mass[...] + shift * radial[...]) / 12.0 - scale * stiff[...]
    per_node = diag[0:1, :] + shift * diag[1:2, :] + scale * diag[2:3, :]
    return per_elem, per_node


def row_sum(array):
    return jnp.sum(array, axis=1, keepdims=True)


def rhs_kernel(forcing, touch, at_iface, diag, mass, local, edge):
    blocks = forcing.shape[0]
    given = jnp.concatenate([forcing[b] for b in range(blocks)], axis=1)
    sums = product(given, touch[...], 0)
    image = diag[0:1, :] * given + product(sums * (mass[...] / 12.0), touch[...], 1)
    local[...] = image
    edge[...] = product(image, at_iface[...], 0, 3)


def first_kernel(per_dev, modes, place, local, edge, touch, at_iface, diag, mass, radial, stiff, rhs_out, image_out, sums_out, edge_out):
    rows, shared = edge.shape
    per_elem, per_node = operator_parts(place, rows, per_dev, modes, mass, radial, stiff, diag)
    rhs = local[...] + product(edge[...], at_iface[...], 1, 3)
    rhs_out[...] = rhs
    sums = product(rhs, touch[...], 0)
    sums_out[...] = sums
    spread = per_elem * sums
    image = per_node * rhs + product(spread, touch[...], 1)
    image_out[...] = image
    norm = row_sum(diag[3:4, :] * rhs * rhs)
    curvature = row_sum(per_node * rhs * rhs) + row_sum(spread * sums)
    edge_out[:, :shared] = product(image, at_iface[...], 0, 3)
    lane = lax.broadcasted_iota(jnp.int32, (rows, 128), 1)
    edge_out[:, shared:] = jnp.where(lane == 0, norm, curvature)


def second_kernel(per_dev, modes, place, image, edge, own, touch, at_iface, diag, mass, radial, stiff, rhs, sums, resid_out, norms_out):
    rows = image.shape[0]
    shared = edge.shape[1] - 128
    per_elem, per_node = operator_parts(place, rows, per_dev, modes, mass, radial, stiff, diag)
    norm = own[:, shared : shared + 1] + edge[:, shared : shared + 1]
    curvature = own[:, shared + 1 : shared + 2] + edge[:, shared + 1 : shared + 2]
    alpha = norm / curvature
    full = image[...] + product(edge[:, :shared], at_iface[...], 1, 3)
    resid = rhs[...] - alpha * full
    resid_out[...] = resid
    new = product(resid, touch[...], 0)
    after = row_sum(diag[3:4, :] * resid * resid)
    square = row_sum(per_node * resid * resid) + row_sum(per_elem * new * new)
    mixed = row_sum(per_node * resid * rhs[...]) + row_sum(per_elem * new * sums[...])
    lane = lax.broadcasted_iota(jnp.int32, (rows, 128), 1)
    norms_out[...] = jnp.where(lane == 0, after, jnp.where(lane == 1, square, mixed))


def last_kernel(edge, own, norms_own, norms, resid, rhs, vel_out, mag_out):
    shared = edge.shape[1] - 128
    norm = own[:, shared : shared + 1] + edge[:, shared : shared + 1]
    curvature = own[:, shared + 1 : shared + 2] + edge[:, shared + 1 : shared + 2]
    alpha = norm / curvature
    after = norms_own[:, 0:1] + norms[:, 0:1]
    square = norms_own[:, 1:2] + norms[:, 1:2]
    mixed = norms_own[:, 2:3] + norms[:, 2:3]
    beta = after / norm
    alpha_next = after / (square + 2.0 * beta * mixed + beta * beta * curvature)
    answer = (alpha + alpha_next * beta) * rhs[...] + alpha_next * resid[...]
    row = 0
    for out in (vel_out, mag_out):
        comps, _, per_dev, _ = out.shape
        for c in range(comps):
            for s in range(2):
                out[c, s] = answer[row : row + per_dev]
                row += per_dev


def per_device(velocity, vorticity, magnetic, current, elem_nodes, mass_coef, stiff_coef, radial_coef, iface):
    comps, _, per_dev, nodes = velocity.shape
    owners = lax.axis_size("mode")
    modes = per_dev * owners
    block = nodes // owners
    rows = 4 * comps * per_dev
    elems = elem_nodes.shape[1]
    shared = iface.shape[1]
    mass, radial, stiff = (a.reshape(1, elems) for a in (mass_coef, radial_coef, stiff_coef))
    synthesis, analysis = trig_tables(modes, per_dev)
    place = lax.axis_index("mode").astype(jnp.int32).reshape(1)

    def shape(*dims, kind=f32):
        return jax.ShapeDtypeStruct(dims, kind)

    if block % 128 == 0:
        packed = pl.pallas_call(
            pack_kernel, out_shape=shape(owners, 2 * rows, block), compiler_params=params(), name="pack"
        )(velocity, magnetic, vorticity, current)
    else:
        packed = jnp.concatenate(
            [a.reshape(rows // 2, owners, block) for a in (velocity, magnetic, vorticity, current)], axis=0
        ).transpose(1, 0, 2)
    columns = lax.all_to_all(packed, "mode", 0, 0, tiled=True)
    touch, at_iface, diag = pl.pallas_call(
        mesh_kernel,
        out_shape=(shape(nodes, elems, kind=bf16), shape(nodes, shared, kind=bf16), shape(8, nodes)),
        compiler_params=params(),
        name="incidence",
        cost_estimate=pl.CostEstimate(flops=2**31, bytes_accessed=2**23, transcendentals=0),
    )(elem_nodes, mass, radial, stiff, iface)
    terms = pl.pallas_call(
        nonlinear_kernel, out_shape=shape(owners, rows, block), compiler_params=params(), name="nonlinear"
    )(columns, synthesis, analysis)
    forcing = lax.all_to_all(terms, "mode", 0, 0, tiled=True)
    if block % 128:
        forcing = forcing.transpose(1, 0, 2).reshape(1, rows, nodes)

    def swap(array):
        return lax.ppermute(array, "mer", [(0, 1), (1, 0)])

    in_smem = pl.BlockSpec(memory_space=pltpu.SMEM)
    in_vmem = pl.BlockSpec(memory_space=pltpu.VMEM)
    local, edge = pl.pallas_call(
        rhs_kernel, out_shape=(shape(rows, nodes), shape(rows, shared)), compiler_params=params(), name="rhs"
    )(forcing, touch, at_iface, diag, mass)
    rhs, image, sums, edge_own = pl.pallas_call(
        functools.partial(first_kernel, per_dev, modes),
        in_specs=[in_smem] + [in_vmem] * 8,
        out_shape=(shape(rows, nodes), shape(rows, nodes), shape(rows, elems), shape(rows, shared + 128)),
        compiler_params=params(),
        name="first",
    )(place, local, swap(edge), touch, at_iface, diag, mass, radial, stiff)
    edge_other = swap(edge_own)
    resid, norms_own = pl.pallas_call(
        functools.partial(second_kernel, per_dev, modes),
        in_specs=[in_smem] + [in_vmem] * 11,
        out_shape=(shape(rows, nodes), shape(rows, 128)),
        compiler_params=params(),
        name="second",
    )(place, image, edge_other, edge_own, touch, at_iface, diag, mass, radial, stiff, rhs, sums)
    out = shape(*velocity.shape)
    return pl.pallas_call(
        last_kernel, out_shape=(out, out), compiler_params=params(), name="last"
    )(edge_other, edge_own, norms_own, swap(norms_own), resid, rhs)


def solution(mesh):
    field = P("runs", None, "mode", "mer")
    placed = (field, field, field, field, P(None, "mer"), P("mer"), P("mer"), P("mer"), P("mer", None))
    return jax.shard_map(
        per_device, mesh=mesh, in_specs=placed, out_specs=(field, field), check_vma=False
    )
```

```python
import functools
import math

import jax
import jax.numpy as jnp
import numpy as np
from jax import lax
from jax.experimental import pallas as pl
from jax.experimental.pallas import tpu as pltpu
from jax.sharding import PartitionSpec as P

step_size = 0.05
diffusion_ratio = 2.0
f32 = jnp.float32
bf16 = jnp.bfloat16
small, medium, large = 16 * 2**20, 54 * 2**20, 60 * 2**20


def params(limit=small):
    return pltpu.CompilerParams(vmem_limit_bytes=limit)


def halves(table):
    high = table.astype(np.float32).astype(jnp.bfloat16)
    low = (table - high.astype(np.float64)).astype(np.float32).astype(jnp.bfloat16)
    return high, low


def trig_tables(modes, per_dev):
    angles = 2 * modes
    order = np.arange(modes)
    points = np.arange(angles)
    phase = (points[:, None] * order[None, :] % angles) * (2.0 * math.pi / angles)
    both = np.stack([np.cos(phase), np.sin(phase)])
    both = both.reshape(2, angles, modes // per_dev, per_dev)
    factor = np.where(order == 0, 1.0, 2.0).reshape(modes // per_dev, per_dev) / angles
    same = np.eye(2)
    synthesis = np.einsum("pq,sajk->pajqsk", same, both).reshape(2 * angles, -1)
    analysis = np.einsum("pq,sajk,jk->jqskpa", same, both, factor * step_size).reshape(-1, 2 * angles)
    out = []
    for table in (synthesis, analysis):
        high, low = halves(table)
        out.append(jnp.asarray(np.concatenate([high, high, low], axis=1)))
    return out


def pieces(array, count):
    parts = []
    rest = array
    for i in range(count):
        part = rest.astype(bf16).astype(f32)
        parts.append(part)
        rest = rest - part
    return jnp.concatenate(parts, axis=0).astype(bf16)


def product(array, exact, contract, count=2):
    rows = array.shape[0]
    out = lax.dot_general(
        pieces(array, count), exact, (((1,), (contract,)), ((), ())), preferred_element_type=f32
    )
    total = out[:rows]
    for i in range(1, count):
        total = total + out[i * rows : (i + 1) * rows]
    return total


def table_product(table, values):
    high = values.astype(bf16)
    low = (values - high.astype(f32)).astype(bf16)
    return jnp.dot(table, jnp.concatenate([high, low, high], axis=0), preferred_element_type=f32)


def start_all(sources, targets, sems):
    copies = [
        pltpu.make_async_copy(source, target, sems.at[i])
        for i, (source, target) in enumerate(zip(sources, targets))
    ]
    for copy in copies:
        copy.start()
    return copies


def pack_kernel(vel, mag, vort, cur, out, held, ready, in_sems, out_sems):
    blocks, rows, block = out.shape
    copies = start_all((vel, mag, vort, cur), [held.at[i] for i in range(4)], in_sems)
    sent = []
    row = 0
    for i in range(4):
        copies[i].wait()
        field = held.at[i]
        comps, _, per_dev, _ = field.shape
        for c in range(comps):
            for s in range(2):
                piece = field[c, s]
                for b in range(blocks):
                    ready[b, row : row + per_dev, :] = piece[:, b * block : (b + 1) * block]
                row += per_dev
        if i % 2:
            half = pl.ds(i // 2 * (rows // 2), rows // 2)
            sent.append(pltpu.make_async_copy(ready.at[:, half, :], out.at[:, half, :], out_sems.at[i // 2]))
            sent[-1].start()
    for copy in sent:
        copy.wait()


def nonlinear_kernel(fields, synthesis, analysis, touch_hbm, iface_hbm, diag_hbm, coefs_hbm, out, touch, at_iface, diag, coefs, sems):
    owners, rows, block = fields.shape
    part = touch.shape[0] // 4
    spans = [pl.ds(i * part, part) for i in range(4)]
    loads = start_all(
        [touch_hbm.at[span, :] for span in spans] + [iface_hbm, diag_hbm, coefs_hbm],
        [touch.at[span, :] for span in spans] + [at_iface, diag, coefs],
        sems,
    )
    pair = rows // 6
    angles = synthesis.shape[0] // 2
    phys = []
    for t in range(6):
        coef = jnp.concatenate([fields[j, t * pair : (t + 1) * pair, :] for j in range(owners)], axis=0)
        values = table_product(synthesis[...], coef)
        phys += [values[:angles], values[angles:]]
    vel, mag, vort, cur = phys[0:3], phys[3:6], phys[6:9], phys[9:12]

    def cross(a, b, i):
        j, k = (i + 1) % 3, (i + 2) % 3
        return a[j] * b[k] - a[k] * b[j]

    terms = [cross(vel, vort, i) + cross(cur, mag, i) for i in range(3)]
    terms += [cross(vel, mag, i) for i in range(3)]
    for t in range(3):
        coef = table_product(analysis[...], jnp.concatenate([terms[2 * t], terms[2 * t + 1]], axis=0))
        for j in range(owners):
            span = slice(t * pair, (t + 1) * pair)
            out[j, span, :] = fields[j, span, :] + coef[j * pair : (j + 1) * pair]
    for load in loads:
        load.wait()


def mesh_kernel(nodes_hbm, mass_hbm, radial_hbm, stiff_hbm, iface_hbm, touch_out, at_iface, diag, coefs, touch, elem_nodes, mass, radial, stiff, iface, in_sems, out_sems):
    loads = start_all(
        (nodes_hbm, mass_hbm, radial_hbm, stiff_hbm, iface_hbm), (elem_nodes, mass, radial, stiff, iface), in_sems
    )
    for load in loads:
        load.wait()
    nodes, elems = touch.shape
    shared = iface.shape[1]
    fields = 8
    words = nodes // fields
    width = math.gcd(elems, 256)
    sent = []
    for c in range(elems // width):
        span = slice(c * width, (c + 1) * width)
        word = lax.broadcasted_iota(jnp.int32, (words, width), 0)
        total = jnp.zeros((words, width), jnp.int32)
        for i in range(elem_nodes.shape[0]):
            ids = elem_nodes[i : i + 1, span]
            field = ids // words
            value = jnp.left_shift(1, field * 4)
            total = total + jnp.where(ids - field * words == word, value, 0)
        for q in range(fields):
            count = jnp.right_shift(total, 4 * q) & 15
            touch[q * words : (q + 1) * words, span] = count.astype(f32).astype(bf16)
        column = pl.ds(c * width, width)
        sent.append(pltpu.make_async_copy(touch.at[:, column], touch_out.at[:, column], out_sems.at[c]))
        sent[-1].start()
    node = lax.broadcasted_iota(jnp.int32, (nodes, shared), 0)
    at_iface[...] = jnp.where(iface[...] == node, 1.0, 0.0).astype(bf16)
    zero = jnp.zeros((5, elems), f32)
    coefs[...] = jnp.concatenate([mass[...] / 12.0, radial[...] / 12.0, stiff[...], zero], axis=0)
    scaled = jnp.concatenate([mass[...] / 12.0, radial[...] / 12.0, 6.0 * stiff[...], zero], axis=0)
    sums = product(scaled, touch[...], 1, 3)
    ones = jnp.ones((16, shared), bf16)
    hits = lax.dot_general(ones, at_iface[...], (((1,), (1,)), ((), ())), preferred_element_type=f32)
    row = lax.broadcasted_iota(jnp.int32, (8, nodes), 0)
    diag[...] = jnp.where(row == 3, 1.0 - 0.5 * hits[:8], sums)
    for copy in sent:
        copy.wait()


def row_factors(rows, per_dev, modes):
    row = lax.broadcasted_iota(jnp.int32, (rows, 1), 0)
    order = (lax.axis_index("mode") * per_dev + row % per_dev).astype(f32)
    shift = (order / modes) ** 2
    scale = jnp.where(row < rows // 2, 1.0, diffusion_ratio).astype(f32)
    return shift, scale


def operator_parts(rows, per_dev, modes, coefs, diag):
    shift, scale = row_factors(rows, per_dev, modes)
    per_elem = coefs[0:1, :] + shift * coefs[1:2, :] - scale * coefs[2:3, :]
    per_node = diag[0:1, :] + shift * diag[1:2, :] + scale * diag[2:3, :]
    return per_elem, per_node


def row_sum(array):
    return jnp.sum(array, axis=1, keepdims=True)


def rhs_kernel(forcing, touch, at_iface, diag, coefs, local, edge):
    blocks = forcing.shape[0]
    given = jnp.concatenate([forcing[b] for b in range(blocks)], axis=1)
    sums = product(given, touch[...], 0)
    image = diag[0:1, :] * given + product(sums * coefs[0:1, :], touch[...], 1)
    local[...] = image
    edge[...] = product(image, at_iface[...], 0, 3)


def first_kernel(per_dev, modes, local, edge, touch, at_iface, diag, coefs, rhs_out, image_out, sums_out, edge_out):
    rows, shared = edge.shape
    per_elem, per_node = operator_parts(rows, per_dev, modes, coefs, diag)
    rhs = local[...] + product(edge[...], at_iface[...], 1, 3)
    rhs_out[...] = rhs
    sums = product(rhs, touch[...], 0)
    sums_out[...] = sums
    spread = per_elem * sums
    image = per_node * rhs + product(spread, touch[...], 1)
    image_out[...] = image
    norm = row_sum(diag[3:4, :] * rhs * rhs)
    curvature = row_sum(per_node * rhs * rhs) + row_sum(spread * sums)
    edge_out[:, :shared] = product(image, at_iface[...], 0, 3)
    lane = lax.broadcasted_iota(jnp.int32, (rows, 128), 1)
    edge_out[:, shared:] = jnp.where(lane == 0, norm, curvature)


def second_kernel(per_dev, modes, image, edge, own, touch, at_iface, diag, coefs, rhs, sums, resid_out, norms_out):
    rows = image.shape[0]
    shared = edge.shape[1] - 128
    per_elem, per_node = operator_parts(rows, per_dev, modes, coefs, diag)
    norm = own[:, shared : shared + 1] + edge[:, shared : shared + 1]
    curvature = own[:, shared + 1 : shared + 2] + edge[:, shared + 1 : shared + 2]
    alpha = norm / curvature
    full = image[...] + product(edge[:, :shared], at_iface[...], 1, 3)
    resid = rhs[...] - alpha * full
    resid_out[...] = resid
    new = product(resid, touch[...], 0)
    after = row_sum(diag[3:4, :] * resid * resid)
    square = row_sum(per_node * resid * resid) + row_sum(per_elem * new * new)
    mixed = row_sum(per_node * resid * rhs[...]) + row_sum(per_elem * new * sums[...])
    lane = lax.broadcasted_iota(jnp.int32, (rows, 128), 1)
    norms_out[...] = jnp.where(lane == 0, after, jnp.where(lane == 1, square, mixed))


def last_kernel(edge, own, norms_own, norms, resid, rhs, vel_out, mag_out):
    shared = edge.shape[1] - 128
    norm = own[:, shared : shared + 1] + edge[:, shared : shared + 1]
    curvature = own[:, shared + 1 : shared + 2] + edge[:, shared + 1 : shared + 2]
    alpha = norm / curvature
    after = norms_own[:, 0:1] + norms[:, 0:1]
    square = norms_own[:, 1:2] + norms[:, 1:2]
    mixed = norms_own[:, 2:3] + norms[:, 2:3]
    beta = after / norm
    alpha_next = after / (square + 2.0 * beta * mixed + beta * beta * curvature)
    answer = (alpha + alpha_next * beta) * rhs[...] + alpha_next * resid[...]
    row = 0
    for out in (vel_out, mag_out):
        comps, _, per_dev, _ = out.shape
        for c in range(comps):
            for s in range(2):
                out[c, s] = answer[row : row + per_dev]
                row += per_dev


def per_device(velocity, vorticity, magnetic, current, elem_nodes, mass_coef, stiff_coef, radial_coef, iface):
    comps, _, per_dev, nodes = velocity.shape
    owners = lax.axis_size("mode")
    modes = per_dev * owners
    block = nodes // owners
    rows = 4 * comps * per_dev
    elems = elem_nodes.shape[1]
    shared = iface.shape[1]
    mass, radial, stiff = (a.reshape(1, elems) for a in (mass_coef, radial_coef, stiff_coef))
    synthesis, analysis = trig_tables(modes, per_dev)

    def shape(*dims, kind=f32):
        return jax.ShapeDtypeStruct(dims, kind)

    in_hbm = pl.BlockSpec(memory_space=pltpu.HBM)
    if block % 128 == 0:
        packed = pl.pallas_call(
            pack_kernel,
            in_specs=[in_hbm] * 4,
            out_shape=shape(owners, 2 * rows, block),
            out_specs=in_hbm,
            scratch_shapes=[
                pltpu.VMEM((4, *velocity.shape), f32),
                pltpu.VMEM((owners, 2 * rows, block), f32),
                pltpu.SemaphoreType.DMA((4,)),
                pltpu.SemaphoreType.DMA((2,)),
            ],
            compiler_params=params(large),
            name="pack",
        )(velocity, magnetic, vorticity, current)
    else:
        packed = jnp.concatenate(
            [a.reshape(rows // 2, owners, block) for a in (velocity, magnetic, vorticity, current)], axis=0
        ).transpose(1, 0, 2)
    columns = lax.all_to_all(packed, "mode", 0, 0, tiled=True)
    tables = (
        shape(nodes, elems, kind=bf16),
        shape(nodes, shared, kind=bf16),
        shape(8, nodes),
        shape(8, elems),
    )
    in_vmem = pl.BlockSpec(memory_space=pltpu.VMEM)
    built = pl.pallas_call(
        mesh_kernel,
        in_specs=[in_hbm] * 5,
        out_specs=(in_hbm, in_vmem, in_vmem, in_vmem),
        out_shape=tables,
        scratch_shapes=[
            pltpu.VMEM((nodes, elems), bf16),
            pltpu.VMEM(elem_nodes.shape, jnp.int32),
            pltpu.VMEM((1, elems), f32),
            pltpu.VMEM((1, elems), f32),
            pltpu.VMEM((1, elems), f32),
            pltpu.VMEM(iface.shape, jnp.int32),
            pltpu.SemaphoreType.DMA((5,)),
            pltpu.SemaphoreType.DMA((elems // math.gcd(elems, 256),)),
        ],
        compiler_params=params(large),
        name="incidence",
        cost_estimate=pl.CostEstimate(flops=2**31, bytes_accessed=2**23, transcendentals=0),
    )(elem_nodes, mass, radial, stiff, iface)
    columns, *built = lax.optimization_barrier((columns, *built))
    terms, touch, at_iface, diag, coefs = pl.pallas_call(
        nonlinear_kernel,
        in_specs=[in_vmem] * 3 + [in_hbm] * 4,
        out_shape=(pltpu.VMEM((owners, rows, block), f32), *(pltpu.VMEM(t.shape, t.dtype) for t in tables)),
        scratch_shapes=[pltpu.SemaphoreType.DMA((7,))],
        compiler_params=params(medium),
        name="nonlinear",
    )(pltpu.with_memory_space_constraint(columns, pltpu.VMEM), synthesis, analysis, *built)
    forcing = lax.all_to_all(terms, "mode", 0, 0, tiled=True)
    if block % 128:
        forcing = forcing.transpose(1, 0, 2).reshape(1, rows, nodes)

    def swap(array):
        return lax.ppermute(array, "mer", [(0, 1), (1, 0)])

    local, edge = pl.pallas_call(
        rhs_kernel, out_shape=(shape(rows, nodes), shape(rows, shared)), compiler_params=params(), name="rhs"
    )(forcing, touch, at_iface, diag, coefs)
    rhs, image, sums, edge_own = pl.pallas_call(
        functools.partial(first_kernel, per_dev, modes),
        out_shape=(shape(rows, nodes), shape(rows, nodes), shape(rows, elems), shape(rows, shared + 128)),
        compiler_params=params(),
        name="first",
    )(local, swap(edge), touch, at_iface, diag, coefs)
    edge_other = swap(edge_own)
    resid, norms_own = pl.pallas_call(
        functools.partial(second_kernel, per_dev, modes),
        out_shape=(shape(rows, nodes), shape(rows, 128)),
        compiler_params=params(),
        name="second",
    )(image, edge_other, edge_own, touch, at_iface, diag, coefs, rhs, sums)
    out = shape(*velocity.shape)
    return pl.pallas_call(
        last_kernel, out_shape=(out, out), compiler_params=params(), name="last"
    )(edge_other, edge_own, norms_own, swap(norms_own), resid, rhs)


def solution(mesh):
    field = P("runs", None, "mode", "mer")
    placed = (field, field, field, field, P(None, "mer"), P("mer"), P("mer"), P("mer"), P("mer", None))
    return jax.shard_map(
        per_device, mesh=mesh, in_specs=placed, out_specs=(field, field), check_vma=False
    )
```

```python
import functools
import math

import jax
import jax.numpy as jnp
import numpy as np
from jax import lax
from jax.experimental import pallas as pl
from jax.experimental.pallas import tpu as pltpu
from jax.sharding import PartitionSpec as P

step_size = 0.05
diffusion_ratio = 2.0
f32 = jnp.float32
bf16 = jnp.bfloat16
small, medium, large = 16 * 2**20, 54 * 2**20, 60 * 2**20


def params(limit=small):
    return pltpu.CompilerParams(vmem_limit_bytes=limit)


def halves(table):
    high = table.astype(np.float32).astype(jnp.bfloat16)
    low = (table - high.astype(np.float64)).astype(np.float32).astype(jnp.bfloat16)
    return high, low


def trig_tables(modes, per_dev):
    angles = 2 * modes
    order = np.arange(modes)
    points = np.arange(angles)
    phase = (points[:, None] * order[None, :] % angles) * (2.0 * math.pi / angles)
    both = np.stack([np.cos(phase), np.sin(phase)])
    both = both.reshape(2, angles, modes // per_dev, per_dev)
    factor = np.where(order == 0, 1.0, 2.0).reshape(modes // per_dev, per_dev) / angles
    same = np.eye(2)
    synthesis = np.einsum("pq,sajk->pajqsk", same, both).reshape(2 * angles, -1)
    analysis = np.einsum("pq,sajk,jk->jqskpa", same, both, factor * step_size).reshape(-1, 2 * angles)
    out = []
    for table in (synthesis, analysis):
        high, low = halves(table)
        out.append(jnp.asarray(np.concatenate([high, high, low], axis=1)))
    return out


def pieces(array, count):
    parts = []
    rest = array
    for i in range(count):
        part = rest.astype(bf16).astype(f32)
        parts.append(part)
        rest = rest - part
    return jnp.concatenate(parts, axis=0).astype(bf16)


def product(array, exact, contract, count=2):
    rows = array.shape[0]
    out = lax.dot_general(
        pieces(array, count), exact, (((1,), (contract,)), ((), ())), preferred_element_type=f32
    )
    total = out[:rows]
    for i in range(1, count):
        total = total + out[i * rows : (i + 1) * rows]
    return total


def table_product(table, values):
    high = values.astype(bf16)
    low = (values - high.astype(f32)).astype(bf16)
    return jnp.dot(table, jnp.concatenate([high, low, high], axis=0), preferred_element_type=f32)


def start_all(sources, targets, sems):
    copies = [
        pltpu.make_async_copy(source, target, sems.at[i])
        for i, (source, target) in enumerate(zip(sources, targets))
    ]
    for copy in copies:
        copy.start()
    return copies


def pack_kernel(vel, mag, vort, cur, out, held, ready, in_sems, out_sems):
    blocks, rows, block = out.shape
    copies = start_all((vel, mag, vort, cur), [held.at[i] for i in range(4)], in_sems)
    sent = []
    row = 0
    for i in range(4):
        copies[i].wait()
        field = held.at[i]
        comps, _, per_dev, _ = field.shape
        for c in range(comps):
            for s in range(2):
                piece = field[c, s]
                for b in range(blocks):
                    ready[b, row : row + per_dev, :] = piece[:, b * block : (b + 1) * block]
                row += per_dev
        if i % 2:
            half = pl.ds(i // 2 * (rows // 2), rows // 2)
            sent.append(pltpu.make_async_copy(ready.at[:, half, :], out.at[:, half, :], out_sems.at[i // 2]))
            sent[-1].start()
    for copy in sent:
        copy.wait()


def nonlinear_kernel(fields, synthesis, analysis, out):
    owners, rows, block = fields.shape
    pair = rows // 6
    angles = synthesis.shape[0] // 2
    phys = []
    for t in range(6):
        coef = jnp.concatenate([fields[j, t * pair : (t + 1) * pair, :] for j in range(owners)], axis=0)
        values = table_product(synthesis[...], coef)
        phys += [values[:angles], values[angles:]]
    vel, mag, vort, cur = phys[0:3], phys[3:6], phys[6:9], phys[9:12]

    def cross(a, b, i):
        j, k = (i + 1) % 3, (i + 2) % 3
        return a[j] * b[k] - a[k] * b[j]

    terms = [cross(vel, vort, i) + cross(cur, mag, i) for i in range(3)]
    terms += [cross(vel, mag, i) for i in range(3)]
    for t in range(3):
        coef = table_product(analysis[...], jnp.concatenate([terms[2 * t], terms[2 * t + 1]], axis=0))
        for j in range(owners):
            span = slice(t * pair, (t + 1) * pair)
            out[j, span, :] = fields[j, span, :] + coef[j * pair : (j + 1) * pair]


def mesh_kernel(nodes_hbm, mass_hbm, radial_hbm, stiff_hbm, iface_hbm, touch_out, at_iface, diag, coefs, touch, elem_nodes, mass, radial, stiff, iface, in_sems, out_sems):
    loads = start_all(
        (nodes_hbm, mass_hbm, radial_hbm, stiff_hbm, iface_hbm), (elem_nodes, mass, radial, stiff, iface), in_sems
    )
    for load in loads:
        load.wait()
    nodes, elems = touch.shape
    shared = iface.shape[1]
    fields = 8
    words = nodes // fields
    width = math.gcd(elems, 256)
    sent = []
    for c in range(elems // width):
        span = slice(c * width, (c + 1) * width)
        word = lax.broadcasted_iota(jnp.int32, (words, width), 0)
        total = jnp.zeros((words, width), jnp.int32)
        for i in range(elem_nodes.shape[0]):
            ids = elem_nodes[i : i + 1, span]
            field = ids // words
            value = jnp.left_shift(1, field * 4)
            total = total + jnp.where(ids - field * words == word, value, 0)
        for q in range(fields):
            count = jnp.right_shift(total, 4 * q) & 15
            touch[q * words : (q + 1) * words, span] = count.astype(f32).astype(bf16)
        column = pl.ds(c * width, width)
        sent.append(pltpu.make_async_copy(touch.at[:, column], touch_out.at[:, column], out_sems.at[c]))
        sent[-1].start()
    node = lax.broadcasted_iota(jnp.int32, (nodes, shared), 0)
    at_iface[...] = jnp.where(iface[...] == node, 1.0, 0.0).astype(bf16)
    zero = jnp.zeros((5, elems), f32)
    coefs[...] = jnp.concatenate([mass[...] / 12.0, radial[...] / 12.0, stiff[...], zero], axis=0)
    scaled = jnp.concatenate([mass[...] / 12.0, radial[...] / 12.0, 6.0 * stiff[...], zero], axis=0)
    sums = product(scaled, touch[...], 1, 3)
    ones = jnp.ones((16, shared), bf16)
    hits = lax.dot_general(ones, at_iface[...], (((1,), (1,)), ((), ())), preferred_element_type=f32)
    row = lax.broadcasted_iota(jnp.int32, (8, nodes), 0)
    diag[...] = jnp.where(row == 3, 1.0 - 0.5 * hits[:8], sums)
    for copy in sent:
        copy.wait()


def row_factors(rows, per_dev, modes):
    row = lax.broadcasted_iota(jnp.int32, (rows, 1), 0)
    order = (lax.axis_index("mode") * per_dev + row % per_dev).astype(f32)
    shift = (order / modes) ** 2
    scale = jnp.where(row < rows // 2, 1.0, diffusion_ratio).astype(f32)
    return shift, scale


def operator_parts(rows, per_dev, modes, coefs, diag):
    shift, scale = row_factors(rows, per_dev, modes)
    per_elem = coefs[0:1, :] + shift * coefs[1:2, :] - scale * coefs[2:3, :]
    per_node = diag[0:1, :] + shift * diag[1:2, :] + scale * diag[2:3, :]
    return per_elem, per_node


def row_sum(array):
    return jnp.sum(array, axis=1, keepdims=True)


def rhs_kernel(forcing, touch, at_iface, diag, coefs, local, edge):
    blocks = forcing.shape[0]
    given = jnp.concatenate([forcing[b] for b in range(blocks)], axis=1)
    sums = product(given, touch[...], 0)
    image = diag[0:1, :] * given + product(sums * coefs[0:1, :], touch[...], 1)
    local[...] = image
    edge[...] = product(image, at_iface[...], 0, 3)


def first_kernel(per_dev, modes, local, edge, touch, at_iface, diag, coefs, rhs_out, image_out, sums_out, edge_out):
    rows, shared = edge.shape
    per_elem, per_node = operator_parts(rows, per_dev, modes, coefs, diag)
    rhs = local[...] + product(edge[...], at_iface[...], 1, 3)
    rhs_out[...] = rhs
    sums = product(rhs, touch[...], 0)
    sums_out[...] = sums
    spread = per_elem * sums
    image = per_node * rhs + product(spread, touch[...], 1)
    image_out[...] = image
    norm = row_sum(diag[3:4, :] * rhs * rhs)
    curvature = row_sum(per_node * rhs * rhs) + row_sum(spread * sums)
    edge_out[:, :shared] = product(image, at_iface[...], 0, 3)
    lane = lax.broadcasted_iota(jnp.int32, (rows, 128), 1)
    edge_out[:, shared:] = jnp.where(lane == 0, norm, curvature)


def second_kernel(per_dev, modes, image, edge, own, touch, at_iface, diag, coefs, rhs, sums, resid_out, norms_out):
    rows = image.shape[0]
    shared = edge.shape[1] - 128
    per_elem, per_node = operator_parts(rows, per_dev, modes, coefs, diag)
    norm = own[:, shared : shared + 1] + edge[:, shared : shared + 1]
    curvature = own[:, shared + 1 : shared + 2] + edge[:, shared + 1 : shared + 2]
    alpha = norm / curvature
    full = image[...] + product(edge[:, :shared], at_iface[...], 1, 3)
    resid = rhs[...] - alpha * full
    resid_out[...] = resid
    new = product(resid, touch[...], 0)
    after = row_sum(diag[3:4, :] * resid * resid)
    square = row_sum(per_node * resid * resid) + row_sum(per_elem * new * new)
    mixed = row_sum(per_node * resid * rhs[...]) + row_sum(per_elem * new * sums[...])
    lane = lax.broadcasted_iota(jnp.int32, (rows, 128), 1)
    norms_out[...] = jnp.where(lane == 0, after, jnp.where(lane == 1, square, mixed))


def last_kernel(edge, own, norms_own, norms, resid, rhs, vel_out, mag_out):
    shared = edge.shape[1] - 128
    norm = own[:, shared : shared + 1] + edge[:, shared : shared + 1]
    curvature = own[:, shared + 1 : shared + 2] + edge[:, shared + 1 : shared + 2]
    alpha = norm / curvature
    after = norms_own[:, 0:1] + norms[:, 0:1]
    square = norms_own[:, 1:2] + norms[:, 1:2]
    mixed = norms_own[:, 2:3] + norms[:, 2:3]
    beta = after / norm
    alpha_next = after / (square + 2.0 * beta * mixed + beta * beta * curvature)
    answer = (alpha + alpha_next * beta) * rhs[...] + alpha_next * resid[...]
    row = 0
    for out in (vel_out, mag_out):
        comps, _, per_dev, _ = out.shape
        for c in range(comps):
            for s in range(2):
                out[c, s] = answer[row : row + per_dev]
                row += per_dev


def per_device(velocity, vorticity, magnetic, current, elem_nodes, mass_coef, stiff_coef, radial_coef, iface):
    comps, _, per_dev, nodes = velocity.shape
    owners = lax.axis_size("mode")
    modes = per_dev * owners
    block = nodes // owners
    rows = 4 * comps * per_dev
    elems = elem_nodes.shape[1]
    shared = iface.shape[1]
    mass, radial, stiff = (a.reshape(1, elems) for a in (mass_coef, radial_coef, stiff_coef))
    synthesis, analysis = trig_tables(modes, per_dev)

    def shape(*dims, kind=f32):
        return jax.ShapeDtypeStruct(dims, kind)

    in_hbm = pl.BlockSpec(memory_space=pltpu.HBM)
    if block % 128 == 0:
        packed = pl.pallas_call(
            pack_kernel,
            in_specs=[in_hbm] * 4,
            out_shape=shape(owners, 2 * rows, block),
            out_specs=in_hbm,
            scratch_shapes=[
                pltpu.VMEM((4, *velocity.shape), f32),
                pltpu.VMEM((owners, 2 * rows, block), f32),
                pltpu.SemaphoreType.DMA((4,)),
                pltpu.SemaphoreType.DMA((2,)),
            ],
            compiler_params=params(large),
            name="pack",
        )(velocity, magnetic, vorticity, current)
    else:
        packed = jnp.concatenate(
            [a.reshape(rows // 2, owners, block) for a in (velocity, magnetic, vorticity, current)], axis=0
        ).transpose(1, 0, 2)
    columns = lax.all_to_all(packed, "mode", 0, 0, tiled=True)
    tables = (
        shape(nodes, elems, kind=bf16),
        shape(nodes, shared, kind=bf16),
        shape(8, nodes),
        shape(8, elems),
    )
    in_vmem = pl.BlockSpec(memory_space=pltpu.VMEM)
    built = pl.pallas_call(
        mesh_kernel,
        in_specs=[in_hbm] * 5,
        out_specs=(in_hbm, in_vmem, in_vmem, in_vmem),
        out_shape=tables,
        scratch_shapes=[
            pltpu.VMEM((nodes, elems), bf16),
            pltpu.VMEM(elem_nodes.shape, jnp.int32),
            pltpu.VMEM((1, elems), f32),
            pltpu.VMEM((1, elems), f32),
            pltpu.VMEM((1, elems), f32),
            pltpu.VMEM(iface.shape, jnp.int32),
            pltpu.SemaphoreType.DMA((5,)),
            pltpu.SemaphoreType.DMA((elems // math.gcd(elems, 256),)),
        ],
        compiler_params=params(large),
        name="incidence",
        cost_estimate=pl.CostEstimate(flops=2**31, bytes_accessed=2**23, transcendentals=0),
    )(elem_nodes, mass, radial, stiff, iface)
    columns, *built = lax.optimization_barrier((columns, *built))
    touch, at_iface, diag, coefs = built
    terms = pl.pallas_call(
        nonlinear_kernel,
        out_shape=pltpu.VMEM((owners, rows, block), f32),
        compiler_params=params(),
        name="nonlinear",
        cost_estimate=pl.CostEstimate(flops=2**33, bytes_accessed=2**24, transcendentals=0),
    )(pltpu.with_memory_space_constraint(columns, pltpu.VMEM), synthesis, analysis)
    forcing = lax.all_to_all(terms, "mode", 0, 0, tiled=True)
    if block % 128:
        forcing = forcing.transpose(1, 0, 2).reshape(1, rows, nodes)

    def swap(array):
        return lax.ppermute(array, "mer", [(0, 1), (1, 0)])

    local, edge = pl.pallas_call(
        rhs_kernel, out_shape=(shape(rows, nodes), shape(rows, shared)), compiler_params=params(), name="rhs"
    )(forcing, touch, at_iface, diag, coefs)
    rhs, image, sums, edge_own = pl.pallas_call(
        functools.partial(first_kernel, per_dev, modes),
        out_shape=(shape(rows, nodes), shape(rows, nodes), shape(rows, elems), shape(rows, shared + 128)),
        compiler_params=params(),
        name="first",
    )(local, swap(edge), touch, at_iface, diag, coefs)
    edge_other = swap(edge_own)
    resid, norms_own = pl.pallas_call(
        functools.partial(second_kernel, per_dev, modes),
        out_shape=(shape(rows, nodes), shape(rows, 128)),
        compiler_params=params(),
        name="second",
    )(image, edge_other, edge_own, touch, at_iface, diag, coefs, rhs, sums)
    out = shape(*velocity.shape)
    return pl.pallas_call(
        last_kernel, out_shape=(out, out), compiler_params=params(), name="last"
    )(edge_other, edge_own, norms_own, swap(norms_own), resid, rhs)


def solution(mesh):
    field = P("runs", None, "mode", "mer")
    placed = (field, field, field, field, P(None, "mer"), P("mer"), P("mer"), P("mer"), P("mer", None))
    return jax.shard_map(
        per_device, mesh=mesh, in_specs=placed, out_specs=(field, field), check_vma=False
    )
```

```python
import functools
import math

import jax
import jax.numpy as jnp
import numpy as np
from jax import lax
from jax.experimental import pallas as pl
from jax.experimental.pallas import tpu as pltpu
from jax.sharding import PartitionSpec as P

step_size = 0.05
diffusion_ratio = 2.0
f32 = jnp.float32
bf16 = jnp.bfloat16
small, medium, large = 16 * 2**20, 54 * 2**20, 60 * 2**20


def params(limit=small):
    return pltpu.CompilerParams(vmem_limit_bytes=limit)


def halves(table):
    high = table.astype(np.float32).astype(jnp.bfloat16)
    low = (table - high.astype(np.float64)).astype(np.float32).astype(jnp.bfloat16)
    return high, low


def trig_tables(modes, per_dev):
    angles = 2 * modes
    order = np.arange(modes)
    points = np.arange(angles)
    phase = (points[:, None] * order[None, :] % angles) * (2.0 * math.pi / angles)
    both = np.stack([np.cos(phase), np.sin(phase)])
    both = both.reshape(2, angles, modes // per_dev, per_dev)
    factor = np.where(order == 0, 1.0, 2.0).reshape(modes // per_dev, per_dev) / angles
    same = np.eye(2)
    synthesis = np.einsum("pq,sajk->pajqsk", same, both).reshape(2 * angles, -1)
    analysis = np.einsum("pq,sajk,jk->jqskpa", same, both, factor * step_size).reshape(-1, 2 * angles)
    out = []
    for table in (synthesis, analysis):
        high, low = halves(table)
        out.append(jnp.asarray(np.concatenate([high, high, low], axis=1)))
    return out


def pieces(array, count):
    parts = []
    rest = array
    for i in range(count):
        part = rest.astype(bf16).astype(f32)
        parts.append(part)
        rest = rest - part
    return jnp.concatenate(parts, axis=0).astype(bf16)


def product(array, exact, contract, count=2):
    rows = array.shape[0]
    out = lax.dot_general(
        pieces(array, count), exact, (((1,), (contract,)), ((), ())), preferred_element_type=f32
    )
    total = out[:rows]
    for i in range(1, count):
        total = total + out[i * rows : (i + 1) * rows]
    return total


def table_product(table, values):
    high = values.astype(bf16)
    low = (values - high.astype(f32)).astype(bf16)
    return jnp.dot(table, jnp.concatenate([high, low, high], axis=0), preferred_element_type=f32)


def start_all(sources, targets, sems):
    copies = [
        pltpu.make_async_copy(source, target, sems.at[i])
        for i, (source, target) in enumerate(zip(sources, targets))
    ]
    for copy in copies:
        copy.start()
    return copies


def pack_kernel(vel, mag, vort, cur, out, held, ready, in_sems, out_sems):
    blocks, rows, block = out.shape
    copies = start_all((vel, mag, vort, cur), [held.at[i] for i in range(4)], in_sems)
    sent = []
    row = 0
    for i in range(4):
        copies[i].wait()
        field = held.at[i]
        comps, _, per_dev, _ = field.shape
        for c in range(comps):
            for s in range(2):
                piece = field[c, s]
                for b in range(blocks):
                    ready[b, row : row + per_dev, :] = piece[:, b * block : (b + 1) * block]
                row += per_dev
        if i % 2:
            half = pl.ds(i // 2 * (rows // 2), rows // 2)
            sent.append(pltpu.make_async_copy(ready.at[:, half, :], out.at[:, half, :], out_sems.at[i // 2]))
            sent[-1].start()
    for copy in sent:
        copy.wait()


def nonlinear_kernel(fields, synthesis, analysis, out):
    owners, rows, block = fields.shape
    pair = rows // 6
    angles = synthesis.shape[0] // 2
    phys = []
    for t in range(6):
        coef = jnp.concatenate([fields[j, t * pair : (t + 1) * pair, :] for j in range(owners)], axis=0)
        values = table_product(synthesis[...], coef)
        phys += [values[:angles], values[angles:]]
    vel, mag, vort, cur = phys[0:3], phys[3:6], phys[6:9], phys[9:12]

    def cross(a, b, i):
        j, k = (i + 1) % 3, (i + 2) % 3
        return a[j] * b[k] - a[k] * b[j]

    terms = [cross(vel, vort, i) + cross(cur, mag, i) for i in range(3)]
    terms += [cross(vel, mag, i) for i in range(3)]
    for t in range(3):
        coef = table_product(analysis[...], jnp.concatenate([terms[2 * t], terms[2 * t + 1]], axis=0))
        for j in range(owners):
            span = slice(t * pair, (t + 1) * pair)
            out[j, span, :] = fields[j, span, :] + coef[j * pair : (j + 1) * pair]


def mesh_kernel(nodes_hbm, mass_hbm, radial_hbm, stiff_hbm, iface_hbm, touch_out, at_iface, diag, coefs, edge_touch, edge_diag, touch, elem_nodes, mass, radial, stiff, iface, in_sems, out_sems):
    loads = start_all(
        (nodes_hbm, mass_hbm, radial_hbm, stiff_hbm, iface_hbm), (elem_nodes, mass, radial, stiff, iface), in_sems
    )
    for load in loads:
        load.wait()
    nodes, elems = touch.shape
    shared = iface.shape[1]
    fields = 8
    words = nodes // fields
    width = math.gcd(elems, 256)
    sent = []
    for c in range(elems // width):
        span = slice(c * width, (c + 1) * width)
        word = lax.broadcasted_iota(jnp.int32, (words, width), 0)
        total = jnp.zeros((words, width), jnp.int32)
        for i in range(elem_nodes.shape[0]):
            ids = elem_nodes[i : i + 1, span]
            field = ids // words
            value = jnp.left_shift(1, field * 4)
            total = total + jnp.where(ids - field * words == word, value, 0)
        for q in range(fields):
            count = jnp.right_shift(total, 4 * q) & 15
            touch[q * words : (q + 1) * words, span] = count.astype(f32).astype(bf16)
        column = pl.ds(c * width, width)
        sent.append(pltpu.make_async_copy(touch.at[:, column], touch_out.at[:, column], out_sems.at[c]))
        sent[-1].start()
    node = lax.broadcasted_iota(jnp.int32, (nodes, shared), 0)
    at_iface[...] = jnp.where(iface[...] == node, 1.0, 0.0).astype(bf16)
    zero = jnp.zeros((5, elems), f32)
    coefs[...] = jnp.concatenate([mass[...] / 12.0, radial[...] / 12.0, stiff[...], zero], axis=0)
    scaled = jnp.concatenate([mass[...] / 12.0, radial[...] / 12.0, 6.0 * stiff[...], zero], axis=0)
    sums = product(scaled, touch[...], 1, 3)
    ones = jnp.ones((16, shared), bf16)
    hits = lax.dot_general(ones, at_iface[...], (((1,), (1,)), ((), ())), preferred_element_type=f32)
    row = lax.broadcasted_iota(jnp.int32, (8, nodes), 0)
    diag[...] = jnp.where(row == 3, 1.0 - 0.5 * hits[:8], sums)
    edge_diag[...] = product(sums, at_iface[...], 0, 3)
    counts = lax.dot_general(at_iface[...], touch[...], (((0,), (0,)), ((), ())), preferred_element_type=f32)
    edge_touch[...] = counts.astype(bf16)
    for copy in sent:
        copy.wait()


def row_factors(rows, per_dev, modes):
    row = lax.broadcasted_iota(jnp.int32, (rows, 1), 0)
    order = (lax.axis_index("mode") * per_dev + row % per_dev).astype(f32)
    shift = (order / modes) ** 2
    scale = jnp.where(row < rows // 2, 1.0, diffusion_ratio).astype(f32)
    return shift, scale


def at_elems(factors, coefs):
    shift, scale = factors
    return coefs[0:1, :] + shift * coefs[1:2, :] - scale * coefs[2:3, :]


def at_nodes(factors, diag):
    shift, scale = factors
    return diag[0:1, :] + shift * diag[1:2, :] + scale * diag[2:3, :]


def row_sum(array):
    return jnp.sum(array, axis=1, keepdims=True)


def lanes(*columns):
    rows = columns[0].shape[0]
    lane = lax.broadcasted_iota(jnp.int32, (rows, 128), 1)
    out = jnp.broadcast_to(columns[-1], (rows, 128))
    for i in reversed(range(len(columns) - 1)):
        out = jnp.where(lane == i, columns[i], out)
    return out


def together(forcing):
    return jnp.concatenate([forcing[b] for b in range(forcing.shape[0])], axis=1)


def rhs_edge_kernel(forcing, touch, at_iface, edge_touch, edge_diag, coefs, spread_out, edge):
    given = together(forcing)
    spread = product(given, touch[...], 0) * coefs[0:1, :]
    spread_out[...] = spread
    edge[...] = edge_diag[0:1, :] * product(given, at_iface[...], 0, 3) + product(spread, edge_touch[...], 1, 3)


def rhs_kernel(per_dev, modes, forcing, spread, touch, diag, local, sums, inner):
    rows = spread.shape[0]
    image = diag[0:1, :] * together(forcing) + product(spread[...], touch[...], 1)
    local[...] = image
    sums[...] = product(image, touch[...], 0)
    square = (2.0 * diag[3:4, :] - 1.0) * image * image
    inner[...] = lanes(row_sum(square), row_sum(at_nodes(row_factors(rows, per_dev, modes), diag) * square))


def image_edge_kernel(per_dev, modes, edge_own, edge, sums, inner, edge_touch, edge_diag, coefs, sums_out, out):
    rows, shared = edge.shape
    factors = row_factors(rows, per_dev, modes)
    rhs = edge_own[...] + edge[...]
    full = sums[...] + product(edge[...], edge_touch[...], 0, 3)
    sums_out[...] = full
    spread = at_elems(factors, coefs) * full
    image = at_nodes(factors, edge_diag) * rhs
    norm = inner[:, 0:1] + 0.5 * row_sum(rhs * rhs)
    curvature = inner[:, 1:2] + row_sum(image * rhs) + row_sum(spread * full)
    out[:, :shared] = image + product(spread, edge_touch[...], 1, 3)
    out[:, shared:] = lanes(norm, curvature)


def image_kernel(per_dev, modes, local, edge, sums, touch, at_iface, diag, coefs, rhs_out, image_out, sums_out):
    factors = row_factors(local.shape[0], per_dev, modes)
    rhs = local[...] + product(edge[...], at_iface[...], 1, 3)
    rhs_out[...] = rhs
    image = at_nodes(factors, diag) * rhs + product(at_elems(factors, coefs) * sums[...], touch[...], 1)
    image_out[...] = image
    sums_out[...] = product(image, touch[...], 0)


def resid_kernel(per_dev, modes, own, edge, rhs, image, sums, image_sums, at_iface, edge_touch, diag, coefs, resid_out, norms_out):
    rows = rhs.shape[0]
    shared = edge.shape[1] - 128
    factors = row_factors(rows, per_dev, modes)
    per_elem, per_node = at_elems(factors, coefs), at_nodes(factors, diag)
    norm = own[:, shared : shared + 1] + edge[:, shared : shared + 1]
    curvature = own[:, shared + 1 : shared + 2] + edge[:, shared + 1 : shared + 2]
    alpha = norm / curvature
    given = edge[:, :shared]
    resid = rhs[...] - alpha * (image[...] + product(given, at_iface[...], 1, 3))
    resid_out[...] = resid
    new = sums[...] - alpha * (image_sums[...] + product(given, edge_touch[...], 0, 3))
    after = row_sum(diag[3:4, :] * resid * resid)
    square = row_sum(per_node * resid * resid) + row_sum(per_elem * new * new)
    mixed = row_sum(per_node * resid * rhs[...]) + row_sum(per_elem * new * sums[...])
    norms_out[...] = lanes(after, square, mixed)


def last_kernel(edge, own, norms_own, norms, resid, rhs, vel_out, mag_out):
    shared = edge.shape[1] - 128
    norm = own[:, shared : shared + 1] + edge[:, shared : shared + 1]
    curvature = own[:, shared + 1 : shared + 2] + edge[:, shared + 1 : shared + 2]
    alpha = norm / curvature
    after = norms_own[:, 0:1] + norms[:, 0:1]
    square = norms_own[:, 1:2] + norms[:, 1:2]
    mixed = norms_own[:, 2:3] + norms[:, 2:3]
    beta = after / norm
    alpha_next = after / (square + 2.0 * beta * mixed + beta * beta * curvature)
    answer = (alpha + alpha_next * beta) * rhs[...] + alpha_next * resid[...]
    row = 0
    for out in (vel_out, mag_out):
        comps, _, per_dev, _ = out.shape
        for c in range(comps):
            for s in range(2):
                out[c, s] = answer[row : row + per_dev]
                row += per_dev


def per_device(velocity, vorticity, magnetic, current, elem_nodes, mass_coef, stiff_coef, radial_coef, iface):
    comps, _, per_dev, nodes = velocity.shape
    owners = lax.axis_size("mode")
    modes = per_dev * owners
    block = nodes // owners
    rows = 4 * comps * per_dev
    elems = elem_nodes.shape[1]
    shared = iface.shape[1]
    mass, radial, stiff = (a.reshape(1, elems) for a in (mass_coef, radial_coef, stiff_coef))
    synthesis, analysis = trig_tables(modes, per_dev)

    def shape(*dims, kind=f32):
        return jax.ShapeDtypeStruct(dims, kind)

    in_hbm = pl.BlockSpec(memory_space=pltpu.HBM)
    if block % 128 == 0:
        packed = pl.pallas_call(
            pack_kernel,
            in_specs=[in_hbm] * 4,
            out_shape=shape(owners, 2 * rows, block),
            out_specs=in_hbm,
            scratch_shapes=[
                pltpu.VMEM((4, *velocity.shape), f32),
                pltpu.VMEM((owners, 2 * rows, block), f32),
                pltpu.SemaphoreType.DMA((4,)),
                pltpu.SemaphoreType.DMA((2,)),
            ],
            compiler_params=params(large),
            name="pack",
        )(velocity, magnetic, vorticity, current)
    else:
        packed = jnp.concatenate(
            [a.reshape(rows // 2, owners, block) for a in (velocity, magnetic, vorticity, current)], axis=0
        ).transpose(1, 0, 2)
    columns = lax.all_to_all(packed, "mode", 0, 0, tiled=True)
    tables = (
        shape(nodes, elems, kind=bf16),
        shape(nodes, shared, kind=bf16),
        shape(8, nodes),
        shape(8, elems),
        shape(shared, elems, kind=bf16),
        shape(8, shared),
    )
    in_vmem = pl.BlockSpec(memory_space=pltpu.VMEM)
    built = pl.pallas_call(
        mesh_kernel,
        in_specs=[in_hbm] * 5,
        out_specs=(in_hbm, *[in_vmem] * 5),
        out_shape=tables,
        scratch_shapes=[
            pltpu.VMEM((nodes, elems), bf16),
            pltpu.VMEM(elem_nodes.shape, jnp.int32),
            pltpu.VMEM((1, elems), f32),
            pltpu.VMEM((1, elems), f32),
            pltpu.VMEM((1, elems), f32),
            pltpu.VMEM(iface.shape, jnp.int32),
            pltpu.SemaphoreType.DMA((5,)),
            pltpu.SemaphoreType.DMA((elems // math.gcd(elems, 256),)),
        ],
        compiler_params=params(large),
        name="incidence",
        cost_estimate=pl.CostEstimate(flops=2**31, bytes_accessed=2**23, transcendentals=0),
    )(elem_nodes, mass, radial, stiff, iface)
    columns, *built = lax.optimization_barrier((columns, *built))
    touch, at_iface, diag, coefs, edge_touch, edge_diag = built
    terms = pl.pallas_call(
        nonlinear_kernel,
        out_shape=pltpu.VMEM((owners, rows, block), f32),
        compiler_params=params(),
        name="nonlinear",
        cost_estimate=pl.CostEstimate(flops=2**33, bytes_accessed=2**24, transcendentals=0),
    )(pltpu.with_memory_space_constraint(columns, pltpu.VMEM), synthesis, analysis)
    forcing = lax.all_to_all(terms, "mode", 0, 0, tiled=True)
    if block % 128:
        forcing = forcing.transpose(1, 0, 2).reshape(1, rows, nodes)

    def swap(array):
        return lax.ppermute(array, "mer", [(0, 1), (1, 0)])

    def call(kernel, name, outs, work=0):
        own = () if kernel is rhs_edge_kernel else (per_dev, modes)
        cost = pl.CostEstimate(flops=work, bytes_accessed=work // 512, transcendentals=0) if work else None
        return pl.pallas_call(
            functools.partial(kernel, *own),
            out_shape=tuple(outs),
            compiler_params=params(),
            name=name,
            cost_estimate=cost,
        )

    full, part, small_row = shape(rows, nodes), shape(rows, elems), shape(rows, 128)
    spread, edge_own = call(rhs_edge_kernel, "rhs_edge", (part, shape(rows, shared)))(
        forcing, touch, at_iface, edge_touch, edge_diag, coefs
    )
    edge = swap(edge_own)
    local, sums, inner = call(rhs_kernel, "rhs", (full, part, small_row), 2**30)(forcing, spread, touch, diag)
    sums, image_edge_own = call(image_edge_kernel, "image_edge", (part, shape(rows, shared + 128)))(
        edge_own, edge, sums, inner, edge_touch, edge_diag, coefs
    )
    image_edge = swap(image_edge_own)
    rhs, image, image_sums = call(image_kernel, "image", (full, full, part), 2**30)(
        local, edge, sums, touch, at_iface, diag, coefs
    )
    resid, norms_own = call(resid_kernel, "resid", (full, small_row))(
        image_edge_own, image_edge, rhs, image, sums, image_sums, at_iface, edge_touch, diag, coefs
    )
    out = shape(*velocity.shape)
    return pl.pallas_call(
        last_kernel, out_shape=(out, out), compiler_params=params(), name="last"
    )(image_edge, image_edge_own, norms_own, swap(norms_own), resid, rhs)


def solution(mesh):
    field = P("runs", None, "mode", "mer")
    placed = (field, field, field, field, P(None, "mer"), P("mer"), P("mer"), P("mer"), P("mer", None))
    return jax.shard_map(
        per_device, mesh=mesh, in_specs=placed, out_specs=(field, field), check_vma=False
    )
```

```python
import functools
import math

import jax
import jax.numpy as jnp
import numpy as np
from jax import lax
from jax.experimental import pallas as pl
from jax.experimental.pallas import tpu as pltpu
from jax.sharding import PartitionSpec as P

step_size = 0.05
diffusion_ratio = 2.0
f32 = jnp.float32
bf16 = jnp.bfloat16
small, medium, large = 16 * 2**20, 54 * 2**20, 60 * 2**20


def params(limit=small):
    return pltpu.CompilerParams(vmem_limit_bytes=limit)


def halves(table):
    high = table.astype(np.float32).astype(jnp.bfloat16)
    low = (table - high.astype(np.float64)).astype(np.float32).astype(jnp.bfloat16)
    return high, low


def trig_tables(modes, per_dev):
    angles = 2 * modes
    order = np.arange(modes)
    points = np.arange(angles)
    phase = (points[:, None] * order[None, :] % angles) * (2.0 * math.pi / angles)
    both = np.stack([np.cos(phase), np.sin(phase)])
    both = both.reshape(2, angles, modes // per_dev, per_dev)
    factor = np.where(order == 0, 1.0, 2.0).reshape(modes // per_dev, per_dev) / angles
    same = np.eye(2)
    synthesis = np.einsum("pq,sajk->pajqsk", same, both).reshape(2 * angles, -1)
    analysis = np.einsum("pq,sajk,jk->jqskpa", same, both, factor * step_size).reshape(-1, 2 * angles)
    out = []
    for table in (synthesis, analysis):
        high, low = halves(table)
        out.append(jnp.asarray(np.concatenate([high, high, low], axis=1)))
    return out


def pieces(array, count):
    parts = []
    rest = array
    for i in range(count):
        part = rest.astype(bf16).astype(f32)
        parts.append(part)
        rest = rest - part
    return jnp.concatenate(parts, axis=0).astype(bf16)


def product(array, exact, count=2):
    rows = array.shape[0]
    out = jnp.dot(pieces(array, count), exact[...], preferred_element_type=f32)
    total = out[:rows]
    for i in range(1, count):
        total = total + out[i * rows : (i + 1) * rows]
    return total


def table_product(table, values):
    high = values.astype(bf16)
    low = (values - high.astype(f32)).astype(bf16)
    return jnp.dot(table, jnp.concatenate([high, low, high], axis=0), preferred_element_type=f32)


def start_all(sources, targets, sems):
    copies = [
        pltpu.make_async_copy(source, target, sems.at[i])
        for i, (source, target) in enumerate(zip(sources, targets))
    ]
    for copy in copies:
        copy.start()
    return copies


def pack_kernel(vel, mag, vort, cur, out, held, ready, in_sems, out_sems):
    blocks, rows, block = out.shape
    copies = start_all((vel, mag, vort, cur), [held.at[i] for i in range(4)], in_sems)
    sent = []
    row = 0
    for i in range(4):
        copies[i].wait()
        field = held.at[i]
        comps, _, per_dev, _ = field.shape
        for c in range(comps):
            for s in range(2):
                piece = field[c, s]
                for b in range(blocks):
                    ready[b, row : row + per_dev, :] = piece[:, b * block : (b + 1) * block]
                row += per_dev
        if i % 2:
            half = pl.ds(i // 2 * (rows // 2), rows // 2)
            sent.append(pltpu.make_async_copy(ready.at[:, half, :], out.at[:, half, :], out_sems.at[i // 2]))
            sent[-1].start()
    for copy in sent:
        copy.wait()


def nonlinear_kernel(fields, synthesis, analysis, out):
    owners, rows, block = fields.shape
    pair = rows // 6
    angles = synthesis.shape[0] // 2
    phys = []
    for t in range(6):
        coef = jnp.concatenate([fields[j, t * pair : (t + 1) * pair, :] for j in range(owners)], axis=0)
        values = table_product(synthesis[...], coef)
        phys += [values[:angles], values[angles:]]
    vel, mag, vort, cur = phys[0:3], phys[3:6], phys[6:9], phys[9:12]

    def cross(a, b, i):
        j, k = (i + 1) % 3, (i + 2) % 3
        return a[j] * b[k] - a[k] * b[j]

    terms = [cross(vel, vort, i) + cross(cur, mag, i) for i in range(3)]
    terms += [cross(vel, mag, i) for i in range(3)]
    for t in range(3):
        coef = table_product(analysis[...], jnp.concatenate([terms[2 * t], terms[2 * t + 1]], axis=0))
        for j in range(owners):
            span = slice(t * pair, (t + 1) * pair)
            out[j, span, :] = fields[j, span, :] + coef[j * pair : (j + 1) * pair]


def mesh_kernel(nodes_hbm, mass_hbm, radial_hbm, stiff_hbm, iface_hbm, touch_out, back_out, at_iface, from_iface, diag, coefs, edge_touch, edge_back, edge_diag, touch, back, elem_nodes, mass, radial, stiff, iface, in_sems, out_sems):
    loads = start_all(
        (nodes_hbm, mass_hbm, radial_hbm, stiff_hbm, iface_hbm), (elem_nodes, mass, radial, stiff, iface), in_sems
    )
    for load in loads:
        load.wait()
    nodes, elems = touch.shape
    shared = iface.shape[1]
    fields = 8
    words = nodes // fields
    width = math.gcd(elems, 256)
    sent = []
    for c in range(elems // width):
        span = slice(c * width, (c + 1) * width)
        word = lax.broadcasted_iota(jnp.int32, (words, width), 0)
        total = jnp.zeros((words, width), jnp.int32)
        for i in range(elem_nodes.shape[0]):
            ids = elem_nodes[i : i + 1, span]
            field = ids // words
            value = jnp.left_shift(1, field * 4)
            total = total + jnp.where(ids - field * words == word, value, 0)
        for q in range(fields):
            count = jnp.right_shift(total, 4 * q) & 15
            touch[q * words : (q + 1) * words, span] = count.astype(f32).astype(bf16)
        column = pl.ds(c * width, width)
        sent.append(pltpu.make_async_copy(touch.at[:, column], touch_out.at[:, column], out_sems.at[c]))
        sent[-1].start()
        back[span, :] = touch[:, span].T
        sent.append(pltpu.make_async_copy(back.at[column, :], back_out.at[column, :], out_sems.at[elems // width + c]))
        sent[-1].start()
    node = lax.broadcasted_iota(jnp.int32, (nodes, shared), 0)
    hit = jnp.where(iface[...] == node, 1.0, 0.0)
    at_iface[...] = hit.astype(bf16)
    from_iface[...] = hit.T.astype(bf16)
    zero = jnp.zeros((5, elems), f32)
    coefs[...] = jnp.concatenate([mass[...] / 12.0, radial[...] / 12.0, stiff[...], zero], axis=0)
    scaled = jnp.concatenate([mass[...] / 12.0, radial[...] / 12.0, 6.0 * stiff[...], zero], axis=0)
    sums = product(scaled, back, 3)
    hits = jnp.dot(jnp.ones((16, shared), bf16), from_iface[...], preferred_element_type=f32)
    row = lax.broadcasted_iota(jnp.int32, (8, nodes), 0)
    diag[...] = jnp.where(row == 3, 1.0 - 0.5 * hits[:8], sums)
    edge_diag[...] = product(sums, at_iface, 3)
    counts = jnp.dot(from_iface[...], touch[...], preferred_element_type=f32)
    edge_touch[...] = counts.astype(bf16)
    edge_back[...] = counts.T.astype(bf16)
    for copy in sent:
        copy.wait()


def row_factors(rows, per_dev, modes):
    row = lax.broadcasted_iota(jnp.int32, (rows, 1), 0)
    order = (lax.axis_index("mode") * per_dev + row % per_dev).astype(f32)
    shift = (order / modes) ** 2
    scale = jnp.where(row < rows // 2, 1.0, diffusion_ratio).astype(f32)
    return shift, scale


def at_elems(factors, coefs):
    shift, scale = factors
    return coefs[0:1, :] + shift * coefs[1:2, :] - scale * coefs[2:3, :]


def at_nodes(factors, diag):
    shift, scale = factors
    return diag[0:1, :] + shift * diag[1:2, :] + scale * diag[2:3, :]


def row_sum(array):
    return jnp.sum(array, axis=1, keepdims=True)


def lanes(*columns):
    rows = columns[0].shape[0]
    lane = lax.broadcasted_iota(jnp.int32, (rows, 128), 1)
    out = jnp.broadcast_to(columns[-1], (rows, 128))
    for i in reversed(range(len(columns) - 1)):
        out = jnp.where(lane == i, columns[i], out)
    return out


def together(forcing):
    return jnp.concatenate([forcing[b] for b in range(forcing.shape[0])], axis=1)


def rhs_edge_kernel(forcing, touch, at_iface, edge_back, edge_diag, coefs, spread_out, edge):
    given = together(forcing)
    spread = product(given, touch) * coefs[0:1, :]
    spread_out[...] = spread
    edge[...] = edge_diag[0:1, :] * product(given, at_iface, 3) + product(spread, edge_back, 3)


def rhs_kernel(per_dev, modes, forcing, spread, touch, back, diag, local, sums, inner):
    rows = spread.shape[0]
    image = diag[0:1, :] * together(forcing) + product(spread[...], back)
    local[...] = image
    sums[...] = product(image, touch)
    square = (2.0 * diag[3:4, :] - 1.0) * image * image
    inner[...] = lanes(row_sum(square), row_sum(at_nodes(row_factors(rows, per_dev, modes), diag) * square))


def image_edge_kernel(per_dev, modes, edge_own, edge, sums, inner, edge_touch, edge_back, edge_diag, coefs, sums_out, out):
    rows, shared = edge.shape
    factors = row_factors(rows, per_dev, modes)
    rhs = edge_own[...] + edge[...]
    full = sums[...] + product(edge[...], edge_touch, 3)
    sums_out[...] = full
    spread = at_elems(factors, coefs) * full
    image = at_nodes(factors, edge_diag) * rhs
    norm = inner[:, 0:1] + 0.5 * row_sum(rhs * rhs)
    curvature = inner[:, 1:2] + row_sum(image * rhs) + row_sum(spread * full)
    out[:, :shared] = image + product(spread, edge_back, 3)
    out[:, shared:] = lanes(norm, curvature)


def image_kernel(per_dev, modes, local, edge, sums, touch, back, from_iface, diag, coefs, rhs_out, image_out, sums_out):
    factors = row_factors(local.shape[0], per_dev, modes)
    rhs = local[...] + product(edge[...], from_iface, 3)
    rhs_out[...] = rhs
    image = at_nodes(factors, diag) * rhs + product(at_elems(factors, coefs) * sums[...], back)
    image_out[...] = image
    sums_out[...] = product(image, touch)


def resid_kernel(per_dev, modes, own, edge, rhs, image, sums, image_sums, from_iface, edge_touch, diag, coefs, resid_out, norms_out):
    rows = rhs.shape[0]
    shared = edge.shape[1] - 128
    factors = row_factors(rows, per_dev, modes)
    per_elem, per_node = at_elems(factors, coefs), at_nodes(factors, diag)
    norm = own[:, shared : shared + 1] + edge[:, shared : shared + 1]
    curvature = own[:, shared + 1 : shared + 2] + edge[:, shared + 1 : shared + 2]
    alpha = norm / curvature
    given = edge[:, :shared]
    resid = rhs[...] - alpha * (image[...] + product(given, from_iface, 3))
    resid_out[...] = resid
    new = sums[...] - alpha * (image_sums[...] + product(given, edge_touch, 3))
    after = row_sum(diag[3:4, :] * resid * resid)
    square = row_sum(per_node * resid * resid) + row_sum(per_elem * new * new)
    mixed = row_sum(per_node * resid * rhs[...]) + row_sum(per_elem * new * sums[...])
    norms_out[...] = lanes(after, square, mixed)


def last_kernel(edge, own, norms_own, norms, resid, rhs, vel_out, mag_out):
    shared = edge.shape[1] - 128
    norm = own[:, shared : shared + 1] + edge[:, shared : shared + 1]
    curvature = own[:, shared + 1 : shared + 2] + edge[:, shared + 1 : shared + 2]
    alpha = norm / curvature
    after = norms_own[:, 0:1] + norms[:, 0:1]
    square = norms_own[:, 1:2] + norms[:, 1:2]
    mixed = norms_own[:, 2:3] + norms[:, 2:3]
    beta = after / norm
    alpha_next = after / (square + 2.0 * beta * mixed + beta * beta * curvature)
    answer = (alpha + alpha_next * beta) * rhs[...] + alpha_next * resid[...]
    row = 0
    for out in (vel_out, mag_out):
        comps, _, per_dev, _ = out.shape
        for c in range(comps):
            for s in range(2):
                out[c, s] = answer[row : row + per_dev]
                row += per_dev


def per_device(velocity, vorticity, magnetic, current, elem_nodes, mass_coef, stiff_coef, radial_coef, iface):
    comps, _, per_dev, nodes = velocity.shape
    owners = lax.axis_size("mode")
    modes = per_dev * owners
    block = nodes // owners
    rows = 4 * comps * per_dev
    elems = elem_nodes.shape[1]
    shared = iface.shape[1]
    mass, radial, stiff = (a.reshape(1, elems) for a in (mass_coef, radial_coef, stiff_coef))
    synthesis, analysis = trig_tables(modes, per_dev)

    def shape(*dims, kind=f32):
        return jax.ShapeDtypeStruct(dims, kind)

    in_hbm = pl.BlockSpec(memory_space=pltpu.HBM)
    if block % 128 == 0:
        packed = pl.pallas_call(
            pack_kernel,
            in_specs=[in_hbm] * 4,
            out_shape=shape(owners, 2 * rows, block),
            out_specs=in_hbm,
            scratch_shapes=[
                pltpu.VMEM((4, *velocity.shape), f32),
                pltpu.VMEM((owners, 2 * rows, block), f32),
                pltpu.SemaphoreType.DMA((4,)),
                pltpu.SemaphoreType.DMA((2,)),
            ],
            compiler_params=params(large),
            name="pack",
        )(velocity, magnetic, vorticity, current)
    else:
        packed = jnp.concatenate(
            [a.reshape(rows // 2, owners, block) for a in (velocity, magnetic, vorticity, current)], axis=0
        ).transpose(1, 0, 2)
    columns = lax.all_to_all(packed, "mode", 0, 0, tiled=True)
    tables = (
        shape(nodes, elems, kind=bf16),
        shape(elems, nodes, kind=bf16),
        shape(nodes, shared, kind=bf16),
        shape(shared, nodes, kind=bf16),
        shape(8, nodes),
        shape(8, elems),
        shape(shared, elems, kind=bf16),
        shape(elems, shared, kind=bf16),
        shape(8, shared),
    )
    in_vmem = pl.BlockSpec(memory_space=pltpu.VMEM)
    built = pl.pallas_call(
        mesh_kernel,
        in_specs=[in_hbm] * 5,
        out_specs=(in_hbm, in_hbm, *[in_vmem] * 7),
        out_shape=tables,
        scratch_shapes=[
            pltpu.VMEM((nodes, elems), bf16),
            pltpu.VMEM((elems, nodes), bf16),
            pltpu.VMEM(elem_nodes.shape, jnp.int32),
            pltpu.VMEM((1, elems), f32),
            pltpu.VMEM((1, elems), f32),
            pltpu.VMEM((1, elems), f32),
            pltpu.VMEM(iface.shape, jnp.int32),
            pltpu.SemaphoreType.DMA((5,)),
            pltpu.SemaphoreType.DMA((2 * elems // math.gcd(elems, 256),)),
        ],
        compiler_params=params(large),
        name="incidence",
        cost_estimate=pl.CostEstimate(flops=2**31, bytes_accessed=2**23, transcendentals=0),
    )(elem_nodes, mass, radial, stiff, iface)
    columns, *built = lax.optimization_barrier((columns, *built))
    touch, back, at_iface, from_iface, diag, coefs, edge_touch, edge_back, edge_diag = built
    terms = pl.pallas_call(
        nonlinear_kernel,
        out_shape=pltpu.VMEM((owners, rows, block), f32),
        compiler_params=params(),
        name="nonlinear",
        cost_estimate=pl.CostEstimate(flops=2**33, bytes_accessed=2**24, transcendentals=0),
    )(pltpu.with_memory_space_constraint(columns, pltpu.VMEM), synthesis, analysis)
    forcing = lax.all_to_all(terms, "mode", 0, 0, tiled=True)
    if block % 128:
        forcing = forcing.transpose(1, 0, 2).reshape(1, rows, nodes)

    def swap(array):
        return lax.ppermute(array, "mer", [(0, 1), (1, 0)])

    def call(kernel, name, outs, work=0):
        own = () if kernel is rhs_edge_kernel else (per_dev, modes)
        cost = pl.CostEstimate(flops=work, bytes_accessed=work // 512, transcendentals=0) if work else None
        return pl.pallas_call(
            functools.partial(kernel, *own),
            out_shape=tuple(outs),
            compiler_params=params(),
            name=name,
            cost_estimate=cost,
        )

    full, part, small_row = shape(rows, nodes), shape(rows, elems), shape(rows, 128)
    spread, edge_own = call(rhs_edge_kernel, "rhs_edge", (part, shape(rows, shared)))(
        forcing, touch, at_iface, edge_back, edge_diag, coefs
    )
    edge = swap(edge_own)
    local, sums, inner = call(rhs_kernel, "rhs", (full, part, small_row), 2**30)(
        forcing, spread, touch, back, diag
    )
    sums, image_edge_own = call(image_edge_kernel, "image_edge", (part, shape(rows, shared + 128)))(
        edge_own, edge, sums, inner, edge_touch, edge_back, edge_diag, coefs
    )
    image_edge = swap(image_edge_own)
    rhs, image, image_sums = call(image_kernel, "image", (full, full, part), 2**30)(
        local, edge, sums, touch, back, from_iface, diag, coefs
    )
    resid, norms_own = call(resid_kernel, "resid", (full, small_row))(
        image_edge_own, image_edge, rhs, image, sums, image_sums, from_iface, edge_touch, diag, coefs
    )
    out = shape(*velocity.shape)
    return pl.pallas_call(
        last_kernel, out_shape=(out, out), compiler_params=params(), name="last"
    )(image_edge, image_edge_own, norms_own, swap(norms_own), resid, rhs)


def solution(mesh):
    field = P("runs", None, "mode", "mer")
    placed = (field, field, field, field, P(None, "mer"), P("mer"), P("mer"), P("mer"), P("mer", None))
    return jax.shard_map(
        per_device, mesh=mesh, in_specs=placed, out_specs=(field, field), check_vma=False
    )
```

```python
import functools
import math

import jax
import jax.numpy as jnp
import numpy as np
from jax import lax
from jax.experimental import pallas as pl
from jax.experimental.pallas import tpu as pltpu
from jax.sharding import PartitionSpec as P

step_size = 0.05
diffusion_ratio = 2.0
f32 = jnp.float32
bf16 = jnp.bfloat16
f8 = jnp.float8_e4m3fn
small, medium, large = 16 * 2**20, 54 * 2**20, 60 * 2**20


def params(limit=small):
    return pltpu.CompilerParams(vmem_limit_bytes=limit)


def halves(table):
    high = table.astype(np.float32).astype(jnp.bfloat16)
    low = (table - high.astype(np.float64)).astype(np.float32).astype(jnp.bfloat16)
    return high, low


def trig_tables(modes, per_dev):
    angles = 2 * modes
    order = np.arange(modes)
    points = np.arange(angles)
    phase = (points[:, None] * order[None, :] % angles) * (2.0 * math.pi / angles)
    both = np.stack([np.cos(phase), np.sin(phase)])
    both = both.reshape(2, angles, modes // per_dev, per_dev)
    factor = np.where(order == 0, 1.0, 2.0).reshape(modes // per_dev, per_dev) / angles
    same = np.eye(2)
    synthesis = np.einsum("pq,sajk->pajqsk", same, both).reshape(2 * angles, -1)
    analysis = np.einsum("pq,sajk,jk->jqskpa", same, both, factor * step_size).reshape(-1, 2 * angles)
    out = []
    for table in (synthesis, analysis):
        high, low = halves(table)
        out.append(jnp.asarray(np.concatenate([high, high, low], axis=1)))
    return out


def pieces(array, count):
    parts = []
    rest = array
    for i in range(count):
        part = rest.astype(bf16).astype(f32)
        parts.append(part)
        rest = rest - part
    return jnp.concatenate(parts, axis=0).astype(bf16)


def product(array, exact, count=2):
    rows = array.shape[0]
    out = jnp.dot(pieces(array, count), exact[...], preferred_element_type=f32)
    total = out[:rows]
    for i in range(1, count):
        total = total + out[i * rows : (i + 1) * rows]
    return total


def table_product(table, values):
    high = values.astype(bf16)
    low = (values - high.astype(f32)).astype(bf16)
    return jnp.dot(table, jnp.concatenate([high, low, high], axis=0), preferred_element_type=f32)


def start_all(sources, targets, sems):
    copies = [
        pltpu.make_async_copy(source, target, sems.at[i])
        for i, (source, target) in enumerate(zip(sources, targets))
    ]
    for copy in copies:
        copy.start()
    return copies


def pack_kernel(vel, mag, vort, cur, out, held, ready, in_sems, out_sems):
    blocks, rows, block = out.shape
    copies = start_all((vel, mag, vort, cur), [held.at[i] for i in range(4)], in_sems)
    sent = []
    row = 0
    for i in range(4):
        copies[i].wait()
        field = held.at[i]
        comps, _, per_dev, _ = field.shape
        for c in range(comps):
            for s in range(2):
                piece = field[c, s]
                for b in range(blocks):
                    ready[b, row : row + per_dev, :] = piece[:, b * block : (b + 1) * block]
                row += per_dev
        if i % 2:
            half = pl.ds(i // 2 * (rows // 2), rows // 2)
            sent.append(pltpu.make_async_copy(ready.at[:, half, :], out.at[:, half, :], out_sems.at[i // 2]))
            sent[-1].start()
    for copy in sent:
        copy.wait()


def nonlinear_kernel(fields, synthesis, analysis, out):
    owners, rows, block = fields.shape
    pair = rows // 6
    angles = synthesis.shape[0] // 2
    phys = []
    for t in range(6):
        coef = jnp.concatenate([fields[j, t * pair : (t + 1) * pair, :] for j in range(owners)], axis=0)
        values = table_product(synthesis[...], coef)
        phys += [values[:angles], values[angles:]]
    vel, mag, vort, cur = phys[0:3], phys[3:6], phys[6:9], phys[9:12]

    def cross(a, b, i):
        j, k = (i + 1) % 3, (i + 2) % 3
        return a[j] * b[k] - a[k] * b[j]

    terms = [cross(vel, vort, i) + cross(cur, mag, i) for i in range(3)]
    terms += [cross(vel, mag, i) for i in range(3)]
    for t in range(3):
        coef = table_product(analysis[...], jnp.concatenate([terms[2 * t], terms[2 * t + 1]], axis=0))
        for j in range(owners):
            span = slice(t * pair, (t + 1) * pair)
            out[j, span, :] = fields[j, span, :] + coef[j * pair : (j + 1) * pair]


def mesh_kernel(nodes_hbm, mass_hbm, radial_hbm, stiff_hbm, iface_hbm, touch_out, back_out, at_iface, from_iface, diag, coefs, edge_touch, edge_back, edge_diag, gram, touch, back, elem_nodes, mass, radial, stiff, iface, in_sems, out_sems):
    loads = start_all(
        (nodes_hbm, mass_hbm, radial_hbm, stiff_hbm, iface_hbm), (elem_nodes, mass, radial, stiff, iface), in_sems
    )
    for load in loads:
        load.wait()
    nodes, elems = touch.shape
    shared = iface.shape[1]
    fields = 8
    words = nodes // fields
    width = math.gcd(elems, 256)
    sent = []
    for c in range(elems // width):
        span = slice(c * width, (c + 1) * width)
        word = lax.broadcasted_iota(jnp.int32, (words, width), 0)
        total = jnp.zeros((words, width), jnp.int32)
        for i in range(elem_nodes.shape[0]):
            ids = elem_nodes[i : i + 1, span]
            field = ids // words
            value = jnp.left_shift(1, field * 4)
            total = total + jnp.where(ids - field * words == word, value, 0)
        for q in range(fields):
            count = jnp.right_shift(total, 4 * q) & 15
            touch[q * words : (q + 1) * words, span] = count.astype(f32).astype(bf16)
        column = pl.ds(c * width, width)
        sent.append(pltpu.make_async_copy(touch.at[:, column], touch_out.at[:, column], out_sems.at[c]))
        sent[-1].start()
        back[span, :] = touch[:, span].T
        sent.append(pltpu.make_async_copy(back.at[column, :], back_out.at[column, :], out_sems.at[elems // width + c]))
        sent[-1].start()
    node = lax.broadcasted_iota(jnp.int32, (nodes, shared), 0)
    hit = jnp.where(iface[...] == node, 1.0, 0.0)
    at_iface[...] = hit.astype(bf16)
    from_iface[...] = hit.T.astype(bf16)
    zero = jnp.zeros((5, elems), f32)
    coefs[...] = jnp.concatenate([mass[...] / 12.0, radial[...] / 12.0, stiff[...], zero], axis=0)
    scaled = jnp.concatenate([mass[...] / 12.0, radial[...] / 12.0, 6.0 * stiff[...], zero], axis=0)
    sums = product(scaled, back, 3)
    hits = jnp.dot(jnp.ones((16, shared), bf16), from_iface[...], preferred_element_type=f32)
    row = lax.broadcasted_iota(jnp.int32, (8, nodes), 0)
    diag[...] = jnp.where(row == 3, 1.0 - 0.5 * hits[:8], sums)
    edge_diag[...] = product(sums, at_iface, 3)
    counts = jnp.dot(from_iface[...], touch[...], preferred_element_type=f32)
    edge_touch[...] = counts.astype(bf16)
    edge_back[...] = counts.T.astype(bf16)
    short = touch[...].astype(f32).astype(f8)
    for c in range(elems // width):
        span = slice(c * width, (c + 1) * width)
        left = back[span, :].astype(f32).astype(f8)
        counts = jnp.dot(left, short[:, c * width :], preferred_element_type=f32)
        gram[span, c * width :] = counts.astype(bf16)
        for d in range(c + 1, elems // width):
            block = counts[:, (d - c) * width : (d - c + 1) * width]
            gram[d * width : (d + 1) * width, span] = block.T.astype(bf16)
    for copy in sent:
        copy.wait()


def row_factors(rows, per_dev, modes):
    row = lax.broadcasted_iota(jnp.int32, (rows, 1), 0)
    order = (lax.axis_index("mode") * per_dev + row % per_dev).astype(f32)
    shift = (order / modes) ** 2
    scale = jnp.where(row < rows // 2, 1.0, diffusion_ratio).astype(f32)
    return shift, scale


def at_elems(factors, coefs):
    shift, scale = factors
    return coefs[0:1, :] + shift * coefs[1:2, :] - scale * coefs[2:3, :]


def at_nodes(factors, diag):
    shift, scale = factors
    return diag[0:1, :] + shift * diag[1:2, :] + scale * diag[2:3, :]


def row_sum(array):
    return jnp.sum(array, axis=1, keepdims=True)


def lanes(*columns):
    rows = columns[0].shape[0]
    lane = lax.broadcasted_iota(jnp.int32, (rows, 128), 1)
    out = jnp.broadcast_to(columns[-1], (rows, 128))
    for i in reversed(range(len(columns) - 1)):
        out = jnp.where(lane == i, columns[i], out)
    return out


def together(forcing):
    return jnp.concatenate([forcing[b] for b in range(forcing.shape[0])], axis=1)


def rhs_edge_kernel(forcing, touch, at_iface, edge_back, edge_diag, coefs, spread_out, edge):
    given = together(forcing)
    spread = product(given, touch) * coefs[0:1, :]
    spread_out[...] = spread
    edge[...] = edge_diag[0:1, :] * product(given, at_iface, 3) + product(spread, edge_back, 3)


def rhs_kernel(per_dev, modes, forcing, spread, touch, back, diag, local, sums, scaled_sums, inner):
    rows = spread.shape[0]
    image = diag[0:1, :] * together(forcing) + product(spread[...], back)
    local[...] = image
    scaled = at_nodes(row_factors(rows, per_dev, modes), diag) * image
    both = product(jnp.concatenate([image, scaled], axis=0), touch)
    sums[...] = both[:rows]
    scaled_sums[...] = both[rows:]
    own = 2.0 * diag[3:4, :] - 1.0
    inner[...] = lanes(row_sum(own * image * image), row_sum(own * image * scaled))


def image_edge_kernel(per_dev, modes, edge_own, edge, sums, inner, edge_touch, edge_back, edge_diag, coefs, sums_out, out):
    rows, shared = edge.shape
    factors = row_factors(rows, per_dev, modes)
    rhs = edge_own[...] + edge[...]
    full = sums[...] + product(edge[...], edge_touch, 3)
    sums_out[...] = full
    spread = at_elems(factors, coefs) * full
    image = at_nodes(factors, edge_diag) * rhs
    norm = inner[:, 0:1] + 0.5 * row_sum(rhs * rhs)
    curvature = inner[:, 1:2] + row_sum(image * rhs) + row_sum(spread * full)
    out[:, :shared] = image + product(spread, edge_back, 3)
    out[:, shared:] = lanes(norm, curvature)


def image_kernel(per_dev, modes, local, edge, sums, scaled_sums, back, from_iface, edge_touch, edge_diag, gram, diag, coefs, rhs_out, image_out, sums_out):
    factors = row_factors(local.shape[0], per_dev, modes)
    rhs = local[...] + product(edge[...], from_iface, 3)
    rhs_out[...] = rhs
    spread = at_elems(factors, coefs) * sums[...]
    image_out[...] = at_nodes(factors, diag) * rhs + product(spread, back)
    arrived = product(at_nodes(factors, edge_diag) * edge[...], edge_touch, 3)
    sums_out[...] = scaled_sums[...] + arrived + product(spread, gram)


def resid_kernel(per_dev, modes, own, edge, rhs, image, sums, image_sums, from_iface, edge_touch, diag, coefs, resid_out, norms_out):
    rows = rhs.shape[0]
    shared = edge.shape[1] - 128
    factors = row_factors(rows, per_dev, modes)
    per_elem, per_node = at_elems(factors, coefs), at_nodes(factors, diag)
    norm = own[:, shared : shared + 1] + edge[:, shared : shared + 1]
    curvature = own[:, shared + 1 : shared + 2] + edge[:, shared + 1 : shared + 2]
    alpha = norm / curvature
    given = edge[:, :shared]
    resid = rhs[...] - alpha * (image[...] + product(given, from_iface, 3))
    resid_out[...] = resid
    new = sums[...] - alpha * (image_sums[...] + product(given, edge_touch, 3))
    after = row_sum(diag[3:4, :] * resid * resid)
    square = row_sum(per_node * resid * resid) + row_sum(per_elem * new * new)
    mixed = row_sum(per_node * resid * rhs[...]) + row_sum(per_elem * new * sums[...])
    norms_out[...] = lanes(after, square, mixed)


def last_kernel(edge, own, norms_own, norms, resid, rhs, vel_out, mag_out):
    shared = edge.shape[1] - 128
    norm = own[:, shared : shared + 1] + edge[:, shared : shared + 1]
    curvature = own[:, shared + 1 : shared + 2] + edge[:, shared + 1 : shared + 2]
    alpha = norm / curvature
    after = norms_own[:, 0:1] + norms[:, 0:1]
    square = norms_own[:, 1:2] + norms[:, 1:2]
    mixed = norms_own[:, 2:3] + norms[:, 2:3]
    beta = after / norm
    alpha_next = after / (square + 2.0 * beta * mixed + beta * beta * curvature)
    answer = (alpha + alpha_next * beta) * rhs[...] + alpha_next * resid[...]
    row = 0
    for out in (vel_out, mag_out):
        comps, _, per_dev, _ = out.shape
        for c in range(comps):
            for s in range(2):
                out[c, s] = answer[row : row + per_dev]
                row += per_dev


def per_device(velocity, vorticity, magnetic, current, elem_nodes, mass_coef, stiff_coef, radial_coef, iface):
    comps, _, per_dev, nodes = velocity.shape
    owners = lax.axis_size("mode")
    modes = per_dev * owners
    block = nodes // owners
    rows = 4 * comps * per_dev
    elems = elem_nodes.shape[1]
    shared = iface.shape[1]
    mass, radial, stiff = (a.reshape(1, elems) for a in (mass_coef, radial_coef, stiff_coef))
    synthesis, analysis = trig_tables(modes, per_dev)

    def shape(*dims, kind=f32):
        return jax.ShapeDtypeStruct(dims, kind)

    in_hbm = pl.BlockSpec(memory_space=pltpu.HBM)
    if block % 128 == 0:
        packed = pl.pallas_call(
            pack_kernel,
            in_specs=[in_hbm] * 4,
            out_shape=shape(owners, 2 * rows, block),
            out_specs=in_hbm,
            scratch_shapes=[
                pltpu.VMEM((4, *velocity.shape), f32),
                pltpu.VMEM((owners, 2 * rows, block), f32),
                pltpu.SemaphoreType.DMA((4,)),
                pltpu.SemaphoreType.DMA((2,)),
            ],
            compiler_params=params(large),
            name="pack",
        )(velocity, magnetic, vorticity, current)
    else:
        packed = jnp.concatenate(
            [a.reshape(rows // 2, owners, block) for a in (velocity, magnetic, vorticity, current)], axis=0
        ).transpose(1, 0, 2)
    columns = lax.all_to_all(packed, "mode", 0, 0, tiled=True)
    tables = (
        shape(nodes, elems, kind=bf16),
        shape(elems, nodes, kind=bf16),
        shape(nodes, shared, kind=bf16),
        shape(shared, nodes, kind=bf16),
        shape(8, nodes),
        shape(8, elems),
        shape(shared, elems, kind=bf16),
        shape(elems, shared, kind=bf16),
        shape(8, shared),
        shape(elems, elems, kind=bf16),
    )
    in_vmem = pl.BlockSpec(memory_space=pltpu.VMEM)
    built = pl.pallas_call(
        mesh_kernel,
        in_specs=[in_hbm] * 5,
        out_specs=(in_hbm, in_hbm, *[in_vmem] * 8),
        out_shape=tables,
        scratch_shapes=[
            pltpu.VMEM((nodes, elems), bf16),
            pltpu.VMEM((elems, nodes), bf16),
            pltpu.VMEM(elem_nodes.shape, jnp.int32),
            pltpu.VMEM((1, elems), f32),
            pltpu.VMEM((1, elems), f32),
            pltpu.VMEM((1, elems), f32),
            pltpu.VMEM(iface.shape, jnp.int32),
            pltpu.SemaphoreType.DMA((5,)),
            pltpu.SemaphoreType.DMA((2 * elems // math.gcd(elems, 256),)),
        ],
        compiler_params=params(large),
        name="incidence",
        cost_estimate=pl.CostEstimate(flops=2**31, bytes_accessed=2**23, transcendentals=0),
    )(elem_nodes, mass, radial, stiff, iface)
    columns, *built = lax.optimization_barrier((columns, *built))
    touch, back, at_iface, from_iface, diag, coefs, edge_touch, edge_back, edge_diag, gram = built
    terms = pl.pallas_call(
        nonlinear_kernel,
        out_shape=pltpu.VMEM((owners, rows, block), f32),
        compiler_params=params(),
        name="nonlinear",
        cost_estimate=pl.CostEstimate(flops=2**33, bytes_accessed=2**24, transcendentals=0),
    )(pltpu.with_memory_space_constraint(columns, pltpu.VMEM), synthesis, analysis)
    forcing = lax.all_to_all(terms, "mode", 0, 0, tiled=True)
    if block % 128:
        forcing = forcing.transpose(1, 0, 2).reshape(1, rows, nodes)

    def swap(array):
        return lax.ppermute(array, "mer", [(0, 1), (1, 0)])

    def call(kernel, name, outs, work=0):
        own = () if kernel is rhs_edge_kernel else (per_dev, modes)
        cost = pl.CostEstimate(flops=work, bytes_accessed=work // 512, transcendentals=0) if work else None
        return pl.pallas_call(
            functools.partial(kernel, *own),
            out_shape=tuple(outs),
            compiler_params=params(),
            name=name,
            cost_estimate=cost,
        )

    full, part, small_row = shape(rows, nodes), shape(rows, elems), shape(rows, 128)
    spread, edge_own = call(rhs_edge_kernel, "rhs_edge", (part, shape(rows, shared)))(
        forcing, touch, at_iface, edge_back, edge_diag, coefs
    )
    edge = swap(edge_own)
    local, sums, scaled_sums, inner = call(rhs_kernel, "rhs", (full, part, part, small_row), 2**30)(
        forcing, spread, touch, back, diag
    )
    sums, image_edge_own = call(image_edge_kernel, "image_edge", (part, shape(rows, shared + 128)))(
        edge_own, edge, sums, inner, edge_touch, edge_back, edge_diag, coefs
    )
    image_edge = swap(image_edge_own)
    rhs, image, image_sums = call(image_kernel, "image", (full, full, part), 2**30)(
        local, edge, sums, scaled_sums, back, from_iface, edge_touch, edge_diag, gram, diag, coefs
    )
    resid, norms_own = call(resid_kernel, "resid", (full, small_row))(
        image_edge_own, image_edge, rhs, image, sums, image_sums, from_iface, edge_touch, diag, coefs
    )
    out = shape(*velocity.shape)
    return pl.pallas_call(
        last_kernel, out_shape=(out, out), compiler_params=params(), name="last"
    )(image_edge, image_edge_own, norms_own, swap(norms_own), resid, rhs)


def solution(mesh):
    field = P("runs", None, "mode", "mer")
    placed = (field, field, field, field, P(None, "mer"), P("mer"), P("mer"), P("mer"), P("mer", None))
    return jax.shard_map(
        per_device, mesh=mesh, in_specs=placed, out_specs=(field, field), check_vma=False
    )
```

```python
import functools
import math

import jax
import jax.numpy as jnp
import numpy as np
from jax import lax
from jax.experimental import pallas as pl
from jax.experimental.pallas import tpu as pltpu
from jax.sharding import PartitionSpec as P

step_size = 0.05
diffusion_ratio = 2.0
f32 = jnp.float32
bf16 = jnp.bfloat16
f8 = jnp.float8_e4m3fn
small, medium, large = 16 * 2**20, 54 * 2**20, 60 * 2**20


def params(limit=small):
    return pltpu.CompilerParams(vmem_limit_bytes=limit)


def halves(table):
    high = table.astype(np.float32).astype(jnp.bfloat16)
    low = (table - high.astype(np.float64)).astype(np.float32).astype(jnp.bfloat16)
    return high, low


def trig_tables(modes, per_dev):
    angles = 2 * modes
    order = np.arange(modes)
    points = np.arange(angles)
    phase = (points[:, None] * order[None, :] % angles) * (2.0 * math.pi / angles)
    both = np.stack([np.cos(phase), np.sin(phase)])
    both = both.reshape(2, angles, modes // per_dev, per_dev)
    factor = np.where(order == 0, 1.0, 2.0).reshape(modes // per_dev, per_dev) / angles
    same = np.eye(2)
    synthesis = np.einsum("pq,sajk->pajqsk", same, both).reshape(2 * angles, -1)
    analysis = np.einsum("pq,sajk,jk->jqskpa", same, both, factor * step_size).reshape(-1, 2 * angles)
    out = []
    for table in (synthesis, analysis):
        high, low = halves(table)
        out.append(jnp.asarray(np.concatenate([high, high, low], axis=1)))
    return out


def product(array, exact, count=5):
    rows = array.shape[0]
    top = jnp.maximum(jnp.max(jnp.abs(array), axis=1, keepdims=True), 1e-30)
    parts = []
    rest = array * (200.0 / top)
    for _ in range(count):
        part = rest.astype(f8).astype(f32)
        parts.append(part)
        rest = (rest - part) * 16.0
    out = jnp.dot(jnp.concatenate(parts, axis=0).astype(f8), exact[...], preferred_element_type=f32)
    total = out[(count - 1) * rows :]
    for i in reversed(range(count - 1)):
        total = total * (1.0 / 16.0) + out[i * rows : (i + 1) * rows]
    return total * (top / 200.0)


def table_product(table, values):
    high = values.astype(bf16)
    low = (values - high.astype(f32)).astype(bf16)
    return jnp.dot(table, jnp.concatenate([high, low, high], axis=0), preferred_element_type=f32)


def start_all(sources, targets, sems):
    copies = [
        pltpu.make_async_copy(source, target, sems.at[i])
        for i, (source, target) in enumerate(zip(sources, targets))
    ]
    for copy in copies:
        copy.start()
    return copies


def pack_kernel(vel, mag, vort, cur, out, held, ready, in_sems, out_sems):
    blocks, rows, block = out.shape
    copies = start_all((vel, mag, vort, cur), [held.at[i] for i in range(4)], in_sems)
    sent = []
    row = 0
    for i in range(4):
        copies[i].wait()
        field = held.at[i]
        comps, _, per_dev, _ = field.shape
        for c in range(comps):
            for s in range(2):
                piece = field[c, s]
                for b in range(blocks):
                    ready[b, row : row + per_dev, :] = piece[:, b * block : (b + 1) * block]
                row += per_dev
        if i % 2:
            half = pl.ds(i // 2 * (rows // 2), rows // 2)
            sent.append(pltpu.make_async_copy(ready.at[:, half, :], out.at[:, half, :], out_sems.at[i // 2]))
            sent[-1].start()
    for copy in sent:
        copy.wait()


def nonlinear_kernel(fields, synthesis, analysis, out):
    owners, rows, block = fields.shape
    pair = rows // 6
    angles = synthesis.shape[0] // 2
    phys = []
    for t in range(6):
        coef = jnp.concatenate([fields[j, t * pair : (t + 1) * pair, :] for j in range(owners)], axis=0)
        values = table_product(synthesis[...], coef)
        phys += [values[:angles], values[angles:]]
    vel, mag, vort, cur = phys[0:3], phys[3:6], phys[6:9], phys[9:12]

    def cross(a, b, i):
        j, k = (i + 1) % 3, (i + 2) % 3
        return a[j] * b[k] - a[k] * b[j]

    terms = [cross(vel, vort, i) + cross(cur, mag, i) for i in range(3)]
    terms += [cross(vel, mag, i) for i in range(3)]
    for t in range(3):
        coef = table_product(analysis[...], jnp.concatenate([terms[2 * t], terms[2 * t + 1]], axis=0))
        for j in range(owners):
            span = slice(t * pair, (t + 1) * pair)
            out[j, span, :] = fields[j, span, :] + coef[j * pair : (j + 1) * pair]


def mesh_kernel(nodes_hbm, mass_hbm, radial_hbm, stiff_hbm, iface_hbm, touch_out, back_out, at_iface, from_iface, diag, coefs, edge_touch, edge_back, edge_diag, touch, back, elem_nodes, mass, radial, stiff, iface, in_sems, out_sems):
    loads = start_all(
        (nodes_hbm, mass_hbm, radial_hbm, stiff_hbm, iface_hbm), (elem_nodes, mass, radial, stiff, iface), in_sems
    )
    for load in loads:
        load.wait()
    nodes, elems = touch.shape
    shared = iface.shape[1]
    fields = 8
    words = nodes // fields
    width = math.gcd(elems, 256)
    sent = []
    for c in range(elems // width):
        span = slice(c * width, (c + 1) * width)
        word = lax.broadcasted_iota(jnp.int32, (words, width), 0)
        total = jnp.zeros((words, width), jnp.int32)
        for i in range(elem_nodes.shape[0]):
            ids = elem_nodes[i : i + 1, span]
            field = ids // words
            value = jnp.left_shift(1, field * 4)
            total = total + jnp.where(ids - field * words == word, value, 0)
        for q in range(fields):
            count = (jnp.right_shift(total, 4 * q) & 15).astype(f32)
            touch[q * words : (q + 1) * words, span] = count.astype(f8)
            back[span, q * words : (q + 1) * words] = count.T.astype(f8)
        column = pl.ds(c * width, width)
        sent.append(pltpu.make_async_copy(touch.at[:, column], touch_out.at[:, column], out_sems.at[c]))
        sent[-1].start()
        sent.append(pltpu.make_async_copy(back.at[column, :], back_out.at[column, :], out_sems.at[elems // width + c]))
        sent[-1].start()
    node = lax.broadcasted_iota(jnp.int32, (nodes, shared), 0)
    hit = jnp.where(iface[...] == node, 1.0, 0.0)
    at_iface[...] = hit.astype(f8)
    from_iface[...] = hit.T.astype(f8)
    zero = jnp.zeros((5, elems), f32)
    coefs[...] = jnp.concatenate([mass[...] / 12.0, radial[...] / 12.0, stiff[...], zero], axis=0)
    scaled = jnp.concatenate([mass[...] / 12.0, radial[...] / 12.0, 6.0 * stiff[...], zero], axis=0)
    sums = product(scaled, back)
    hits = jnp.dot(jnp.ones((32, shared), f8), from_iface[...], preferred_element_type=f32)
    row = lax.broadcasted_iota(jnp.int32, (8, nodes), 0)
    diag[...] = jnp.where(row == 3, 1.0 - 0.5 * hits[:8], sums)
    edge_diag[...] = product(sums, at_iface)
    counts = jnp.dot(from_iface[...], touch[...], preferred_element_type=f32)
    edge_touch[...] = counts.astype(f8)
    edge_back[...] = counts.T.astype(f8)
    for copy in sent:
        copy.wait()


def row_factors(rows, per_dev, modes):
    row = lax.broadcasted_iota(jnp.int32, (rows, 1), 0)
    order = (lax.axis_index("mode") * per_dev + row % per_dev).astype(f32)
    shift = (order / modes) ** 2
    scale = jnp.where(row < rows // 2, 1.0, diffusion_ratio).astype(f32)
    return shift, scale


def at_elems(factors, coefs):
    shift, scale = factors
    return coefs[0:1, :] + shift * coefs[1:2, :] - scale * coefs[2:3, :]


def at_nodes(factors, diag):
    shift, scale = factors
    return diag[0:1, :] + shift * diag[1:2, :] + scale * diag[2:3, :]


def row_sum(array):
    return jnp.sum(array, axis=1, keepdims=True)


def lanes(*columns):
    rows = columns[0].shape[0]
    lane = lax.broadcasted_iota(jnp.int32, (rows, 128), 1)
    out = jnp.broadcast_to(columns[-1], (rows, 128))
    for i in reversed(range(len(columns) - 1)):
        out = jnp.where(lane == i, columns[i], out)
    return out


def together(forcing):
    return jnp.concatenate([forcing[b] for b in range(forcing.shape[0])], axis=1)


def rhs_edge_kernel(forcing, touch, at_iface, edge_back, edge_diag, coefs, spread_out, edge):
    given = together(forcing)
    spread = product(given, touch) * coefs[0:1, :]
    spread_out[...] = spread
    edge[...] = edge_diag[0:1, :] * product(given, at_iface) + product(spread, edge_back)


def rhs_kernel(per_dev, modes, forcing, spread, touch, back, diag, local, sums, inner):
    rows = spread.shape[0]
    image = diag[0:1, :] * together(forcing) + product(spread[...], back)
    local[...] = image
    sums[...] = product(image, touch)
    square = (2.0 * diag[3:4, :] - 1.0) * image * image
    inner[...] = lanes(row_sum(square), row_sum(at_nodes(row_factors(rows, per_dev, modes), diag) * square))


def image_edge_kernel(per_dev, modes, edge_own, edge, sums, inner, edge_touch, edge_back, edge_diag, coefs, sums_out, out):
    rows, shared = edge.shape
    factors = row_factors(rows, per_dev, modes)
    rhs = edge_own[...] + edge[...]
    full = sums[...] + product(edge[...], edge_touch)
    sums_out[...] = full
    spread = at_elems(factors, coefs) * full
    image = at_nodes(factors, edge_diag) * rhs
    norm = inner[:, 0:1] + 0.5 * row_sum(rhs * rhs)
    curvature = inner[:, 1:2] + row_sum(image * rhs) + row_sum(spread * full)
    out[:, :shared] = image + product(spread, edge_back)
    out[:, shared:] = lanes(norm, curvature)


def image_kernel(per_dev, modes, local, edge, sums, touch, back, from_iface, diag, coefs, rhs_out, image_out, sums_out):
    factors = row_factors(local.shape[0], per_dev, modes)
    rhs = local[...] + product(edge[...], from_iface)
    rhs_out[...] = rhs
    image = at_nodes(factors, diag) * rhs + product(at_elems(factors, coefs) * sums[...], back)
    image_out[...] = image
    sums_out[...] = product(image, touch)


def resid_kernel(per_dev, modes, own, edge, rhs, image, sums, image_sums, from_iface, edge_touch, diag, coefs, resid_out, norms_out):
    rows = rhs.shape[0]
    shared = edge.shape[1] - 128
    factors = row_factors(rows, per_dev, modes)
    per_elem, per_node = at_elems(factors, coefs), at_nodes(factors, diag)
    norm = own[:, shared : shared + 1] + edge[:, shared : shared + 1]
    curvature = own[:, shared + 1 : shared + 2] + edge[:, shared + 1 : shared + 2]
    alpha = norm / curvature
    given = edge[:, :shared]
    resid = rhs[...] - alpha * (image[...] + product(given, from_iface))
    resid_out[...] = resid
    new = sums[...] - alpha * (image_sums[...] + product(given, edge_touch))
    after = row_sum(diag[3:4, :] * resid * resid)
    square = row_sum(per_node * resid * resid) + row_sum(per_elem * new * new)
    mixed = row_sum(per_node * resid * rhs[...]) + row_sum(per_elem * new * sums[...])
    norms_out[...] = lanes(after, square, mixed)


def last_kernel(edge, own, norms_own, norms, resid, rhs, vel_out, mag_out):
    shared = edge.shape[1] - 128
    norm = own[:, shared : shared + 1] + edge[:, shared : shared + 1]
    curvature = own[:, shared + 1 : shared + 2] + edge[:, shared + 1 : shared + 2]
    alpha = norm / curvature
    after = norms_own[:, 0:1] + norms[:, 0:1]
    square = norms_own[:, 1:2] + norms[:, 1:2]
    mixed = norms_own[:, 2:3] + norms[:, 2:3]
    beta = after / norm
    alpha_next = after / (square + 2.0 * beta * mixed + beta * beta * curvature)
    answer = (alpha + alpha_next * beta) * rhs[...] + alpha_next * resid[...]
    row = 0
    for out in (vel_out, mag_out):
        comps, _, per_dev, _ = out.shape
        for c in range(comps):
            for s in range(2):
                out[c, s] = answer[row : row + per_dev]
                row += per_dev


def per_device(velocity, vorticity, magnetic, current, elem_nodes, mass_coef, stiff_coef, radial_coef, iface):
    comps, _, per_dev, nodes = velocity.shape
    owners = lax.axis_size("mode")
    modes = per_dev * owners
    block = nodes // owners
    rows = 4 * comps * per_dev
    elems = elem_nodes.shape[1]
    shared = iface.shape[1]
    mass, radial, stiff = (a.reshape(1, elems) for a in (mass_coef, radial_coef, stiff_coef))
    synthesis, analysis = trig_tables(modes, per_dev)

    def shape(*dims, kind=f32):
        return jax.ShapeDtypeStruct(dims, kind)

    in_hbm = pl.BlockSpec(memory_space=pltpu.HBM)
    if block % 128 == 0:
        packed = pl.pallas_call(
            pack_kernel,
            in_specs=[in_hbm] * 4,
            out_shape=shape(owners, 2 * rows, block),
            out_specs=in_hbm,
            scratch_shapes=[
                pltpu.VMEM((4, *velocity.shape), f32),
                pltpu.VMEM((owners, 2 * rows, block), f32),
                pltpu.SemaphoreType.DMA((4,)),
                pltpu.SemaphoreType.DMA((2,)),
            ],
            compiler_params=params(large),
            name="pack",
        )(velocity, magnetic, vorticity, current)
    else:
        packed = jnp.concatenate(
            [a.reshape(rows // 2, owners, block) for a in (velocity, magnetic, vorticity, current)], axis=0
        ).transpose(1, 0, 2)
    columns = lax.all_to_all(packed, "mode", 0, 0, tiled=True)
    tables = (
        shape(nodes, elems, kind=f8),
        shape(elems, nodes, kind=f8),
        shape(nodes, shared, kind=f8),
        shape(shared, nodes, kind=f8),
        shape(8, nodes),
        shape(8, elems),
        shape(shared, elems, kind=f8),
        shape(elems, shared, kind=f8),
        shape(8, shared),
    )
    in_vmem = pl.BlockSpec(memory_space=pltpu.VMEM)
    built = pl.pallas_call(
        mesh_kernel,
        in_specs=[in_hbm] * 5,
        out_specs=(in_hbm, in_hbm, *[in_vmem] * 7),
        out_shape=tables,
        scratch_shapes=[
            pltpu.VMEM((nodes, elems), f8),
            pltpu.VMEM((elems, nodes), f8),
            pltpu.VMEM(elem_nodes.shape, jnp.int32),
            pltpu.VMEM((1, elems), f32),
            pltpu.VMEM((1, elems), f32),
            pltpu.VMEM((1, elems), f32),
            pltpu.VMEM(iface.shape, jnp.int32),
            pltpu.SemaphoreType.DMA((5,)),
            pltpu.SemaphoreType.DMA((2 * elems // math.gcd(elems, 256),)),
        ],
        compiler_params=params(large),
        name="incidence",
        cost_estimate=pl.CostEstimate(flops=2**31, bytes_accessed=2**23, transcendentals=0),
    )(elem_nodes, mass, radial, stiff, iface)
    columns, *built = lax.optimization_barrier((columns, *built))
    touch, back, at_iface, from_iface, diag, coefs, edge_touch, edge_back, edge_diag = built
    terms = pl.pallas_call(
        nonlinear_kernel,
        out_shape=pltpu.VMEM((owners, rows, block), f32),
        compiler_params=params(),
        name="nonlinear",
        cost_estimate=pl.CostEstimate(flops=2**33, bytes_accessed=2**24, transcendentals=0),
    )(pltpu.with_memory_space_constraint(columns, pltpu.VMEM), synthesis, analysis)
    forcing = lax.all_to_all(terms, "mode", 0, 0, tiled=True)
    if block % 128:
        forcing = forcing.transpose(1, 0, 2).reshape(1, rows, nodes)

    def swap(array):
        return lax.ppermute(array, "mer", [(0, 1), (1, 0)])

    def call(kernel, name, outs, work=0):
        own = () if kernel is rhs_edge_kernel else (per_dev, modes)
        cost = pl.CostEstimate(flops=work, bytes_accessed=work // 512, transcendentals=0) if work else None
        return pl.pallas_call(
            functools.partial(kernel, *own),
            out_shape=tuple(outs),
            compiler_params=params(),
            name=name,
            cost_estimate=cost,
        )

    full, part, small_row = shape(rows, nodes), shape(rows, elems), shape(rows, 128)
    spread, edge_own = call(rhs_edge_kernel, "rhs_edge", (part, shape(rows, shared)))(
        forcing, touch, at_iface, edge_back, edge_diag, coefs
    )
    edge = swap(edge_own)
    local, sums, inner = call(rhs_kernel, "rhs", (full, part, small_row), 2**30)(
        forcing, spread, touch, back, diag
    )
    sums, image_edge_own = call(image_edge_kernel, "image_edge", (part, shape(rows, shared + 128)))(
        edge_own, edge, sums, inner, edge_touch, edge_back, edge_diag, coefs
    )
    image_edge = swap(image_edge_own)
    rhs, image, image_sums = call(image_kernel, "image", (full, full, part), 2**30)(
        local, edge, sums, touch, back, from_iface, diag, coefs
    )
    resid, norms_own = call(resid_kernel, "resid", (full, small_row))(
        image_edge_own, image_edge, rhs, image, sums, image_sums, from_iface, edge_touch, diag, coefs
    )
    out = shape(*velocity.shape)
    return pl.pallas_call(
        last_kernel, out_shape=(out, out), compiler_params=params(), name="last"
    )(image_edge, image_edge_own, norms_own, swap(norms_own), resid, rhs)


def solution(mesh):
    field = P("runs", None, "mode", "mer")
    placed = (field, field, field, field, P(None, "mer"), P("mer"), P("mer"), P("mer"), P("mer", None))
    return jax.shard_map(
        per_device, mesh=mesh, in_specs=placed, out_specs=(field, field), check_vma=False
    )
```

```python
import functools
import math

import jax
import jax.numpy as jnp
import numpy as np
from jax import lax
from jax.experimental import pallas as pl
from jax.experimental.pallas import tpu as pltpu
from jax.sharding import PartitionSpec as P

step_size = 0.05
diffusion_ratio = 2.0
f32 = jnp.float32
bf16 = jnp.bfloat16
f8 = jnp.float8_e4m3fn
largest, radix, exact_below = 16.0, 32.0, 2048.0
small, medium, large = 16 * 2**20, 54 * 2**20, 60 * 2**20


def params(limit=small):
    return pltpu.CompilerParams(vmem_limit_bytes=limit)


def halves(table):
    high = table.astype(np.float32).astype(jnp.bfloat16)
    low = (table - high.astype(np.float64)).astype(np.float32).astype(jnp.bfloat16)
    return high, low


def trig_tables(modes, per_dev):
    angles = 2 * modes
    order = np.arange(modes)
    points = np.arange(angles)
    phase = (points[:, None] * order[None, :] % angles) * (2.0 * math.pi / angles)
    both = np.stack([np.cos(phase), np.sin(phase)])
    both = both.reshape(2, angles, modes // per_dev, per_dev)
    factor = np.where(order == 0, 1.0, 2.0).reshape(modes // per_dev, per_dev) / angles
    same = np.eye(2)
    synthesis = np.einsum("pq,sajk->pajqsk", same, both).reshape(2 * angles, -1)
    analysis = np.einsum("pq,sajk,jk->jqskpa", same, both, factor * step_size).reshape(-1, 2 * angles)
    out = []
    for table in (synthesis, analysis):
        high, low = halves(table)
        out.append(jnp.asarray(np.concatenate([high, high, low], axis=1)))
    return out


def pieces(array, count):
    parts = []
    rest = array
    for i in range(count):
        part = rest.astype(bf16).astype(f32)
        parts.append(part)
        rest = rest - part
    return jnp.concatenate(parts, axis=0).astype(bf16)


def product(array, exact, count=2):
    rows = array.shape[0]
    out = jnp.dot(pieces(array, count), exact[...], preferred_element_type=f32)
    total = out[:rows]
    for i in range(1, count):
        total = total + out[i * rows : (i + 1) * rows]
    return total


def short_product(array, exact, count=4):
    rows = array.shape[0]
    top = jnp.maximum(jnp.max(jnp.abs(array), axis=1, keepdims=True), 1e-30)
    parts = []
    rest = array * (largest / top)
    for _ in range(count):
        part = jnp.round(rest)
        parts.append(part)
        rest = (rest - part) * radix
    out = jnp.dot(jnp.concatenate(parts, axis=0).astype(f8), exact[...], preferred_element_type=f32)
    total = out[(count - 1) * rows :]
    for i in reversed(range(count - 1)):
        total = total * (1.0 / radix) + out[i * rows : (i + 1) * rows]
    return total * (top / largest)


def spread_into(target, values, back, diag, base):
    few = jnp.max(diag[4:5, :]) * largest <= exact_below

    @pl.when(few)
    def _():
        target[...] = base + short_product(values, back)

    @pl.when(jnp.logical_not(few))
    def _():
        target[...] = base + product(values, back[...].astype(f32).astype(bf16), 3)


def table_product(table, values):
    high = values.astype(bf16)
    low = (values - high.astype(f32)).astype(bf16)
    return jnp.dot(table, jnp.concatenate([high, low, high], axis=0), preferred_element_type=f32)


def start_all(sources, targets, sems):
    copies = [
        pltpu.make_async_copy(source, target, sems.at[i])
        for i, (source, target) in enumerate(zip(sources, targets))
    ]
    for copy in copies:
        copy.start()
    return copies


def pack_kernel(vel, mag, vort, cur, out, held, ready, in_sems, out_sems):
    blocks, rows, block = out.shape
    copies = start_all((vel, mag, vort, cur), [held.at[i] for i in range(4)], in_sems)
    sent = []
    row = 0
    for i in range(4):
        copies[i].wait()
        field = held.at[i]
        comps, _, per_dev, _ = field.shape
        for c in range(comps):
            for s in range(2):
                piece = field[c, s]
                for b in range(blocks):
                    ready[b, row : row + per_dev, :] = piece[:, b * block : (b + 1) * block]
                row += per_dev
        if i % 2:
            half = pl.ds(i // 2 * (rows // 2), rows // 2)
            sent.append(pltpu.make_async_copy(ready.at[:, half, :], out.at[:, half, :], out_sems.at[i // 2]))
            sent[-1].start()
    for copy in sent:
        copy.wait()


def nonlinear_kernel(fields, synthesis, analysis, out):
    owners, rows, block = fields.shape
    pair = rows // 6
    angles = synthesis.shape[0] // 2
    phys = []
    for t in range(6):
        coef = jnp.concatenate([fields[j, t * pair : (t + 1) * pair, :] for j in range(owners)], axis=0)
        values = table_product(synthesis[...], coef)
        phys += [values[:angles], values[angles:]]
    vel, mag, vort, cur = phys[0:3], phys[3:6], phys[6:9], phys[9:12]

    def cross(a, b, i):
        j, k = (i + 1) % 3, (i + 2) % 3
        return a[j] * b[k] - a[k] * b[j]

    terms = [cross(vel, vort, i) + cross(cur, mag, i) for i in range(3)]
    terms += [cross(vel, mag, i) for i in range(3)]
    for t in range(3):
        coef = table_product(analysis[...], jnp.concatenate([terms[2 * t], terms[2 * t + 1]], axis=0))
        for j in range(owners):
            span = slice(t * pair, (t + 1) * pair)
            out[j, span, :] = fields[j, span, :] + coef[j * pair : (j + 1) * pair]


def mesh_kernel(nodes_hbm, mass_hbm, radial_hbm, stiff_hbm, iface_hbm, touch_out, back_out, at_iface, from_iface, diag, coefs, edge_touch, edge_back, edge_diag, touch, back, touch8, back8, elem_nodes, mass, radial, stiff, iface, in_sems, out_sems):
    loads = start_all(
        (nodes_hbm, mass_hbm, radial_hbm, stiff_hbm, iface_hbm), (elem_nodes, mass, radial, stiff, iface), in_sems
    )
    for load in loads:
        load.wait()
    nodes, elems = touch.shape
    shared = iface.shape[1]
    fields = 8
    words = nodes // fields
    width = math.gcd(elems, 256)
    sent = []
    for c in range(elems // width):
        span = slice(c * width, (c + 1) * width)
        word = lax.broadcasted_iota(jnp.int32, (words, width), 0)
        total = jnp.zeros((words, width), jnp.int32)
        for i in range(elem_nodes.shape[0]):
            ids = elem_nodes[i : i + 1, span]
            field = ids // words
            value = jnp.left_shift(1, field * 4)
            total = total + jnp.where(ids - field * words == word, value, 0)
        for q in range(fields):
            count = jnp.right_shift(total, 4 * q) & 15
            touch[q * words : (q + 1) * words, span] = count.astype(f32).astype(bf16)
        column = pl.ds(c * width, width)
        touch8[:, span] = touch[:, span].astype(f32).astype(f8)
        sent.append(pltpu.make_async_copy(touch8.at[:, column], touch_out.at[:, column], out_sems.at[c]))
        sent[-1].start()
        back[span, :] = touch[:, span].T
        back8[span, :] = back[span, :].astype(f32).astype(f8)
        sent.append(pltpu.make_async_copy(back8.at[column, :], back_out.at[column, :], out_sems.at[elems // width + c]))
        sent[-1].start()
    node = lax.broadcasted_iota(jnp.int32, (nodes, shared), 0)
    hit = jnp.where(iface[...] == node, 1.0, 0.0)
    at_iface[...] = hit.astype(bf16)
    last = pl.ds(elems, shared)
    touch8[:, elems:] = hit.astype(f8)
    sent.append(pltpu.make_async_copy(touch8.at[:, last], touch_out.at[:, last], out_sems.at[2 * elems // width]))
    sent[-1].start()
    from_iface[...] = hit.T.astype(bf16)
    zero = jnp.zeros((5, elems), f32)
    one = jnp.ones((1, elems), f32)
    coefs[...] = jnp.concatenate([mass[...] / 12.0, radial[...] / 12.0, stiff[...], zero], axis=0)
    scaled = jnp.concatenate([mass[...] / 12.0, radial[...] / 12.0, 6.0 * stiff[...], one * 0.0, one, zero[:3]], axis=0)
    sums = product(scaled, back, 3)
    hits = jnp.dot(jnp.ones((16, shared), bf16), from_iface[...], preferred_element_type=f32)
    row = lax.broadcasted_iota(jnp.int32, (8, nodes), 0)
    diag[...] = jnp.where(row == 3, 1.0 - 0.5 * hits[:8], sums)
    edge_diag[...] = product(sums, at_iface, 3)
    counts = jnp.dot(from_iface[...], touch[...], preferred_element_type=f32)
    edge_touch[...] = counts.astype(bf16)
    edge_back[...] = counts.T.astype(bf16)
    for copy in sent:
        copy.wait()


def row_factors(rows, per_dev, modes):
    row = lax.broadcasted_iota(jnp.int32, (rows, 1), 0)
    order = (lax.axis_index("mode") * per_dev + row % per_dev).astype(f32)
    shift = (order / modes) ** 2
    scale = jnp.where(row < rows // 2, 1.0, diffusion_ratio).astype(f32)
    return shift, scale


def at_elems(factors, coefs):
    shift, scale = factors
    return coefs[0:1, :] + shift * coefs[1:2, :] - scale * coefs[2:3, :]


def at_nodes(factors, diag):
    shift, scale = factors
    return diag[0:1, :] + shift * diag[1:2, :] + scale * diag[2:3, :]


def row_sum(array):
    return jnp.sum(array, axis=1, keepdims=True)


def lanes(*columns):
    rows = columns[0].shape[0]
    lane = lax.broadcasted_iota(jnp.int32, (rows, 128), 1)
    out = jnp.broadcast_to(columns[-1], (rows, 128))
    for i in reversed(range(len(columns) - 1)):
        out = jnp.where(lane == i, columns[i], out)
    return out


def together(forcing):
    return jnp.concatenate([forcing[b] for b in range(forcing.shape[0])], axis=1)


def rhs_edge_kernel(forcing, touch, edge_back, edge_diag, coefs, spread_out, edge):
    elems = coefs.shape[1]
    sums = short_product(together(forcing), touch)
    spread = sums[:, :elems] * coefs[0:1, :]
    spread_out[...] = spread
    edge[...] = edge_diag[0:1, :] * sums[:, elems:] + product(spread, edge_back, 3)


def rhs_kernel(per_dev, modes, forcing, spread, touch, back, diag, local, sums, inner):
    rows = spread.shape[0]
    spread_into(local, spread[...], back, diag, diag[0:1, :] * together(forcing))
    image = local[...]
    sums[...] = short_product(image, touch.at[:, : spread.shape[1]])
    square = (2.0 * diag[3:4, :] - 1.0) * image * image
    inner[...] = lanes(row_sum(square), row_sum(at_nodes(row_factors(rows, per_dev, modes), diag) * square))


def image_edge_kernel(per_dev, modes, edge_own, edge, sums, inner, edge_touch, edge_back, edge_diag, coefs, sums_out, out):
    rows, shared = edge.shape
    factors = row_factors(rows, per_dev, modes)
    rhs = edge_own[...] + edge[...]
    full = sums[...] + product(edge[...], edge_touch, 3)
    sums_out[...] = full
    spread = at_elems(factors, coefs) * full
    image = at_nodes(factors, edge_diag) * rhs
    norm = inner[:, 0:1] + 0.5 * row_sum(rhs * rhs)
    curvature = inner[:, 1:2] + row_sum(image * rhs) + row_sum(spread * full)
    out[:, :shared] = image + product(spread, edge_back, 3)
    out[:, shared:] = lanes(norm, curvature)


def image_kernel(per_dev, modes, local, edge, sums, touch, back, from_iface, diag, coefs, rhs_out, image_out, sums_out):
    factors = row_factors(local.shape[0], per_dev, modes)
    rhs = local[...] + product(edge[...], from_iface, 3)
    rhs_out[...] = rhs
    spread = at_elems(factors, coefs) * sums[...]
    spread_into(image_out, spread, back, diag, at_nodes(factors, diag) * rhs)
    sums_out[...] = short_product(image_out[...], touch.at[:, : spread.shape[1]])


def resid_kernel(per_dev, modes, own, edge, rhs, image, sums, image_sums, from_iface, edge_touch, diag, coefs, resid_out, norms_out):
    rows = rhs.shape[0]
    shared = edge.shape[1] - 128
    factors = row_factors(rows, per_dev, modes)
    per_elem, per_node = at_elems(factors, coefs), at_nodes(factors, diag)
    norm = own[:, shared : shared + 1] + edge[:, shared : shared + 1]
    curvature = own[:, shared + 1 : shared + 2] + edge[:, shared + 1 : shared + 2]
    alpha = norm / curvature
    given = edge[:, :shared]
    resid = rhs[...] - alpha * (image[...] + product(given, from_iface, 3))
    resid_out[...] = resid
    new = sums[...] - alpha * (image_sums[...] + product(given, edge_touch, 3))
    after = row_sum(diag[3:4, :] * resid * resid)
    square = row_sum(per_node * resid * resid) + row_sum(per_elem * new * new)
    mixed = row_sum(per_node * resid * rhs[...]) + row_sum(per_elem * new * sums[...])
    norms_out[...] = lanes(after, square, mixed)


def last_kernel(edge, own, norms_own, norms, resid, rhs, vel_out, mag_out):
    shared = edge.shape[1] - 128
    norm = own[:, shared : shared + 1] + edge[:, shared : shared + 1]
    curvature = own[:, shared + 1 : shared + 2] + edge[:, shared + 1 : shared + 2]
    alpha = norm / curvature
    after = norms_own[:, 0:1] + norms[:, 0:1]
    square = norms_own[:, 1:2] + norms[:, 1:2]
    mixed = norms_own[:, 2:3] + norms[:, 2:3]
    beta = after / norm
    alpha_next = after / (square + 2.0 * beta * mixed + beta * beta * curvature)
    answer = (alpha + alpha_next * beta) * rhs[...] + alpha_next * resid[...]
    row = 0
    for out in (vel_out, mag_out):
        comps, _, per_dev, _ = out.shape
        for c in range(comps):
            for s in range(2):
                out[c, s] = answer[row : row + per_dev]
                row += per_dev


def per_device(velocity, vorticity, magnetic, current, elem_nodes, mass_coef, stiff_coef, radial_coef, iface):
    comps, _, per_dev, nodes = velocity.shape
    owners = lax.axis_size("mode")
    modes = per_dev * owners
    block = nodes // owners
    rows = 4 * comps * per_dev
    elems = elem_nodes.shape[1]
    shared = iface.shape[1]
    mass, radial, stiff = (a.reshape(1, elems) for a in (mass_coef, radial_coef, stiff_coef))
    synthesis, analysis = trig_tables(modes, per_dev)

    def shape(*dims, kind=f32):
        return jax.ShapeDtypeStruct(dims, kind)

    in_hbm = pl.BlockSpec(memory_space=pltpu.HBM)
    if block % 128 == 0:
        packed = pl.pallas_call(
            pack_kernel,
            in_specs=[in_hbm] * 4,
            out_shape=shape(owners, 2 * rows, block),
            out_specs=in_hbm,
            scratch_shapes=[
                pltpu.VMEM((4, *velocity.shape), f32),
                pltpu.VMEM((owners, 2 * rows, block), f32),
                pltpu.SemaphoreType.DMA((4,)),
                pltpu.SemaphoreType.DMA((2,)),
            ],
            compiler_params=params(large),
            name="pack",
        )(velocity, magnetic, vorticity, current)
    else:
        packed = jnp.concatenate(
            [a.reshape(rows // 2, owners, block) for a in (velocity, magnetic, vorticity, current)], axis=0
        ).transpose(1, 0, 2)
    columns = lax.all_to_all(packed, "mode", 0, 0, tiled=True)
    tables = (
        shape(nodes, elems + shared, kind=f8),
        shape(elems, nodes, kind=f8),
        shape(nodes, shared, kind=bf16),
        shape(shared, nodes, kind=bf16),
        shape(8, nodes),
        shape(8, elems),
        shape(shared, elems, kind=bf16),
        shape(elems, shared, kind=bf16),
        shape(8, shared),
    )
    in_vmem = pl.BlockSpec(memory_space=pltpu.VMEM)
    built = pl.pallas_call(
        mesh_kernel,
        in_specs=[in_hbm] * 5,
        out_specs=(in_hbm, in_hbm, *[in_vmem] * 7),
        out_shape=tables,
        scratch_shapes=[
            pltpu.VMEM((nodes, elems), bf16),
            pltpu.VMEM((elems, nodes), bf16),
            pltpu.VMEM((nodes, elems + shared), f8),
            pltpu.VMEM((elems, nodes), f8),
            pltpu.VMEM(elem_nodes.shape, jnp.int32),
            pltpu.VMEM((1, elems), f32),
            pltpu.VMEM((1, elems), f32),
            pltpu.VMEM((1, elems), f32),
            pltpu.VMEM(iface.shape, jnp.int32),
            pltpu.SemaphoreType.DMA((5,)),
            pltpu.SemaphoreType.DMA((2 * elems // math.gcd(elems, 256) + 1,)),
        ],
        compiler_params=params(large),
        name="incidence",
        cost_estimate=pl.CostEstimate(flops=2**31, bytes_accessed=2**23, transcendentals=0),
    )(elem_nodes, mass, radial, stiff, iface)
    columns, *built = lax.optimization_barrier((columns, *built))
    touch, back, at_iface, from_iface, diag, coefs, edge_touch, edge_back, edge_diag = built
    terms = pl.pallas_call(
        nonlinear_kernel,
        out_shape=pltpu.VMEM((owners, rows, block), f32),
        compiler_params=params(),
        name="nonlinear",
        cost_estimate=pl.CostEstimate(flops=2**33, bytes_accessed=2**24, transcendentals=0),
    )(pltpu.with_memory_space_constraint(columns, pltpu.VMEM), synthesis, analysis)
    forcing = lax.all_to_all(terms, "mode", 0, 0, tiled=True)
    if block % 128:
        forcing = forcing.transpose(1, 0, 2).reshape(1, rows, nodes)

    def swap(array):
        return lax.ppermute(array, "mer", [(0, 1), (1, 0)])

    def call(kernel, name, outs, work=0):
        own = () if kernel is rhs_edge_kernel else (per_dev, modes)
        cost = pl.CostEstimate(flops=work, bytes_accessed=work // 512, transcendentals=0) if work else None
        return pl.pallas_call(
            functools.partial(kernel, *own),
            out_shape=tuple(outs),
            compiler_params=params(),
            name=name,
            cost_estimate=cost,
        )

    full, part, small_row = shape(rows, nodes), shape(rows, elems), shape(rows, 128)
    spread, edge_own = call(rhs_edge_kernel, "rhs_edge", (part, shape(rows, shared)))(
        forcing, touch, edge_back, edge_diag, coefs
    )
    edge = swap(edge_own)
    local, sums, inner = call(rhs_kernel, "rhs", (full, part, small_row), 2**30)(
        forcing, spread, touch, back, diag
    )
    sums, image_edge_own = call(image_edge_kernel, "image_edge", (part, shape(rows, shared + 128)))(
        edge_own, edge, sums, inner, edge_touch, edge_back, edge_diag, coefs
    )
    image_edge = swap(image_edge_own)
    rhs, image, image_sums = call(image_kernel, "image", (full, full, part), 2**30)(
        local, edge, sums, touch, back, from_iface, diag, coefs
    )
    resid, norms_own = call(resid_kernel, "resid", (full, small_row))(
        image_edge_own, image_edge, rhs, image, sums, image_sums, from_iface, edge_touch, diag, coefs
    )
    out = shape(*velocity.shape)
    return pl.pallas_call(
        last_kernel, out_shape=(out, out), compiler_params=params(), name="last"
    )(image_edge, image_edge_own, norms_own, swap(norms_own), resid, rhs)


def solution(mesh):
    field = P("runs", None, "mode", "mer")
    placed = (field, field, field, field, P(None, "mer"), P("mer"), P("mer"), P("mer"), P("mer", None))
    return jax.shard_map(
        per_device, mesh=mesh, in_specs=placed, out_specs=(field, field), check_vma=False
    )
```

```python
import functools
import math

import jax
import jax.numpy as jnp
import numpy as np
from jax import lax
from jax.experimental import pallas as pl
from jax.experimental.pallas import tpu as pltpu
from jax.sharding import PartitionSpec as P

step_size = 0.05
diffusion_ratio = 2.0
f32 = jnp.float32
bf16 = jnp.bfloat16
f8 = jnp.float8_e4m3fn
largest, radix, exact_below = 16.0, 32.0, 2048.0
small, medium, large = 16 * 2**20, 54 * 2**20, 60 * 2**20


def params(limit=small):
    return pltpu.CompilerParams(vmem_limit_bytes=limit)


def halves(table):
    high = table.astype(np.float32).astype(jnp.bfloat16)
    low = (table - high.astype(np.float64)).astype(np.float32).astype(jnp.bfloat16)
    return high, low


def trig_tables(modes, per_dev):
    angles = 2 * modes
    order = np.arange(modes)
    points = np.arange(angles)
    phase = (points[:, None] * order[None, :] % angles) * (2.0 * math.pi / angles)
    both = np.stack([np.cos(phase), np.sin(phase)])
    both = both.reshape(2, angles, modes // per_dev, per_dev)
    factor = np.where(order == 0, 1.0, 2.0).reshape(modes // per_dev, per_dev) / angles
    same = np.eye(2)
    synthesis = np.einsum("pq,sajk->pajqsk", same, both).reshape(2 * angles, -1)
    analysis = np.einsum("pq,sajk,jk->jqskpa", same, both, factor * step_size).reshape(-1, 2 * angles)
    out = []
    for table in (synthesis, analysis):
        high, low = halves(table)
        out.append(jnp.asarray(np.concatenate([high, high, low], axis=1)))
    return out


def pieces(array, count):
    parts = []
    rest = array
    for i in range(count):
        part = rest.astype(bf16).astype(f32)
        parts.append(part)
        rest = rest - part
    return jnp.concatenate(parts, axis=0).astype(bf16)


def product(array, exact, count=2):
    rows = array.shape[0]
    out = jnp.dot(pieces(array, count), exact[...], preferred_element_type=f32)
    total = out[:rows]
    for i in range(1, count):
        total = total + out[i * rows : (i + 1) * rows]
    return total


def short_parts(array, count=4):
    top = jnp.maximum(jnp.max(jnp.abs(array), axis=1, keepdims=True), 1e-30)
    parts = []
    rest = array * (largest / top)
    for _ in range(count):
        part = jnp.round(rest)
        parts.append(part)
        rest = (rest - part) * radix
    return jnp.concatenate(parts, axis=0), top / largest


def short_total(out, scale, count=4):
    rows = scale.shape[0]
    total = out[(count - 1) * rows :]
    for i in reversed(range(count - 1)):
        total = total * (1.0 / radix) + out[i * rows : (i + 1) * rows]
    return total * scale


def short_product(array, exact):
    parts, scale = short_parts(array)
    return short_total(jnp.dot(parts.astype(f8), exact[...], preferred_element_type=f32), scale)


def spread_into(target, values, back, diag, base):
    few = jnp.max(diag[4:5, :]) * largest <= exact_below

    @pl.when(few)
    def _():
        target[...] = base + short_product(values, back)

    @pl.when(jnp.logical_not(few))
    def _():
        target[...] = base + product(values, back[...].astype(f32).astype(bf16), 3)


def table_product(table, values):
    high = values.astype(bf16)
    low = (values - high.astype(f32)).astype(bf16)
    return jnp.dot(table, jnp.concatenate([high, low, high], axis=0), preferred_element_type=f32)


def start_all(sources, targets, sems):
    copies = [
        pltpu.make_async_copy(source, target, sems.at[i])
        for i, (source, target) in enumerate(zip(sources, targets))
    ]
    for copy in copies:
        copy.start()
    return copies


def ring_pack_kernel(vel, mag, vort, cur, synthesis_hbm, analysis_hbm, *rest):
    *outs, synthesis, analysis, held, in_sems = rest
    owners, block = len(outs), outs[0].shape[1]
    me = lax.axis_index("mode")
    copies = start_all(
        (vel, mag, vort, cur, synthesis_hbm, analysis_hbm),
        [*(held.at[i] for i in range(4)), synthesis, analysis],
        in_sems,
    )
    starts = [pl.multiple_of(lax.rem(me + d, owners) * block, block) for d in range(owners)]
    row = 0
    for i in range(4):
        copies[i].wait()
        _, comps, _, per_dev, _ = held.shape
        for c in range(comps):
            for s in range(2):
                for d in range(owners):
                    outs[d][row : row + per_dev, :] = held[i, c, s, :, pl.ds(starts[d], block)]
                row += per_dev
    for copy in copies[4:]:
        copy.wait()


def ring_nonlinear_kernel(*refs):
    *blocks, synthesis, analysis, out, fields = refs
    owners = len(blocks)
    me = lax.axis_index("mode")
    for d in range(owners):
        fields[lax.rem(me + owners - d, owners)] = blocks[d][...]
    nonlinear_kernel(fields, synthesis, analysis, out)


def nonlinear_kernel(fields, synthesis, analysis, out):
    owners, rows, block = fields.shape
    pair = rows // 6
    angles = synthesis.shape[0] // 2
    phys = []
    for t in range(6):
        coef = jnp.concatenate([fields[j, t * pair : (t + 1) * pair, :] for j in range(owners)], axis=0)
        values = table_product(synthesis[...], coef)
        phys += [values[:angles], values[angles:]]
    vel, mag, vort, cur = phys[0:3], phys[3:6], phys[6:9], phys[9:12]

    def cross(a, b, i):
        j, k = (i + 1) % 3, (i + 2) % 3
        return a[j] * b[k] - a[k] * b[j]

    terms = [cross(vel, vort, i) + cross(cur, mag, i) for i in range(3)]
    terms += [cross(vel, mag, i) for i in range(3)]
    for t in range(3):
        coef = table_product(analysis[...], jnp.concatenate([terms[2 * t], terms[2 * t + 1]], axis=0))
        for j in range(owners):
            span = slice(t * pair, (t + 1) * pair)
            out[j, span, :] = fields[j, span, :] + coef[j * pair : (j + 1) * pair]


def mesh_kernel(nodes_hbm, mass_hbm, radial_hbm, stiff_hbm, iface_hbm, touch_out, back_out, at_iface, from_iface, diag, coefs, edge_touch, edge_back, edge_diag, touch, back, touch8, back8, elem_nodes, mass, radial, stiff, iface, in_sems, out_sems):
    loads = start_all(
        (nodes_hbm, mass_hbm, radial_hbm, stiff_hbm, iface_hbm), (elem_nodes, mass, radial, stiff, iface), in_sems
    )
    for load in loads:
        load.wait()
    nodes, elems = touch.shape
    shared = iface.shape[1]
    fields = 8
    words = nodes // fields
    width = math.gcd(elems, 256)
    sent = []
    for c in range(elems // width):
        span = slice(c * width, (c + 1) * width)
        word = lax.broadcasted_iota(jnp.int32, (words, width), 0)
        total = jnp.zeros((words, width), jnp.int32)
        for i in range(elem_nodes.shape[0]):
            ids = elem_nodes[i : i + 1, span]
            field = ids // words
            value = jnp.left_shift(1, field * 4)
            total = total + jnp.where(ids - field * words == word, value, 0)
        for q in range(fields):
            count = jnp.right_shift(total, 4 * q) & 15
            touch[q * words : (q + 1) * words, span] = count.astype(f32).astype(bf16)
        column = pl.ds(c * width, width)
        touch8[:, span] = touch[:, span].astype(f32).astype(f8)
        sent.append(pltpu.make_async_copy(touch8.at[:, column], touch_out.at[:, column], out_sems.at[c]))
        sent[-1].start()
        back[span, :] = touch[:, span].T
        back8[span, :] = back[span, :].astype(f32).astype(f8)
        sent.append(pltpu.make_async_copy(back8.at[column, :], back_out.at[column, :], out_sems.at[elems // width + c]))
        sent[-1].start()
    node = lax.broadcasted_iota(jnp.int32, (nodes, shared), 0)
    hit = jnp.where(iface[...] == node, 1.0, 0.0)
    at_iface[...] = hit.astype(bf16)
    last = pl.ds(elems, shared)
    touch8[:, elems:] = hit.astype(f8)
    sent.append(pltpu.make_async_copy(touch8.at[:, last], touch_out.at[:, last], out_sems.at[2 * elems // width]))
    sent[-1].start()
    from_iface[...] = hit.T.astype(bf16)
    zero = jnp.zeros((5, elems), f32)
    one = jnp.ones((1, elems), f32)
    coefs[...] = jnp.concatenate([mass[...] / 12.0, radial[...] / 12.0, stiff[...], zero], axis=0)
    scaled = jnp.concatenate([mass[...] / 12.0, radial[...] / 12.0, 6.0 * stiff[...], one * 0.0, one, zero[:3]], axis=0)
    sums = product(scaled, back, 3)
    hits = jnp.dot(jnp.ones((16, shared), bf16), from_iface[...], preferred_element_type=f32)
    row = lax.broadcasted_iota(jnp.int32, (8, nodes), 0)
    diag[...] = jnp.where(row == 3, 1.0 - 0.5 * hits[:8], sums)
    edge_diag[...] = product(sums, at_iface, 3)
    counts = jnp.dot(from_iface[...], touch[...], preferred_element_type=f32)
    edge_touch[...] = counts.astype(bf16)
    edge_back[...] = counts.T.astype(bf16)
    for copy in sent:
        copy.wait()


def row_factors(rows, per_dev, modes):
    row = lax.broadcasted_iota(jnp.int32, (rows, 1), 0)
    order = (lax.axis_index("mode") * per_dev + row % per_dev).astype(f32)
    shift = (order / modes) ** 2
    scale = jnp.where(row < rows // 2, 1.0, diffusion_ratio).astype(f32)
    return shift, scale


def at_elems(factors, coefs):
    shift, scale = factors
    return coefs[0:1, :] + shift * coefs[1:2, :] - scale * coefs[2:3, :]


def at_nodes(factors, diag):
    shift, scale = factors
    return diag[0:1, :] + shift * diag[1:2, :] + scale * diag[2:3, :]


def row_sum(array):
    return jnp.sum(array, axis=1, keepdims=True)


def lanes(*columns):
    rows = columns[0].shape[0]
    lane = lax.broadcasted_iota(jnp.int32, (rows, 128), 1)
    out = jnp.broadcast_to(columns[-1], (rows, 128))
    for i in reversed(range(len(columns) - 1)):
        out = jnp.where(lane == i, columns[i], out)
    return out


def together(forcing):
    return jnp.concatenate([forcing[b] for b in range(forcing.shape[0])], axis=1)


def rhs_edge_kernel(forcing, touch_hbm, back_hbm, diag_hbm, coefs_hbm, spread_out, edge, touch, edge_back, edge_diag, coefs, sems):
    nodes = touch.shape[0]
    elems = coefs.shape[1]
    width = nodes // 4
    spans = [pl.ds(i * width, width) for i in range(4)]
    loads = start_all(
        [touch_hbm.at[span, :] for span in spans] + [coefs_hbm, back_hbm, diag_hbm],
        [touch.at[span, :] for span in spans] + [coefs, edge_back, edge_diag],
        sems,
    )
    parts, scale = short_parts(together(forcing))
    out = 0.0
    for i in range(4):
        loads[i].wait()
        some = parts[:, i * width : (i + 1) * width].astype(f8)
        out = out + jnp.dot(some, touch[i * width : (i + 1) * width, :], preferred_element_type=f32)
    sums = short_total(out, scale)
    for load in loads[4:]:
        load.wait()
    spread = sums[:, :elems] * coefs[0:1, :]
    spread_out[...] = spread
    edge[...] = edge_diag[0:1, :] * sums[:, elems:] + product(spread, edge_back, 3)


def rhs_kernel(per_dev, modes, forcing, spread, touch, back, diag, local, sums, inner):
    rows = spread.shape[0]
    spread_into(local, spread[...], back, diag, diag[0:1, :] * together(forcing))
    image = local[...]
    sums[...] = short_product(image, touch.at[:, : spread.shape[1]])
    square = (2.0 * diag[3:4, :] - 1.0) * image * image
    inner[...] = lanes(row_sum(square), row_sum(at_nodes(row_factors(rows, per_dev, modes), diag) * square))


def image_edge_kernel(per_dev, modes, edge_own, edge, sums, inner, edge_touch, edge_back, edge_diag, coefs, sums_out, out):
    rows, shared = edge.shape
    factors = row_factors(rows, per_dev, modes)
    rhs = edge_own[...] + edge[...]
    full = sums[...] + product(edge[...], edge_touch, 3)
    sums_out[...] = full
    spread = at_elems(factors, coefs) * full
    image = at_nodes(factors, edge_diag) * rhs
    norm = inner[:, 0:1] + 0.5 * row_sum(rhs * rhs)
    curvature = inner[:, 1:2] + row_sum(image * rhs) + row_sum(spread * full)
    out[:, :shared] = image + product(spread, edge_back, 3)
    out[:, shared:] = lanes(norm, curvature)


def image_kernel(per_dev, modes, local, edge, sums, touch, back, from_iface, diag, coefs, rhs_out, image_out, sums_out):
    factors = row_factors(local.shape[0], per_dev, modes)
    rhs = local[...] + product(edge[...], from_iface, 3)
    rhs_out[...] = rhs
    spread = at_elems(factors, coefs) * sums[...]
    spread_into(image_out, spread, back, diag, at_nodes(factors, diag) * rhs)
    sums_out[...] = short_product(image_out[...], touch.at[:, : spread.shape[1]])


def resid_kernel(per_dev, modes, own, edge, rhs, image, sums, image_sums, from_iface, edge_touch, diag, coefs, resid_out, norms_out):
    rows = rhs.shape[0]
    shared = edge.shape[1] - 128
    factors = row_factors(rows, per_dev, modes)
    per_elem, per_node = at_elems(factors, coefs), at_nodes(factors, diag)
    norm = own[:, shared : shared + 1] + edge[:, shared : shared + 1]
    curvature = own[:, shared + 1 : shared + 2] + edge[:, shared + 1 : shared + 2]
    alpha = norm / curvature
    given = edge[:, :shared]
    resid = rhs[...] - alpha * (image[...] + product(given, from_iface, 3))
    resid_out[...] = resid
    new = sums[...] - alpha * (image_sums[...] + product(given, edge_touch, 3))
    after = row_sum(diag[3:4, :] * resid * resid)
    square = row_sum(per_node * resid * resid) + row_sum(per_elem * new * new)
    mixed = row_sum(per_node * resid * rhs[...]) + row_sum(per_elem * new * sums[...])
    norms_out[...] = lanes(after, square, mixed)


def last_kernel(edge, own, norms_own, norms, resid, rhs, vel_out, mag_out):
    shared = edge.shape[1] - 128
    norm = own[:, shared : shared + 1] + edge[:, shared : shared + 1]
    curvature = own[:, shared + 1 : shared + 2] + edge[:, shared + 1 : shared + 2]
    alpha = norm / curvature
    after = norms_own[:, 0:1] + norms[:, 0:1]
    square = norms_own[:, 1:2] + norms[:, 1:2]
    mixed = norms_own[:, 2:3] + norms[:, 2:3]
    beta = after / norm
    alpha_next = after / (square + 2.0 * beta * mixed + beta * beta * curvature)
    answer = (alpha + alpha_next * beta) * rhs[...] + alpha_next * resid[...]
    row = 0
    for out in (vel_out, mag_out):
        comps, _, per_dev, _ = out.shape
        for c in range(comps):
            for s in range(2):
                out[c, s] = answer[row : row + per_dev]
                row += per_dev


def per_device(velocity, vorticity, magnetic, current, elem_nodes, mass_coef, stiff_coef, radial_coef, iface):
    comps, _, per_dev, nodes = velocity.shape
    owners = lax.axis_size("mode")
    modes = per_dev * owners
    block = nodes // owners
    rows = 4 * comps * per_dev
    elems = elem_nodes.shape[1]
    shared = iface.shape[1]
    mass, radial, stiff = (a.reshape(1, elems) for a in (mass_coef, radial_coef, stiff_coef))
    synthesis, analysis = trig_tables(modes, per_dev)

    def shape(*dims, kind=f32):
        return jax.ShapeDtypeStruct(dims, kind)

    in_hbm = pl.BlockSpec(memory_space=pltpu.HBM)

    def pin(array):
        return pltpu.with_memory_space_constraint(array, pltpu.HBM)

    nonlinear_cost = pl.CostEstimate(flops=2**33, bytes_accessed=2**24, transcendentals=0)
    if owners <= 8 and block % 128 == 0:
        *blocks, synthesis, analysis = pl.pallas_call(
            ring_pack_kernel,
            in_specs=[in_hbm] * 6,
            out_shape=(pltpu.VMEM((2 * rows, block), f32),) * owners
            + tuple(pltpu.VMEM(t.shape, t.dtype) for t in (synthesis, analysis)),
            scratch_shapes=[pltpu.VMEM((4, *velocity.shape), f32), pltpu.SemaphoreType.DMA((6,))],
            compiler_params=params(medium),
            name="pack",
        )(*(pin(a) for a in (velocity, magnetic, vorticity, current, synthesis, analysis)))
        for d in range(1, owners):
            blocks[d] = lax.ppermute(blocks[d], "mode", [(i, (i + d) % owners) for i in range(owners)])
        terms = pl.pallas_call(
            ring_nonlinear_kernel,
            out_shape=shape(owners, rows, block),
            scratch_shapes=[pltpu.VMEM((owners, 2 * rows, block), f32)],
            compiler_params=params(),
            name="nonlinear",
            cost_estimate=nonlinear_cost,
        )(*blocks, synthesis, analysis)
    else:
        packed = jnp.concatenate(
            [a.reshape(rows // 2, owners, block) for a in (velocity, magnetic, vorticity, current)], axis=0
        ).transpose(1, 0, 2)
        terms = pl.pallas_call(
            nonlinear_kernel,
            out_shape=shape(owners, rows, block),
            compiler_params=params(),
            name="nonlinear",
            cost_estimate=nonlinear_cost,
        )(lax.all_to_all(packed, "mode", 0, 0, tiled=True), synthesis, analysis)
    terms, elem_nodes = lax.optimization_barrier((terms, elem_nodes))
    forcing = lax.all_to_all(terms, "mode", 0, 0, tiled=True)
    tables = (
        shape(nodes, elems + shared, kind=f8),
        shape(elems, nodes, kind=f8),
        shape(nodes, shared, kind=bf16),
        shape(shared, nodes, kind=bf16),
        shape(8, nodes),
        shape(8, elems),
        shape(shared, elems, kind=bf16),
        shape(elems, shared, kind=bf16),
        shape(8, shared),
    )
    in_vmem = pl.BlockSpec(memory_space=pltpu.VMEM)
    built = pl.pallas_call(
        mesh_kernel,
        in_specs=[in_hbm] * 5,
        out_specs=(in_hbm, in_hbm, *[in_vmem] * 7),
        out_shape=tables,
        scratch_shapes=[
            pltpu.VMEM((nodes, elems), bf16),
            pltpu.VMEM((elems, nodes), bf16),
            pltpu.VMEM((nodes, elems + shared), f8),
            pltpu.VMEM((elems, nodes), f8),
            pltpu.VMEM(elem_nodes.shape, jnp.int32),
            pltpu.VMEM((1, elems), f32),
            pltpu.VMEM((1, elems), f32),
            pltpu.VMEM((1, elems), f32),
            pltpu.VMEM(iface.shape, jnp.int32),
            pltpu.SemaphoreType.DMA((5,)),
            pltpu.SemaphoreType.DMA((2 * elems // math.gcd(elems, 256) + 1,)),
        ],
        compiler_params=params(large),
        name="incidence",
        cost_estimate=pl.CostEstimate(flops=2**31, bytes_accessed=2**23, transcendentals=0),
    )(elem_nodes, mass, radial, stiff, iface)
    touch, back, at_iface, from_iface, diag, coefs, edge_touch, edge_back, edge_diag = built
    if block % 128:
        forcing = forcing.transpose(1, 0, 2).reshape(1, rows, nodes)

    def swap(array):
        return lax.ppermute(array, "mer", [(0, 1), (1, 0)])

    def call(kernel, name, outs, work=0):
        cost = pl.CostEstimate(flops=work, bytes_accessed=work // 512, transcendentals=0) if work else None
        return pl.pallas_call(
            functools.partial(kernel, per_dev, modes),
            out_shape=tuple(outs),
            compiler_params=params(),
            name=name,
            cost_estimate=cost,
        )

    full, part, small_row = shape(rows, nodes), shape(rows, elems), shape(rows, 128)
    kept = [pltpu.VMEM(a.shape, a.dtype) for a in (touch, edge_back, edge_diag, coefs)]
    spread, edge_own, touch, edge_back, edge_diag, coefs = pl.pallas_call(
        rhs_edge_kernel,
        in_specs=[in_vmem] + [in_hbm] * 4,
        out_shape=(part, shape(rows, shared), *kept),
        scratch_shapes=[pltpu.SemaphoreType.DMA((7,))],
        compiler_params=params(),
        name="rhs_edge",
    )(forcing, *(pin(a) for a in (touch, edge_back, edge_diag, coefs)))
    edge = swap(edge_own)
    local, sums, inner = call(rhs_kernel, "rhs", (full, part, small_row), 2**30)(
        forcing, spread, touch, back, diag
    )
    sums, image_edge_own = call(image_edge_kernel, "image_edge", (part, shape(rows, shared + 128)))(
        edge_own, edge, sums, inner, edge_touch, edge_back, edge_diag, coefs
    )
    image_edge = swap(image_edge_own)
    rhs, image, image_sums = call(image_kernel, "image", (full, full, part), 2**30)(
        local, edge, sums, touch, back, from_iface, diag, coefs
    )
    resid, norms_own = call(resid_kernel, "resid", (full, small_row))(
        image_edge_own, image_edge, rhs, image, sums, image_sums, from_iface, edge_touch, diag, coefs
    )
    out = shape(*velocity.shape)
    return pl.pallas_call(
        last_kernel, out_shape=(out, out), compiler_params=params(), name="last"
    )(image_edge, image_edge_own, norms_own, swap(norms_own), resid, rhs)


def solution(mesh):
    field = P("runs", None, "mode", "mer")
    placed = (field, field, field, field, P(None, "mer"), P("mer"), P("mer"), P("mer"), P("mer", None))
    return jax.shard_map(
        per_device, mesh=mesh, in_specs=placed, out_specs=(field, field), check_vma=False
    )
```

```python
import functools
import math

import jax
import jax.numpy as jnp
import numpy as np
from jax import lax
from jax.experimental import pallas as pl
from jax.experimental.pallas import tpu as pltpu
from jax.sharding import PartitionSpec as P

step_size = 0.05
diffusion_ratio = 2.0
f32 = jnp.float32
bf16 = jnp.bfloat16
f8 = jnp.float8_e4m3fn
largest, radix, exact_below = 16.0, 32.0, 2048.0
small, medium, large = 16 * 2**20, 54 * 2**20, 60 * 2**20


def params(limit=small):
    return pltpu.CompilerParams(vmem_limit_bytes=limit)


def halves(table):
    high = table.astype(np.float32).astype(jnp.bfloat16)
    low = (table - high.astype(np.float64)).astype(np.float32).astype(jnp.bfloat16)
    return high, low


def trig_tables(modes, per_dev):
    angles = 2 * modes
    order = np.arange(modes)
    points = np.arange(angles)
    phase = (points[:, None] * order[None, :] % angles) * (2.0 * math.pi / angles)
    both = np.stack([np.cos(phase), np.sin(phase)])
    both = both.reshape(2, angles, modes // per_dev, per_dev)
    factor = np.where(order == 0, 1.0, 2.0).reshape(modes // per_dev, per_dev) / angles
    same = np.eye(2)
    synthesis = np.einsum("pq,sajk->pajqsk", same, both).reshape(2 * angles, -1)
    analysis = np.einsum("pq,sajk,jk->jqskpa", same, both, factor * step_size).reshape(-1, 2 * angles)
    out = []
    for table in (synthesis, analysis):
        high, low = halves(table)
        out.append(jnp.asarray(np.concatenate([high, high, low], axis=1)))
    return out


def pieces(array, count):
    parts = []
    rest = array
    for i in range(count):
        part = rest.astype(bf16).astype(f32)
        parts.append(part)
        rest = rest - part
    return jnp.concatenate(parts, axis=0).astype(bf16)


def product(array, exact, count=2):
    rows = array.shape[0]
    out = jnp.dot(pieces(array, count), exact[...], preferred_element_type=f32)
    total = out[:rows]
    for i in range(1, count):
        total = total + out[i * rows : (i + 1) * rows]
    return total


def short_parts(array, count=4):
    top = jnp.maximum(jnp.max(jnp.abs(array), axis=1, keepdims=True), 1e-30)
    parts = []
    rest = array * (largest / top)
    for _ in range(count):
        part = jnp.round(rest)
        parts.append(part)
        rest = (rest - part) * radix
    return jnp.concatenate(parts, axis=0), top / largest


def short_total(out, scale, count=4):
    rows = scale.shape[0]
    total = out[(count - 1) * rows :]
    for i in reversed(range(count - 1)):
        total = total * (1.0 / radix) + out[i * rows : (i + 1) * rows]
    return total * scale


def short_product(array, exact):
    parts, scale = short_parts(array)
    return short_total(jnp.dot(parts.astype(f8), exact[...], preferred_element_type=f32), scale)


def spread_into(target, values, back, diag, base):
    few = jnp.max(diag[4:5, :]) * largest <= exact_below

    @pl.when(few)
    def _():
        target[...] = base + short_product(values, back)

    @pl.when(jnp.logical_not(few))
    def _():
        target[...] = base + product(values, back[...].astype(f32).astype(bf16), 3)


def table_product(table, values):
    high = values.astype(bf16)
    low = (values - high.astype(f32)).astype(bf16)
    return jnp.dot(table, jnp.concatenate([high, low, high], axis=0), preferred_element_type=f32)


def start_all(sources, targets, sems):
    copies = [
        pltpu.make_async_copy(source, target, sems.at[i])
        for i, (source, target) in enumerate(zip(sources, targets))
    ]
    for copy in copies:
        copy.start()
    return copies


def ring_pack_kernel(vel, mag, vort, cur, synthesis_hbm, analysis_hbm, *rest):
    *outs, synthesis, analysis, held, in_sems = rest
    owners, block = len(outs), outs[0].shape[1]
    me = lax.axis_index("mode")
    copies = start_all(
        (vel, mag, vort, cur, synthesis_hbm, analysis_hbm),
        [*(held.at[i] for i in range(4)), synthesis, analysis],
        in_sems,
    )
    starts = [pl.multiple_of(lax.rem(me + d, owners) * block, block) for d in range(owners)]
    row = 0
    for i in range(4):
        copies[i].wait()
        _, comps, _, per_dev, _ = held.shape
        for c in range(comps):
            for s in range(2):
                for d in range(owners):
                    outs[d][row : row + per_dev, :] = held[i, c, s, :, pl.ds(starts[d], block)]
                row += per_dev
    for copy in copies[4:]:
        copy.wait()


def ring_nonlinear_kernel(*refs):
    *blocks, synthesis, analysis, out, fields = refs
    owners = len(blocks)
    me = lax.axis_index("mode")
    for d in range(owners):
        fields[lax.rem(me + owners - d, owners)] = blocks[d][...]
    nonlinear_kernel(fields, synthesis, analysis, out)


def nonlinear_kernel(fields, synthesis, analysis, out):
    owners, rows, block = fields.shape
    pair = rows // 6
    angles = synthesis.shape[0] // 2
    phys = []
    for t in range(6):
        coef = jnp.concatenate([fields[j, t * pair : (t + 1) * pair, :] for j in range(owners)], axis=0)
        values = table_product(synthesis[...], coef)
        phys += [values[:angles], values[angles:]]
    vel, mag, vort, cur = phys[0:3], phys[3:6], phys[6:9], phys[9:12]

    def cross(a, b, i):
        j, k = (i + 1) % 3, (i + 2) % 3
        return a[j] * b[k] - a[k] * b[j]

    terms = [cross(vel, vort, i) + cross(cur, mag, i) for i in range(3)]
    terms += [cross(vel, mag, i) for i in range(3)]
    for t in range(3):
        coef = table_product(analysis[...], jnp.concatenate([terms[2 * t], terms[2 * t + 1]], axis=0))
        for j in range(owners):
            span = slice(t * pair, (t + 1) * pair)
            out[j, span, :] = fields[j, span, :] + coef[j * pair : (j + 1) * pair]


def mesh_kernel(nodes_hbm, mass_hbm, radial_hbm, stiff_hbm, iface_hbm, touch_out, back_out, from_iface, diag, coefs, edge_touch, edge_back, edge_diag, touch, back, elem_nodes, mass, radial, stiff, iface, in_sems, out_sems):
    loads = start_all(
        (nodes_hbm, mass_hbm, radial_hbm, stiff_hbm, iface_hbm), (elem_nodes, mass, radial, stiff, iface), in_sems
    )
    for load in loads:
        load.wait()
    elems, nodes = back.shape
    shared = iface.shape[1]
    fields = 8
    words = nodes // fields
    width = math.gcd(elems, 256)
    sent = []

    def send(source, target):
        sent.append(pltpu.make_async_copy(source, target, out_sems.at[len(sent)]))
        sent[-1].start()

    for c in range(elems // width):
        span = slice(c * width, (c + 1) * width)
        word = lax.broadcasted_iota(jnp.int32, (words, width), 0)
        total = jnp.zeros((words, width), jnp.int32)
        for i in range(elem_nodes.shape[0]):
            ids = elem_nodes[i : i + 1, span]
            field = ids // words
            value = jnp.left_shift(1, field * 4)
            total = total + jnp.where(ids - field * words == word, value, 0)
        for q in range(fields):
            count = (jnp.right_shift(total, 4 * q) & 15).astype(f32)
            touch[q * words : (q + 1) * words, span] = count.astype(f8)
            back[span, q * words : (q + 1) * words] = count.T.astype(f8)
        column = pl.ds(c * width, width)
        send(touch.at[:, column], touch_out.at[:, column])
        send(back.at[column, :], back_out.at[column, :])
    node = lax.broadcasted_iota(jnp.int32, (nodes, shared), 0)
    hit = jnp.where(iface[...] == node, 1.0, 0.0)
    touch[:, elems:] = hit.astype(f8)
    send(touch.at[:, pl.ds(elems, shared)], touch_out.at[:, pl.ds(elems, shared)])
    hit = hit.T
    from_iface[...] = hit.astype(bf16)
    counts = jnp.dot(hit.astype(f8), touch[:, :elems], preferred_element_type=f32)
    edge_touch[...] = counts.astype(bf16)
    edge_back[...] = counts.T.astype(bf16)
    zero = jnp.zeros((5, elems), f32)
    one = jnp.ones((1, elems), f32)
    coefs[...] = jnp.concatenate([mass[...] / 12.0, radial[...] / 12.0, stiff[...], zero], axis=0)
    scaled = jnp.concatenate(
        [mass[...] / 12.0, radial[...] / 12.0, 6.0 * stiff[...], one * 0.0, one, zero[:3]], axis=0
    )
    diag[...] = short_product(scaled, back)

    @pl.when(jnp.max(diag[4:5, :]) * largest > exact_below)
    def _():
        diag[...] = product(scaled, back[...].astype(f32).astype(bf16), 3)

    edge_diag[...] = short_product(diag[...], touch.at[:, elems:])
    hits = jnp.sum(hit, axis=0, keepdims=True)
    row = lax.broadcasted_iota(jnp.int32, (8, nodes), 0)
    diag[...] = jnp.where(row == 3, 1.0 - 0.5 * hits, diag[...])
    for copy in sent:
        copy.wait()


def row_factors(rows, per_dev, modes):
    row = lax.broadcasted_iota(jnp.int32, (rows, 1), 0)
    order = (lax.axis_index("mode") * per_dev + row % per_dev).astype(f32)
    shift = (order / modes) ** 2
    scale = jnp.where(row < rows // 2, 1.0, diffusion_ratio).astype(f32)
    return shift, scale


def at_elems(factors, coefs):
    shift, scale = factors
    return coefs[0:1, :] + shift * coefs[1:2, :] - scale * coefs[2:3, :]


def at_nodes(factors, diag):
    shift, scale = factors
    return diag[0:1, :] + shift * diag[1:2, :] + scale * diag[2:3, :]


def row_sum(array):
    return jnp.sum(array, axis=1, keepdims=True)


def lanes(*columns):
    rows = columns[0].shape[0]
    lane = lax.broadcasted_iota(jnp.int32, (rows, 128), 1)
    out = jnp.broadcast_to(columns[-1], (rows, 128))
    for i in reversed(range(len(columns) - 1)):
        out = jnp.where(lane == i, columns[i], out)
    return out


def together(forcing):
    return jnp.concatenate([forcing[b] for b in range(forcing.shape[0])], axis=1)


def rhs_edge_kernel(forcing, touch_hbm, back_hbm, diag_hbm, coefs_hbm, spread_out, edge, touch, edge_back, edge_diag, coefs, sems):
    nodes = touch.shape[0]
    elems = coefs.shape[1]
    width = nodes // 4
    spans = [pl.ds(i * width, width) for i in range(4)]
    loads = start_all(
        [touch_hbm.at[span, :] for span in spans] + [coefs_hbm, back_hbm, diag_hbm],
        [touch.at[span, :] for span in spans] + [coefs, edge_back, edge_diag],
        sems,
    )
    parts, scale = short_parts(together(forcing))
    out = 0.0
    for i in range(4):
        loads[i].wait()
        some = parts[:, i * width : (i + 1) * width].astype(f8)
        out = out + jnp.dot(some, touch[i * width : (i + 1) * width, :], preferred_element_type=f32)
    sums = short_total(out, scale)
    for load in loads[4:]:
        load.wait()
    spread = sums[:, :elems] * coefs[0:1, :]
    spread_out[...] = spread
    edge[...] = edge_diag[0:1, :] * sums[:, elems:] + product(spread, edge_back, 3)


def rhs_kernel(per_dev, modes, forcing, spread, touch, back, diag, local, sums, inner):
    rows = spread.shape[0]
    spread_into(local, spread[...], back, diag, diag[0:1, :] * together(forcing))
    image = local[...]
    sums[...] = short_product(image, touch.at[:, : spread.shape[1]])
    square = (2.0 * diag[3:4, :] - 1.0) * image * image
    inner[...] = lanes(row_sum(square), row_sum(at_nodes(row_factors(rows, per_dev, modes), diag) * square))


def image_edge_kernel(per_dev, modes, edge_own, edge, sums, inner, edge_touch, edge_back, edge_diag, coefs, sums_out, out):
    rows, shared = edge.shape
    factors = row_factors(rows, per_dev, modes)
    rhs = edge_own[...] + edge[...]
    full = sums[...] + product(edge[...], edge_touch, 3)
    sums_out[...] = full
    spread = at_elems(factors, coefs) * full
    image = at_nodes(factors, edge_diag) * rhs
    norm = inner[:, 0:1] + 0.5 * row_sum(rhs * rhs)
    curvature = inner[:, 1:2] + row_sum(image * rhs) + row_sum(spread * full)
    out[:, :shared] = image + product(spread, edge_back, 3)
    out[:, shared:] = lanes(norm, curvature)


def image_kernel(per_dev, modes, local, edge, sums, touch, back, from_iface, diag, coefs, rhs_out, image_out, sums_out):
    factors = row_factors(local.shape[0], per_dev, modes)
    rhs = local[...] + product(edge[...], from_iface, 3)
    rhs_out[...] = rhs
    spread = at_elems(factors, coefs) * sums[...]
    spread_into(image_out, spread, back, diag, at_nodes(factors, diag) * rhs)
    sums_out[...] = short_product(image_out[...], touch.at[:, : spread.shape[1]])


def resid_kernel(per_dev, modes, own, edge, rhs, image, sums, image_sums, from_iface, edge_touch, diag, coefs, resid_out, norms_out):
    rows = rhs.shape[0]
    shared = edge.shape[1] - 128
    factors = row_factors(rows, per_dev, modes)
    per_elem, per_node = at_elems(factors, coefs), at_nodes(factors, diag)
    norm = own[:, shared : shared + 1] + edge[:, shared : shared + 1]
    curvature = own[:, shared + 1 : shared + 2] + edge[:, shared + 1 : shared + 2]
    alpha = norm / curvature
    given = edge[:, :shared]
    resid = rhs[...] - alpha * (image[...] + product(given, from_iface, 3))
    resid_out[...] = resid
    new = sums[...] - alpha * (image_sums[...] + product(given, edge_touch, 3))
    after = row_sum(diag[3:4, :] * resid * resid)
    square = row_sum(per_node * resid * resid) + row_sum(per_elem * new * new)
    mixed = row_sum(per_node * resid * rhs[...]) + row_sum(per_elem * new * sums[...])
    norms_out[...] = lanes(after, square, mixed)


def last_kernel(edge, own, norms_own, norms, resid, rhs, vel_out, mag_out):
    shared = edge.shape[1] - 128
    norm = own[:, shared : shared + 1] + edge[:, shared : shared + 1]
    curvature = own[:, shared + 1 : shared + 2] + edge[:, shared + 1 : shared + 2]
    alpha = norm / curvature
    after = norms_own[:, 0:1] + norms[:, 0:1]
    square = norms_own[:, 1:2] + norms[:, 1:2]
    mixed = norms_own[:, 2:3] + norms[:, 2:3]
    beta = after / norm
    alpha_next = after / (square + 2.0 * beta * mixed + beta * beta * curvature)
    answer = (alpha + alpha_next * beta) * rhs[...] + alpha_next * resid[...]
    row = 0
    for out in (vel_out, mag_out):
        comps, _, per_dev, _ = out.shape
        for c in range(comps):
            for s in range(2):
                out[c, s] = answer[row : row + per_dev]
                row += per_dev


def per_device(velocity, vorticity, magnetic, current, elem_nodes, mass_coef, stiff_coef, radial_coef, iface):
    comps, _, per_dev, nodes = velocity.shape
    owners = lax.axis_size("mode")
    modes = per_dev * owners
    block = nodes // owners
    rows = 4 * comps * per_dev
    elems = elem_nodes.shape[1]
    shared = iface.shape[1]
    mass, radial, stiff = (a.reshape(1, elems) for a in (mass_coef, radial_coef, stiff_coef))
    synthesis, analysis = trig_tables(modes, per_dev)

    def shape(*dims, kind=f32):
        return jax.ShapeDtypeStruct(dims, kind)

    in_hbm = pl.BlockSpec(memory_space=pltpu.HBM)

    def pin(array):
        return pltpu.with_memory_space_constraint(array, pltpu.HBM)

    nonlinear_cost = pl.CostEstimate(flops=2**33, bytes_accessed=2**24, transcendentals=0)
    if owners <= 8 and block % 128 == 0:
        *blocks, synthesis, analysis = pl.pallas_call(
            ring_pack_kernel,
            in_specs=[in_hbm] * 6,
            out_shape=(pltpu.VMEM((2 * rows, block), f32),) * owners
            + tuple(pltpu.VMEM(t.shape, t.dtype) for t in (synthesis, analysis)),
            scratch_shapes=[pltpu.VMEM((4, *velocity.shape), f32), pltpu.SemaphoreType.DMA((6,))],
            compiler_params=params(medium),
            name="pack",
        )(*(pin(a) for a in (velocity, magnetic, vorticity, current, synthesis, analysis)))
        for d in range(1, owners):
            blocks[d] = lax.ppermute(blocks[d], "mode", [(i, (i + d) % owners) for i in range(owners)])
        terms = pl.pallas_call(
            ring_nonlinear_kernel,
            out_shape=shape(owners, rows, block),
            scratch_shapes=[pltpu.VMEM((owners, 2 * rows, block), f32)],
            compiler_params=params(),
            name="nonlinear",
            cost_estimate=nonlinear_cost,
        )(*blocks, synthesis, analysis)
    else:
        packed = jnp.concatenate(
            [a.reshape(rows // 2, owners, block) for a in (velocity, magnetic, vorticity, current)], axis=0
        ).transpose(1, 0, 2)
        terms = pl.pallas_call(
            nonlinear_kernel,
            out_shape=shape(owners, rows, block),
            compiler_params=params(),
            name="nonlinear",
            cost_estimate=nonlinear_cost,
        )(lax.all_to_all(packed, "mode", 0, 0, tiled=True), synthesis, analysis)
    terms, elem_nodes = lax.optimization_barrier((terms, elem_nodes))
    forcing = lax.all_to_all(terms, "mode", 0, 0, tiled=True)
    tables = (
        shape(nodes, elems + shared, kind=f8),
        shape(elems, nodes, kind=f8),
        shape(shared, nodes, kind=bf16),
        shape(8, nodes),
        shape(8, elems),
        shape(shared, elems, kind=bf16),
        shape(elems, shared, kind=bf16),
        shape(8, shared),
    )
    in_vmem = pl.BlockSpec(memory_space=pltpu.VMEM)
    built = pl.pallas_call(
        mesh_kernel,
        in_specs=[in_hbm] * 5,
        out_specs=(in_hbm, in_hbm, *[in_vmem] * 6),
        out_shape=tables,
        scratch_shapes=[
            pltpu.VMEM((nodes, elems + shared), f8),
            pltpu.VMEM((elems, nodes), f8),
            pltpu.VMEM(elem_nodes.shape, jnp.int32),
            pltpu.VMEM((1, elems), f32),
            pltpu.VMEM((1, elems), f32),
            pltpu.VMEM((1, elems), f32),
            pltpu.VMEM(iface.shape, jnp.int32),
            pltpu.SemaphoreType.DMA((5,)),
            pltpu.SemaphoreType.DMA((2 * elems // math.gcd(elems, 256) + 1,)),
        ],
        compiler_params=params(large),
        name="incidence",
        cost_estimate=pl.CostEstimate(flops=2**31, bytes_accessed=2**23, transcendentals=0),
    )(elem_nodes, mass, radial, stiff, iface)
    touch, back, from_iface, diag, coefs, edge_touch, edge_back, edge_diag = built
    if block % 128:
        forcing = forcing.transpose(1, 0, 2).reshape(1, rows, nodes)

    def swap(array):
        return lax.ppermute(array, "mer", [(0, 1), (1, 0)])

    def call(kernel, name, outs, work=0):
        cost = pl.CostEstimate(flops=work, bytes_accessed=work // 512, transcendentals=0) if work else None
        return pl.pallas_call(
            functools.partial(kernel, per_dev, modes),
            out_shape=tuple(outs),
            compiler_params=params(),
            name=name,
            cost_estimate=cost,
        )

    full, part, small_row = shape(rows, nodes), shape(rows, elems), shape(rows, 128)
    kept = [pltpu.VMEM(a.shape, a.dtype) for a in (touch, edge_back, edge_diag, coefs)]
    spread, edge_own, touch, edge_back, edge_diag, coefs = pl.pallas_call(
        rhs_edge_kernel,
        in_specs=[in_vmem] + [in_hbm] * 4,
        out_shape=(part, shape(rows, shared), *kept),
        scratch_shapes=[pltpu.SemaphoreType.DMA((7,))],
        compiler_params=params(),
        name="rhs_edge",
    )(forcing, *(pin(a) for a in (touch, edge_back, edge_diag, coefs)))
    edge = swap(edge_own)
    local, sums, inner = call(rhs_kernel, "rhs", (full, part, small_row), 2**30)(
        forcing, spread, touch, back, diag
    )
    sums, image_edge_own = call(image_edge_kernel, "image_edge", (part, shape(rows, shared + 128)))(
        edge_own, edge, sums, inner, edge_touch, edge_back, edge_diag, coefs
    )
    image_edge = swap(image_edge_own)
    rhs, image, image_sums = call(image_kernel, "image", (full, full, part), 2**30)(
        local, edge, sums, touch, back, from_iface, diag, coefs
    )
    resid, norms_own = call(resid_kernel, "resid", (full, small_row))(
        image_edge_own, image_edge, rhs, image, sums, image_sums, from_iface, edge_touch, diag, coefs
    )
    out = shape(*velocity.shape)
    return pl.pallas_call(
        last_kernel, out_shape=(out, out), compiler_params=params(), name="last"
    )(image_edge, image_edge_own, norms_own, swap(norms_own), resid, rhs)


def solution(mesh):
    field = P("runs", None, "mode", "mer")
    placed = (field, field, field, field, P(None, "mer"), P("mer"), P("mer"), P("mer"), P("mer", None))
    return jax.shard_map(
        per_device, mesh=mesh, in_specs=placed, out_specs=(field, field), check_vma=False
    )
```

```python
import functools
import math

import jax
import jax.numpy as jnp
import numpy as np
from jax import lax
from jax.experimental import pallas as pl
from jax.experimental.pallas import tpu as pltpu
from jax.sharding import PartitionSpec as P

step_size = 0.05
diffusion_ratio = 2.0
f32 = jnp.float32
bf16 = jnp.bfloat16
f8 = jnp.float8_e4m3fn
largest, radix, exact_below = 16.0, 32.0, 2048.0
small, medium, large = 16 * 2**20, 54 * 2**20, 60 * 2**20


def params(limit=small):
    return pltpu.CompilerParams(vmem_limit_bytes=limit)


def halves(table):
    high = table.astype(np.float32).astype(jnp.bfloat16)
    low = (table - high.astype(np.float64)).astype(np.float32).astype(jnp.bfloat16)
    return high, low


def trig_tables(modes, per_dev):
    angles = 2 * modes
    order = np.arange(modes)
    points = np.arange(angles)
    phase = (points[:, None] * order[None, :] % angles) * (2.0 * math.pi / angles)
    both = np.stack([np.cos(phase), np.sin(phase)])
    both = both.reshape(2, angles, modes // per_dev, per_dev)
    factor = np.where(order == 0, 1.0, 2.0).reshape(modes // per_dev, per_dev) / angles
    same = np.eye(2)
    synthesis = np.einsum("pq,sajk->pajqsk", same, both).reshape(2 * angles, -1)
    analysis = np.einsum("pq,sajk,jk->jqskpa", same, both, factor * step_size).reshape(-1, 2 * angles)
    out = []
    for table in (synthesis, analysis):
        high, low = halves(table)
        out.append(jnp.asarray(np.concatenate([high, high, low], axis=1)))
    return out


def pieces(array, count):
    parts = []
    rest = array
    for i in range(count):
        part = rest.astype(bf16).astype(f32)
        parts.append(part)
        rest = rest - part
    return jnp.concatenate(parts, axis=0).astype(bf16)


def product(array, exact, count=2):
    rows = array.shape[0]
    out = jnp.dot(pieces(array, count), exact[...], preferred_element_type=f32)
    total = out[:rows]
    for i in range(1, count):
        total = total + out[i * rows : (i + 1) * rows]
    return total


def short_parts(array, count=4):
    top = jnp.maximum(jnp.max(jnp.abs(array), axis=1, keepdims=True), 1e-30)
    parts = []
    rest = array * (largest / top)
    for _ in range(count):
        part = jnp.round(rest)
        parts.append(part)
        rest = (rest - part) * radix
    return jnp.concatenate(parts, axis=0), top / largest


def short_total(out, scale, count=4):
    rows = scale.shape[0]
    total = out[(count - 1) * rows :]
    for i in reversed(range(count - 1)):
        total = total * (1.0 / radix) + out[i * rows : (i + 1) * rows]
    return total * scale


def short_product(array, exact):
    parts, scale = short_parts(array)
    return short_total(jnp.dot(parts.astype(f8), exact[...], preferred_element_type=f32), scale)


def spread_into(target, values, back, diag, base):
    few = jnp.max(diag[4:5, :]) * largest <= exact_below

    @pl.when(few)
    def _():
        target[...] = base + short_product(values, back)

    @pl.when(jnp.logical_not(few))
    def _():
        target[...] = base + product(values, back[...].astype(f32).astype(bf16), 3)


def table_product(table, values):
    high = values.astype(bf16)
    low = (values - high.astype(f32)).astype(bf16)
    return jnp.dot(table, jnp.concatenate([high, low, high], axis=0), preferred_element_type=f32)


def start_all(sources, targets, sems):
    copies = [
        pltpu.make_async_copy(source, target, sems.at[i])
        for i, (source, target) in enumerate(zip(sources, targets))
    ]
    for copy in copies:
        copy.start()
    return copies


def ring_pack_kernel(vel, mag, vort, cur, synthesis_hbm, analysis_hbm, *rest):
    *outs, synthesis, analysis, held, in_sems = rest
    owners, block = len(outs), outs[0].shape[1]
    me = lax.axis_index("mode")
    copies = start_all(
        (vel, mag, vort, cur, synthesis_hbm, analysis_hbm),
        [*(held.at[i] for i in range(4)), synthesis, analysis],
        in_sems,
    )
    starts = [pl.multiple_of(lax.rem(me + d, owners) * block, block) for d in range(owners)]
    row = 0
    for i in range(4):
        copies[i].wait()
        _, comps, _, per_dev, _ = held.shape
        for c in range(comps):
            for s in range(2):
                for d in range(owners):
                    outs[d][row : row + per_dev, :] = held[i, c, s, :, pl.ds(starts[d], block)]
                row += per_dev
    for copy in copies[4:]:
        copy.wait()


def ring_nonlinear_kernel(*refs):
    *blocks, synthesis, analysis, out, fields = refs
    owners = len(blocks)
    me = lax.axis_index("mode")
    for d in range(owners):
        fields[lax.rem(me + owners - d, owners)] = blocks[d][...]
    nonlinear_kernel(fields, synthesis, analysis, out)


def nonlinear_kernel(fields, synthesis, analysis, out):
    owners, rows, block = fields.shape
    pair = rows // 6
    angles = synthesis.shape[0] // 2
    phys = []
    for t in range(6):
        coef = jnp.concatenate([fields[j, t * pair : (t + 1) * pair, :] for j in range(owners)], axis=0)
        values = table_product(synthesis[...], coef)
        phys += [values[:angles], values[angles:]]
    vel, mag, vort, cur = phys[0:3], phys[3:6], phys[6:9], phys[9:12]

    def cross(a, b, i):
        j, k = (i + 1) % 3, (i + 2) % 3
        return a[j] * b[k] - a[k] * b[j]

    terms = [cross(vel, vort, i) + cross(cur, mag, i) for i in range(3)]
    terms += [cross(vel, mag, i) for i in range(3)]
    for t in range(3):
        coef = table_product(analysis[...], jnp.concatenate([terms[2 * t], terms[2 * t + 1]], axis=0))
        for j in range(owners):
            span = slice(t * pair, (t + 1) * pair)
            out[j, span, :] = fields[j, span, :] + coef[j * pair : (j + 1) * pair]


def mesh_kernel(nodes_hbm, mass_hbm, radial_hbm, stiff_hbm, iface_hbm, touch, back, from_iface, diag, coefs, edge_touch, edge_back, edge_diag, elem_nodes, mass, radial, stiff, iface, in_sems):
    loads = start_all(
        (nodes_hbm, mass_hbm, radial_hbm, stiff_hbm, iface_hbm), (elem_nodes, mass, radial, stiff, iface), in_sems
    )
    for load in loads:
        load.wait()
    elems, nodes = back.shape
    shared = iface.shape[1]
    fields = 8
    words = nodes // fields
    width = math.gcd(elems, 256)
    for c in range(elems // width):
        span = slice(c * width, (c + 1) * width)
        word = lax.broadcasted_iota(jnp.int32, (words, width), 0)
        total = jnp.zeros((words, width), jnp.int32)
        for i in range(elem_nodes.shape[0]):
            ids = elem_nodes[i : i + 1, span]
            field = ids // words
            value = jnp.left_shift(1, field * 4)
            total = total + jnp.where(ids - field * words == word, value, 0)
        for q in range(fields):
            count = (jnp.right_shift(total, 4 * q) & 15).astype(f32)
            touch[q * words : (q + 1) * words, span] = count.astype(f8)
            back[span, q * words : (q + 1) * words] = count.T.astype(f8)
    node = lax.broadcasted_iota(jnp.int32, (nodes, shared), 0)
    hit = jnp.where(iface[...] == node, 1.0, 0.0)
    touch[:, elems:] = hit.astype(f8)
    hit = hit.T
    from_iface[...] = hit.astype(bf16)
    counts = jnp.dot(hit.astype(f8), touch[:, :elems], preferred_element_type=f32)
    edge_touch[...] = counts.astype(bf16)
    edge_back[...] = counts.T.astype(bf16)
    zero = jnp.zeros((5, elems), f32)
    one = jnp.ones((1, elems), f32)
    coefs[...] = jnp.concatenate([mass[...] / 12.0, radial[...] / 12.0, stiff[...], zero], axis=0)
    scaled = jnp.concatenate(
        [mass[...] / 12.0, radial[...] / 12.0, 6.0 * stiff[...], one * 0.0, one, zero[:3]], axis=0
    )
    diag[...] = short_product(scaled, back)

    @pl.when(jnp.max(diag[4:5, :]) * largest > exact_below)
    def _():
        diag[...] = product(scaled, back[...].astype(f32).astype(bf16), 3)

    edge_diag[...] = short_product(diag[...], touch.at[:, elems:])
    hits = jnp.sum(hit, axis=0, keepdims=True)
    row = lax.broadcasted_iota(jnp.int32, (8, nodes), 0)
    diag[...] = jnp.where(row == 3, 1.0 - 0.5 * hits, diag[...])


def row_factors(rows, per_dev, modes):
    row = lax.broadcasted_iota(jnp.int32, (rows, 1), 0)
    order = (lax.axis_index("mode") * per_dev + row % per_dev).astype(f32)
    shift = (order / modes) ** 2
    scale = jnp.where(row < rows // 2, 1.0, diffusion_ratio).astype(f32)
    return shift, scale


def at_elems(factors, coefs):
    shift, scale = factors
    return coefs[0:1, :] + shift * coefs[1:2, :] - scale * coefs[2:3, :]


def at_nodes(factors, diag):
    shift, scale = factors
    return diag[0:1, :] + shift * diag[1:2, :] + scale * diag[2:3, :]


def row_sum(array):
    return jnp.sum(array, axis=1, keepdims=True)


def lanes(*columns):
    rows = columns[0].shape[0]
    lane = lax.broadcasted_iota(jnp.int32, (rows, 128), 1)
    out = jnp.broadcast_to(columns[-1], (rows, 128))
    for i in reversed(range(len(columns) - 1)):
        out = jnp.where(lane == i, columns[i], out)
    return out


def together(forcing):
    return jnp.concatenate([forcing[b] for b in range(forcing.shape[0])], axis=1)


def rhs_edge_kernel(forcing, touch, edge_back, edge_diag, coefs, spread_out, edge):
    elems = coefs.shape[1]
    sums = short_product(together(forcing), touch)
    spread = sums[:, :elems] * coefs[0:1, :]
    spread_out[...] = spread
    edge[...] = edge_diag[0:1, :] * sums[:, elems:] + product(spread, edge_back, 3)


def rhs_kernel(per_dev, modes, forcing, spread, touch, back, diag, local, sums, inner):
    rows = spread.shape[0]
    spread_into(local, spread[...], back, diag, diag[0:1, :] * together(forcing))
    image = local[...]
    sums[...] = short_product(image, touch.at[:, : spread.shape[1]])
    square = (2.0 * diag[3:4, :] - 1.0) * image * image
    inner[...] = lanes(row_sum(square), row_sum(at_nodes(row_factors(rows, per_dev, modes), diag) * square))


def image_edge_kernel(per_dev, modes, edge_own, edge, sums, inner, edge_touch, edge_back, edge_diag, coefs, sums_out, out):
    rows, shared = edge.shape
    factors = row_factors(rows, per_dev, modes)
    rhs = edge_own[...] + edge[...]
    full = sums[...] + product(edge[...], edge_touch, 3)
    sums_out[...] = full
    spread = at_elems(factors, coefs) * full
    image = at_nodes(factors, edge_diag) * rhs
    norm = inner[:, 0:1] + 0.5 * row_sum(rhs * rhs)
    curvature = inner[:, 1:2] + row_sum(image * rhs) + row_sum(spread * full)
    out[:, :shared] = image + product(spread, edge_back, 3)
    out[:, shared:] = lanes(norm, curvature)


def image_kernel(per_dev, modes, local, edge, sums, touch, back, from_iface, diag, coefs, rhs_out, image_out, sums_out):
    factors = row_factors(local.shape[0], per_dev, modes)
    rhs = local[...] + product(edge[...], from_iface, 3)
    rhs_out[...] = rhs
    spread = at_elems(factors, coefs) * sums[...]
    spread_into(image_out, spread, back, diag, at_nodes(factors, diag) * rhs)
    sums_out[...] = short_product(image_out[...], touch.at[:, : spread.shape[1]])


def resid_kernel(per_dev, modes, own, edge, rhs, image, sums, image_sums, from_iface, edge_touch, diag, coefs, resid_out, norms_out):
    rows = rhs.shape[0]
    shared = edge.shape[1] - 128
    factors = row_factors(rows, per_dev, modes)
    per_elem, per_node = at_elems(factors, coefs), at_nodes(factors, diag)
    norm = own[:, shared : shared + 1] + edge[:, shared : shared + 1]
    curvature = own[:, shared + 1 : shared + 2] + edge[:, shared + 1 : shared + 2]
    alpha = norm / curvature
    given = edge[:, :shared]
    resid = rhs[...] - alpha * (image[...] + product(given, from_iface, 3))
    resid_out[...] = resid
    new = sums[...] - alpha * (image_sums[...] + product(given, edge_touch, 3))
    after = row_sum(diag[3:4, :] * resid * resid)
    square = row_sum(per_node * resid * resid) + row_sum(per_elem * new * new)
    mixed = row_sum(per_node * resid * rhs[...]) + row_sum(per_elem * new * sums[...])
    norms_out[...] = lanes(after, square, mixed)


def last_kernel(edge, own, norms_own, norms, resid, rhs, vel_out, mag_out):
    shared = edge.shape[1] - 128
    norm = own[:, shared : shared + 1] + edge[:, shared : shared + 1]
    curvature = own[:, shared + 1 : shared + 2] + edge[:, shared + 1 : shared + 2]
    alpha = norm / curvature
    after = norms_own[:, 0:1] + norms[:, 0:1]
    square = norms_own[:, 1:2] + norms[:, 1:2]
    mixed = norms_own[:, 2:3] + norms[:, 2:3]
    beta = after / norm
    alpha_next = after / (square + 2.0 * beta * mixed + beta * beta * curvature)
    answer = (alpha + alpha_next * beta) * rhs[...] + alpha_next * resid[...]
    row = 0
    for out in (vel_out, mag_out):
        comps, _, per_dev, _ = out.shape
        for c in range(comps):
            for s in range(2):
                out[c, s] = answer[row : row + per_dev]
                row += per_dev


def per_device(velocity, vorticity, magnetic, current, elem_nodes, mass_coef, stiff_coef, radial_coef, iface):
    comps, _, per_dev, nodes = velocity.shape
    owners = lax.axis_size("mode")
    modes = per_dev * owners
    block = nodes // owners
    rows = 4 * comps * per_dev
    elems = elem_nodes.shape[1]
    shared = iface.shape[1]
    mass, radial, stiff = (a.reshape(1, elems) for a in (mass_coef, radial_coef, stiff_coef))
    synthesis, analysis = trig_tables(modes, per_dev)

    def shape(*dims, kind=f32):
        return jax.ShapeDtypeStruct(dims, kind)

    in_hbm = pl.BlockSpec(memory_space=pltpu.HBM)

    def pin(array):
        return pltpu.with_memory_space_constraint(array, pltpu.HBM)

    nonlinear_cost = pl.CostEstimate(flops=2**33, bytes_accessed=2**24, transcendentals=0)
    tables = (
        shape(nodes, elems + shared, kind=f8),
        shape(elems, nodes, kind=f8),
        shape(shared, nodes, kind=bf16),
        shape(8, nodes),
        shape(8, elems),
        shape(shared, elems, kind=bf16),
        shape(elems, shared, kind=bf16),
        shape(8, shared),
    )
    built = pl.pallas_call(
        mesh_kernel,
        in_specs=[in_hbm] * 5,
        out_shape=tuple(pltpu.VMEM(t.shape, t.dtype) for t in tables),
        scratch_shapes=[
            pltpu.VMEM(elem_nodes.shape, jnp.int32),
            pltpu.VMEM((1, elems), f32),
            pltpu.VMEM((1, elems), f32),
            pltpu.VMEM((1, elems), f32),
            pltpu.VMEM(iface.shape, jnp.int32),
            pltpu.SemaphoreType.DMA((5,)),
        ],
        compiler_params=params(),
        name="incidence",
        cost_estimate=pl.CostEstimate(flops=2**31, bytes_accessed=2**23, transcendentals=0),
    )(*(pin(a) for a in (elem_nodes, mass, radial, stiff, iface)))
    if owners <= 8 and block % 128 == 0:
        *blocks, synthesis, analysis = pl.pallas_call(
            ring_pack_kernel,
            in_specs=[in_hbm] * 6,
            out_shape=(pltpu.VMEM((2 * rows, block), f32),) * owners
            + tuple(pltpu.VMEM(t.shape, t.dtype) for t in (synthesis, analysis)),
            scratch_shapes=[pltpu.VMEM((4, *velocity.shape), f32), pltpu.SemaphoreType.DMA((6,))],
            compiler_params=params(medium),
            name="pack",
        )(*(pin(a) for a in (velocity, magnetic, vorticity, current, synthesis, analysis)))
        for d in range(1, owners):
            blocks[d] = lax.ppermute(blocks[d], "mode", [(i, (i + d) % owners) for i in range(owners)])
        *blocks, built = lax.optimization_barrier((*blocks, built))
        terms = pl.pallas_call(
            ring_nonlinear_kernel,
            out_shape=pltpu.VMEM((owners, rows, block), f32),
            scratch_shapes=[pltpu.VMEM((owners, 2 * rows, block), f32)],
            compiler_params=params(),
            name="nonlinear",
            cost_estimate=nonlinear_cost,
        )(*blocks, synthesis, analysis)
    else:
        packed = jnp.concatenate(
            [a.reshape(rows // 2, owners, block) for a in (velocity, magnetic, vorticity, current)], axis=0
        ).transpose(1, 0, 2)
        terms = pl.pallas_call(
            nonlinear_kernel,
            out_shape=shape(owners, rows, block),
            compiler_params=params(),
            name="nonlinear",
            cost_estimate=nonlinear_cost,
        )(lax.all_to_all(packed, "mode", 0, 0, tiled=True), synthesis, analysis)
    touch, back, from_iface, diag, coefs, edge_touch, edge_back, edge_diag = built
    forcing = lax.all_to_all(terms, "mode", 0, 0, tiled=True)
    if block % 128:
        forcing = forcing.transpose(1, 0, 2).reshape(1, rows, nodes)

    def swap(array):
        return lax.ppermute(array, "mer", [(0, 1), (1, 0)])

    def call(kernel, name, outs, work=0):
        cost = pl.CostEstimate(flops=work, bytes_accessed=work // 512, transcendentals=0) if work else None
        return pl.pallas_call(
            functools.partial(kernel, per_dev, modes),
            out_shape=tuple(outs),
            compiler_params=params(),
            name=name,
            cost_estimate=cost,
        )

    full, part, small_row = shape(rows, nodes), shape(rows, elems), shape(rows, 128)
    spread, edge_own = pl.pallas_call(
        rhs_edge_kernel,
        out_shape=(part, shape(rows, shared)),
        compiler_params=params(),
        name="rhs_edge",
    )(forcing, touch, edge_back, edge_diag, coefs)
    edge = swap(edge_own)
    local, sums, inner = call(rhs_kernel, "rhs", (full, part, small_row), 2**30)(
        forcing, spread, touch, back, diag
    )
    sums, image_edge_own = call(image_edge_kernel, "image_edge", (part, shape(rows, shared + 128)))(
        edge_own, edge, sums, inner, edge_touch, edge_back, edge_diag, coefs
    )
    image_edge = swap(image_edge_own)
    rhs, image, image_sums = call(image_kernel, "image", (full, full, part), 2**30)(
        local, edge, sums, touch, back, from_iface, diag, coefs
    )
    resid, norms_own = call(resid_kernel, "resid", (full, small_row))(
        image_edge_own, image_edge, rhs, image, sums, image_sums, from_iface, edge_touch, diag, coefs
    )
    out = shape(*velocity.shape)
    return pl.pallas_call(
        last_kernel, out_shape=(out, out), compiler_params=params(), name="last"
    )(image_edge, image_edge_own, norms_own, swap(norms_own), resid, rhs)


def solution(mesh):
    field = P("runs", None, "mode", "mer")
    placed = (field, field, field, field, P(None, "mer"), P("mer"), P("mer"), P("mer"), P("mer", None))
    return jax.shard_map(
        per_device, mesh=mesh, in_specs=placed, out_specs=(field, field), check_vma=False
    )
```

```python
import functools
import math

import jax
import jax.numpy as jnp
import numpy as np
from jax import lax
from jax.experimental import pallas as pl
from jax.experimental.pallas import tpu as pltpu
from jax.sharding import PartitionSpec as P

step_size = 0.05
diffusion_ratio = 2.0
f32 = jnp.float32
bf16 = jnp.bfloat16
f8 = jnp.float8_e4m3fn
largest, radix, exact_below = 16.0, 32.0, 2048.0
small, medium, large = 16 * 2**20, 54 * 2**20, 60 * 2**20


def params(limit=small):
    return pltpu.CompilerParams(vmem_limit_bytes=limit)


def halves(table):
    high = table.astype(np.float32).astype(jnp.bfloat16)
    low = (table - high.astype(np.float64)).astype(np.float32).astype(jnp.bfloat16)
    return high, low


def trig_tables(modes, per_dev):
    angles = 2 * modes
    order = np.arange(modes)
    points = np.arange(angles)
    phase = (points[:, None] * order[None, :] % angles) * (2.0 * math.pi / angles)
    both = np.stack([np.cos(phase), np.sin(phase)])
    both = both.reshape(2, angles, modes // per_dev, per_dev)
    factor = np.where(order == 0, 1.0, 2.0).reshape(modes // per_dev, per_dev) / angles
    same = np.eye(2)
    synthesis = np.einsum("pq,sajk->pajqsk", same, both).reshape(2 * angles, -1)
    analysis = np.einsum("pq,sajk,jk->jqskpa", same, both, factor * step_size).reshape(-1, 2 * angles)
    out = []
    for table in (synthesis, analysis):
        high, low = halves(table)
        out.append(jnp.asarray(np.concatenate([high, high, low], axis=1)))
    return out


def pieces(array, count):
    parts = []
    rest = array
    for i in range(count):
        part = rest.astype(bf16).astype(f32)
        parts.append(part)
        rest = rest - part
    return jnp.concatenate(parts, axis=0).astype(bf16)


def product(array, exact, count=2):
    rows = array.shape[0]
    out = jnp.dot(pieces(array, count), exact[...], preferred_element_type=f32)
    total = out[:rows]
    for i in range(1, count):
        total = total + out[i * rows : (i + 1) * rows]
    return total


def short_parts(array, count=4):
    top = jnp.maximum(jnp.max(jnp.abs(array), axis=1, keepdims=True), 1e-30)
    parts = []
    rest = array * (largest / top)
    for _ in range(count):
        part = jnp.round(rest)
        parts.append(part)
        rest = (rest - part) * radix
    return jnp.concatenate(parts, axis=0), top / largest


def short_total(out, scale, count=4):
    rows = scale.shape[0]
    total = out[(count - 1) * rows :]
    for i in reversed(range(count - 1)):
        total = total * (1.0 / radix) + out[i * rows : (i + 1) * rows]
    return total * scale


def short_product(array, exact):
    parts, scale = short_parts(array)
    return short_total(jnp.dot(parts.astype(f8), exact[...], preferred_element_type=f32), scale)


def spread_into(target, values, back, diag, base):
    few = jnp.max(diag[4:5, :]) * largest <= exact_below

    @pl.when(few)
    def _():
        target[...] = base + short_product(values, back)

    @pl.when(jnp.logical_not(few))
    def _():
        target[...] = base + product(values, back[...].astype(f32).astype(bf16), 3)


def table_product(table, values):
    high = values.astype(bf16)
    low = (values - high.astype(f32)).astype(bf16)
    return jnp.dot(table, jnp.concatenate([high, low, high], axis=0), preferred_element_type=f32)


def start_all(sources, targets, sems):
    copies = [
        pltpu.make_async_copy(source, target, sems.at[i])
        for i, (source, target) in enumerate(zip(sources, targets))
    ]
    for copy in copies:
        copy.start()
    return copies


def ring_pack_kernel(vel, mag, vort, cur, *rest):
    *rest, held, in_sems = rest
    small, outs, fetched = rest[:7], rest[7:-7], rest[-7:]
    owners, block = len(outs), outs[0].shape[1]
    me = lax.axis_index("mode")
    copies = start_all(
        (vel, mag, vort, cur, *small),
        [*(held.at[i] for i in range(4)), *fetched],
        in_sems,
    )
    starts = [pl.multiple_of(lax.rem(me + d, owners) * block, block) for d in range(owners)]
    row = 0
    for i in range(4):
        copies[i].wait()
        _, comps, _, per_dev, _ = held.shape
        for c in range(comps):
            for s in range(2):
                for d in range(owners):
                    outs[d][row : row + per_dev, :] = held[i, c, s, :, pl.ds(starts[d], block)]
                row += per_dev
    for copy in copies[4:]:
        copy.wait()


def ring_nonlinear_kernel(*refs):
    *blocks, synthesis, analysis, out, fields = refs
    owners = len(blocks)
    me = lax.axis_index("mode")
    for d in range(owners):
        fields[lax.rem(me + owners - d, owners)] = blocks[d][...]
    nonlinear_kernel(fields, synthesis, analysis, out)


def nonlinear_kernel(fields, synthesis, analysis, out):
    owners, rows, block = fields.shape
    pair = rows // 6
    angles = synthesis.shape[0] // 2
    phys = []
    for t in range(6):
        coef = jnp.concatenate([fields[j, t * pair : (t + 1) * pair, :] for j in range(owners)], axis=0)
        values = table_product(synthesis[...], coef)
        phys += [values[:angles], values[angles:]]
    vel, mag, vort, cur = phys[0:3], phys[3:6], phys[6:9], phys[9:12]

    def cross(a, b, i):
        j, k = (i + 1) % 3, (i + 2) % 3
        return a[j] * b[k] - a[k] * b[j]

    terms = [cross(vel, vort, i) + cross(cur, mag, i) for i in range(3)]
    terms += [cross(vel, mag, i) for i in range(3)]
    for t in range(3):
        coef = table_product(analysis[...], jnp.concatenate([terms[2 * t], terms[2 * t + 1]], axis=0))
        for j in range(owners):
            span = slice(t * pair, (t + 1) * pair)
            out[j, span, :] = fields[j, span, :] + coef[j * pair : (j + 1) * pair]


def mesh_kernel(elem_nodes, mass, radial, stiff, iface, touch, back, from_iface, diag, coefs, edge_touch, edge_back, edge_diag):
    elems, nodes = back.shape
    shared = iface.shape[1]
    fields = 8
    words = nodes // fields
    width = math.gcd(elems, 256)
    for c in range(elems // width):
        span = slice(c * width, (c + 1) * width)
        word = lax.broadcasted_iota(jnp.int32, (words, width), 0)
        total = jnp.zeros((words, width), jnp.int32)
        for i in range(elem_nodes.shape[0]):
            ids = elem_nodes[i : i + 1, span]
            field = ids // words
            value = jnp.left_shift(1, field * 4)
            total = total + jnp.where(ids - field * words == word, value, 0)
        turned = total.T
        for q in range(fields):
            part = slice(q * words, (q + 1) * words)
            touch[part, span] = (jnp.right_shift(total, 4 * q) & 15).astype(f32).astype(f8)
            back[span, part] = (jnp.right_shift(turned, 4 * q) & 15).astype(f32).astype(f8)
    node = lax.broadcasted_iota(jnp.int32, (nodes, shared), 0)
    hit = jnp.where(iface[...] == node, 1.0, 0.0)
    touch[:, elems:] = hit.astype(f8)
    hit = hit.T
    from_iface[...] = hit.astype(bf16)
    counts = jnp.dot(hit.astype(f8), touch[:, :elems], preferred_element_type=f32)
    edge_touch[...] = counts.astype(bf16)
    edge_back[...] = counts.T.astype(bf16)
    zero = jnp.zeros((5, elems), f32)
    one = jnp.ones((1, elems), f32)
    coefs[...] = jnp.concatenate([mass[...] / 12.0, radial[...] / 12.0, stiff[...], zero], axis=0)
    scaled = jnp.concatenate(
        [mass[...] / 12.0, radial[...] / 12.0, 6.0 * stiff[...], one * 0.0, one, zero[:3]], axis=0
    )
    diag[...] = short_product(scaled, back)

    @pl.when(jnp.max(diag[4:5, :]) * largest > exact_below)
    def _():
        diag[...] = product(scaled, back[...].astype(f32).astype(bf16), 3)

    edge_diag[...] = short_product(diag[...], touch.at[:, elems:])
    hits = jnp.sum(hit, axis=0, keepdims=True)
    row = lax.broadcasted_iota(jnp.int32, (8, nodes), 0)
    diag[...] = jnp.where(row == 3, 1.0 - 0.5 * hits, diag[...])


def row_factors(rows, per_dev, modes):
    row = lax.broadcasted_iota(jnp.int32, (rows, 1), 0)
    order = (lax.axis_index("mode") * per_dev + row % per_dev).astype(f32)
    shift = (order / modes) ** 2
    scale = jnp.where(row < rows // 2, 1.0, diffusion_ratio).astype(f32)
    return shift, scale


def at_elems(factors, coefs):
    shift, scale = factors
    return coefs[0:1, :] + shift * coefs[1:2, :] - scale * coefs[2:3, :]


def at_nodes(factors, diag):
    shift, scale = factors
    return diag[0:1, :] + shift * diag[1:2, :] + scale * diag[2:3, :]


def row_sum(array):
    return jnp.sum(array, axis=1, keepdims=True)


def lanes(*columns):
    rows = columns[0].shape[0]
    lane = lax.broadcasted_iota(jnp.int32, (rows, 128), 1)
    out = jnp.broadcast_to(columns[-1], (rows, 128))
    for i in reversed(range(len(columns) - 1)):
        out = jnp.where(lane == i, columns[i], out)
    return out


def together(forcing):
    return jnp.concatenate([forcing[b] for b in range(forcing.shape[0])], axis=1)


def rhs_edge_kernel(forcing, touch, edge_back, edge_diag, coefs, spread_out, edge):
    elems = coefs.shape[1]
    sums = short_product(together(forcing), touch)
    spread = sums[:, :elems] * coefs[0:1, :]
    spread_out[...] = spread
    edge[...] = edge_diag[0:1, :] * sums[:, elems:] + product(spread, edge_back, 3)


def rhs_kernel(per_dev, modes, forcing, spread, touch, back, diag, local, sums, inner):
    rows = spread.shape[0]
    spread_into(local, spread[...], back, diag, diag[0:1, :] * together(forcing))
    image = local[...]
    sums[...] = short_product(image, touch.at[:, : spread.shape[1]])
    square = (2.0 * diag[3:4, :] - 1.0) * image * image
    inner[...] = lanes(row_sum(square), row_sum(at_nodes(row_factors(rows, per_dev, modes), diag) * square))


def image_edge_kernel(per_dev, modes, edge_own, edge, sums, inner, edge_touch, edge_back, edge_diag, coefs, sums_out, out):
    rows, shared = edge.shape
    factors = row_factors(rows, per_dev, modes)
    rhs = edge_own[...] + edge[...]
    full = sums[...] + product(edge[...], edge_touch, 3)
    sums_out[...] = full
    spread = at_elems(factors, coefs) * full
    image = at_nodes(factors, edge_diag) * rhs
    norm = inner[:, 0:1] + 0.5 * row_sum(rhs * rhs)
    curvature = inner[:, 1:2] + row_sum(image * rhs) + row_sum(spread * full)
    out[:, :shared] = image + product(spread, edge_back, 3)
    out[:, shared:] = lanes(norm, curvature)


def image_kernel(per_dev, modes, local, edge, sums, touch, back, from_iface, diag, coefs, rhs_out, image_out, sums_out):
    factors = row_factors(local.shape[0], per_dev, modes)
    rhs = local[...] + product(edge[...], from_iface, 3)
    rhs_out[...] = rhs
    spread = at_elems(factors, coefs) * sums[...]
    spread_into(image_out, spread, back, diag, at_nodes(factors, diag) * rhs)
    sums_out[...] = short_product(image_out[...], touch.at[:, : spread.shape[1]])


def resid_kernel(per_dev, modes, own, edge, rhs, image, sums, image_sums, from_iface, edge_touch, diag, coefs, resid_out, norms_out):
    rows = rhs.shape[0]
    shared = edge.shape[1] - 128
    factors = row_factors(rows, per_dev, modes)
    per_elem, per_node = at_elems(factors, coefs), at_nodes(factors, diag)
    norm = own[:, shared : shared + 1] + edge[:, shared : shared + 1]
    curvature = own[:, shared + 1 : shared + 2] + edge[:, shared + 1 : shared + 2]
    alpha = norm / curvature
    given = edge[:, :shared]
    resid = rhs[...] - alpha * (image[...] + product(given, from_iface, 3))
    resid_out[...] = resid
    new = sums[...] - alpha * (image_sums[...] + product(given, edge_touch, 3))
    after = row_sum(diag[3:4, :] * resid * resid)
    square = row_sum(per_node * resid * resid) + row_sum(per_elem * new * new)
    mixed = row_sum(per_node * resid * rhs[...]) + row_sum(per_elem * new * sums[...])
    norms_out[...] = lanes(after, square, mixed)


def last_kernel(edge, own, norms_own, norms, resid, rhs, vel_out, mag_out):
    shared = edge.shape[1] - 128
    norm = own[:, shared : shared + 1] + edge[:, shared : shared + 1]
    curvature = own[:, shared + 1 : shared + 2] + edge[:, shared + 1 : shared + 2]
    alpha = norm / curvature
    after = norms_own[:, 0:1] + norms[:, 0:1]
    square = norms_own[:, 1:2] + norms[:, 1:2]
    mixed = norms_own[:, 2:3] + norms[:, 2:3]
    beta = after / norm
    alpha_next = after / (square + 2.0 * beta * mixed + beta * beta * curvature)
    answer = (alpha + alpha_next * beta) * rhs[...] + alpha_next * resid[...]
    row = 0
    for out in (vel_out, mag_out):
        comps, _, per_dev, _ = out.shape
        for c in range(comps):
            for s in range(2):
                out[c, s] = answer[row : row + per_dev]
                row += per_dev


def per_device(velocity, vorticity, magnetic, current, elem_nodes, mass_coef, stiff_coef, radial_coef, iface):
    comps, _, per_dev, nodes = velocity.shape
    owners = lax.axis_size("mode")
    modes = per_dev * owners
    block = nodes // owners
    rows = 4 * comps * per_dev
    elems = elem_nodes.shape[1]
    shared = iface.shape[1]
    mass, radial, stiff = (a.reshape(1, elems) for a in (mass_coef, radial_coef, stiff_coef))
    synthesis, analysis = trig_tables(modes, per_dev)

    def shape(*dims, kind=f32):
        return jax.ShapeDtypeStruct(dims, kind)

    in_hbm = pl.BlockSpec(memory_space=pltpu.HBM)

    def pin(array):
        return pltpu.with_memory_space_constraint(array, pltpu.HBM)

    nonlinear_cost = pl.CostEstimate(flops=2**33, bytes_accessed=2**24, transcendentals=0)
    tables = (
        shape(nodes, elems + shared, kind=f8),
        shape(elems, nodes, kind=f8),
        shape(shared, nodes, kind=bf16),
        shape(8, nodes),
        shape(8, elems),
        shape(shared, elems, kind=bf16),
        shape(elems, shared, kind=bf16),
        shape(8, shared),
    )
    incidence = pl.pallas_call(
        mesh_kernel,
        out_shape=tuple(pltpu.VMEM(t.shape, t.dtype) for t in tables),
        compiler_params=params(),
        name="incidence",
        cost_estimate=pl.CostEstimate(flops=2**31, bytes_accessed=2**23, transcendentals=0),
    )
    small_inputs = (elem_nodes, mass, radial, stiff, iface)
    if owners <= 8 and block % 128 == 0:
        small_inputs = (*small_inputs, synthesis, analysis)
        packed = pl.pallas_call(
            ring_pack_kernel,
            in_specs=[in_hbm] * 11,
            out_shape=(pltpu.VMEM((2 * rows, block), f32),) * owners
            + tuple(pltpu.VMEM(t.shape, t.dtype) for t in small_inputs),
            scratch_shapes=[pltpu.VMEM((4, *velocity.shape), f32), pltpu.SemaphoreType.DMA((11,))],
            compiler_params=params(medium),
            name="pack",
        )(*(pin(a) for a in (velocity, magnetic, vorticity, current, *small_inputs)))
        blocks, small_inputs, (synthesis, analysis) = list(packed[:owners]), packed[owners:-2], packed[-2:]
        built = incidence(*small_inputs)
        for d in range(1, owners):
            blocks[d] = lax.ppermute(blocks[d], "mode", [(i, (i + d) % owners) for i in range(owners)])
        *blocks, built = lax.optimization_barrier((*blocks, built))
        terms = pl.pallas_call(
            ring_nonlinear_kernel,
            out_shape=pltpu.VMEM((owners, rows, block), f32),
            scratch_shapes=[pltpu.VMEM((owners, 2 * rows, block), f32)],
            compiler_params=params(),
            name="nonlinear",
            cost_estimate=nonlinear_cost,
        )(*blocks, synthesis, analysis)
    else:
        built = incidence(*small_inputs)
        packed = jnp.concatenate(
            [a.reshape(rows // 2, owners, block) for a in (velocity, magnetic, vorticity, current)], axis=0
        ).transpose(1, 0, 2)
        terms = pl.pallas_call(
            nonlinear_kernel,
            out_shape=shape(owners, rows, block),
            compiler_params=params(),
            name="nonlinear",
            cost_estimate=nonlinear_cost,
        )(lax.all_to_all(packed, "mode", 0, 0, tiled=True), synthesis, analysis)
    touch, back, from_iface, diag, coefs, edge_touch, edge_back, edge_diag = built
    forcing = lax.all_to_all(terms, "mode", 0, 0, tiled=True)
    if block % 128:
        forcing = forcing.transpose(1, 0, 2).reshape(1, rows, nodes)

    def swap(array):
        return lax.ppermute(array, "mer", [(0, 1), (1, 0)])

    def call(kernel, name, outs, work=0):
        cost = pl.CostEstimate(flops=work, bytes_accessed=work // 512, transcendentals=0) if work else None
        return pl.pallas_call(
            functools.partial(kernel, per_dev, modes),
            out_shape=tuple(outs),
            compiler_params=params(),
            name=name,
            cost_estimate=cost,
        )

    full, part, small_row = shape(rows, nodes), shape(rows, elems), shape(rows, 128)
    spread, edge_own = pl.pallas_call(
        rhs_edge_kernel,
        out_shape=(part, shape(rows, shared)),
        compiler_params=params(),
        name="rhs_edge",
    )(forcing, touch, edge_back, edge_diag, coefs)
    edge = swap(edge_own)
    local, sums, inner = call(rhs_kernel, "rhs", (full, part, small_row), 2**30)(
        forcing, spread, touch, back, diag
    )
    sums, image_edge_own = call(image_edge_kernel, "image_edge", (part, shape(rows, shared + 128)))(
        edge_own, edge, sums, inner, edge_touch, edge_back, edge_diag, coefs
    )
    image_edge = swap(image_edge_own)
    rhs, image, image_sums = call(image_kernel, "image", (full, full, part), 2**30)(
        local, edge, sums, touch, back, from_iface, diag, coefs
    )
    resid, norms_own = call(resid_kernel, "resid", (full, small_row))(
        image_edge_own, image_edge, rhs, image, sums, image_sums, from_iface, edge_touch, diag, coefs
    )
    out = shape(*velocity.shape)
    return pl.pallas_call(
        last_kernel, out_shape=(out, out), compiler_params=params(), name="last"
    )(image_edge, image_edge_own, norms_own, swap(norms_own), resid, rhs)


def solution(mesh):
    field = P("runs", None, "mode", "mer")
    placed = (field, field, field, field, P(None, "mer"), P("mer"), P("mer"), P("mer"), P("mer", None))
    return jax.shard_map(
        per_device, mesh=mesh, in_specs=placed, out_specs=(field, field), check_vma=False
    )
```
